32 devices in a mesh: expert: 4 (over z), dp: 4 (over y, x), test: 2 (over core).
Axes of the slice: x: 2, y: 2, z: 4, core: 2. Of those that a mesh axis runs over, the one named last changes fastest.
Arguments:
- tokens: bfloat16 [1024, 3584], P(('expert', 'dp'), 'test'), may hold values from -6 to 6
- out_grad: bfloat16 [1024, 3584], P(('expert', 'dp'), 'test'), may hold values from -6 to 6
- route_ids: int32 [1024, 8], P(('expert', 'dp')), may hold values from 0 to 255, as said below
- route_slots: int32 [1024, 8], P(('expert', 'dp')), may hold values from -1 to 1, as said below
- route_weight: bfloat16 [1024, 8], P(('expert', 'dp')), may hold values from 0.19921875 to 1
- w_gate: bfloat16 [4, 3584, 1024], P('expert', None, ('dp', 'test')), may hold values from -0.09375 to 0.09375
- w_up: bfloat16 [4, 3584, 1024], P('expert', None, ('dp', 'test')), may hold values from -0.09375 to 0.09375
- w_down: bfloat16 [4, 1024, 3584], P('expert', ('dp', 'test')), may hold values from -0.1875 to 0.1875
- proj_hidden: bfloat16 [4, 64, 1024], P('expert', None, ('dp', 'test')), may hold values from -0.1875 to 0.1875
- proj_grad: bfloat16 [4, 64, 3584], P('expert'), may hold values from -0.09375 to 0.09375
- test_feats: bfloat16 [4, 256, 4096], P('expert', 'test'), may hold values from -0.09375 to 0.09375
Outputs:
- in_grad: bfloat16 [1024, 3584], P(('expert', 'dp'), 'test')
- scores: float32 [1024, 256], P(('expert', 'dp'), 'test')
The draws below stay inside these ranges and needn't reach their ends.
Inputs may be any that keep to these rules, and one draw needn't show every extreme that they name: `route_ids`: each row names 8 different experts. `route_slots`: A route's slot is -1 exactly when its expert is 4 or more, or when 2 earlier tokens of the same aligned block of 64 rows already take that expert; otherwise it is the number of earlier tokens of that block routed to that expert.
All inputs are finite; a program needn't handle non-finite values.
Results may differ from the reference program's by a relative error of at most 0.0065.
Values may be sent and summed in bfloat16 or wider, within the bound.
No kernel may reach another device: no remote copies, remote signals or barrier semaphores. Data moves between devices by JAX's collectives and lax.ppermute only.
A program may use at most 64 MiB of HBM per device.

```python
import jax
import jax.numpy as jnp
from jax import lax

D = 3584
FF = 1024
ROUTED = 256
TOPK = 8
PROJ = 64
TOK_DEV = 64
NTEST = 256
CAP = 2
EXPERTS = 4
TOKENS = 1024
N_DP = 4
N_TEST = 2


def route_table(key):
    base_key = jax.random.fold_in(key, 11)
    key_pop, key_noise, key_pick = jax.random.split(base_key, 3)
    blocks = TOKENS // TOK_DEV
    popularity = jax.random.randint(key_pop, (ROUTED,), 0, 3).astype(jnp.int32)
    noise_bits = jax.random.randint(key_noise, (TOKENS, ROUTED), 0, 1 << 20).astype(jnp.int32)
    picked = jax.random.randint(key_pick, (blocks,), 0, EXPERTS).astype(jnp.int32)
    row_ids = jnp.arange(TOKENS, dtype=jnp.int32)
    local_row = row_ids % TOK_DEV
    column = jnp.arange(ROUTED, dtype=jnp.int32)
    forced = (local_row[:, None] < CAP) & (column[None, :] == picked[row_ids // TOK_DEV][:, None])
    priority = (noise_bits + popularity[None, :] * (1 << 18)) * ROUTED + column[None, :] + forced.astype(jnp.int32) * (1 << 30)
    chosen_ids = lax.top_k(priority, TOPK)[1].astype(jnp.int32)
    chosen = jnp.sum((chosen_ids[:, :, None] == column[None, None, :]).astype(jnp.int32), axis=1)
    earlier = jnp.cumsum(chosen.reshape(blocks, TOK_DEV, ROUTED), axis=1).reshape(TOKENS, ROUTED) - chosen
    order_rank = jnp.take_along_axis(earlier, chosen_ids, axis=1)
    live_mask = (chosen_ids < EXPERTS) & (order_rank < CAP)
    slot_ids = jnp.where(live_mask, order_rank, -1).astype(jnp.int32)
    return (chosen_ids, slot_ids)


def draw_route_ids(key, part):
    return route_table(key)[0]


def draw_route_slots(key, part):
    return route_table(key)[1]


def block_scale(own_key, dims, cuts, low, largest):
    def one(position, parts):
        steps = jax.random.uniform(jax.random.fold_in(jax.random.fold_in(own_key, 6), position), (parts,), jnp.float32, low / len(cuts), largest / len(cuts))
        return jnp.repeat(jnp.exp(steps), dims[position] // parts).reshape((-1,) + (1,) * (len(dims) - position - 1))

    factor_of = one(*cuts[0])
    for cut in cuts[1:]:
        factor_of = factor_of * one(*cut)
    return factor_of


def bell_draw(rng, shape, scale, limit, cuts=(), kind=jnp.bfloat16):
    loudness = block_scale(rng, shape, cuts, -0.22, 0.18) if cuts else 1.0
    result = jax.random.normal(rng, shape, jnp.float32) * scale * loudness
    return jnp.minimum(jnp.maximum(result, -limit), limit).astype(kind)


def setup_inputs(seed: int = 0) -> dict:
    streams_of = jax.random.split(jax.random.key(seed), 12)
    return {
        "tokens": bell_draw(streams_of[0], (TOKENS, D), 1.0, 6.0, ((0, 16), (1, 2))),
        "out_grad": bell_draw(streams_of[1], (TOKENS, D), 1.0, 6.0, ((0, 16), (1, 2))),
        "route_ids": draw_route_ids(jax.random.fold_in(streams_of[11], 71), 0),
        "route_slots": draw_route_slots(jax.random.fold_in(streams_of[11], 71), 0),
        "route_weight": jnp.clip(0.19921875 + 0.80078125 * jax.random.uniform(streams_of[4], (TOKENS, TOPK), jnp.float32) ** block_scale(streams_of[4], (TOKENS, TOPK), ((0, 16),), -0.2, 0.2), 0.19921875, 1.0).astype(jnp.bfloat16),
        "w_gate": bell_draw(streams_of[5], (EXPERTS, D, FF), D ** -0.5, 0.09375, ((0, 4), (2, 8))),
        "w_up": bell_draw(streams_of[6], (EXPERTS, D, FF), D ** -0.5, 0.09375, ((0, 4), (2, 8))),
        "w_down": bell_draw(streams_of[7], (EXPERTS, FF, D), FF ** -0.5, 0.1875, ((0, 4), (1, 8))),
        "proj_hidden": bell_draw(streams_of[8], (EXPERTS, PROJ, FF), FF ** -0.5, 0.1875, ((0, 4), (2, 8))),
        "proj_grad": bell_draw(streams_of[9], (EXPERTS, PROJ, D), D ** -0.5, 0.09375, ((0, 4),)),
        "test_feats": bell_draw(streams_of[10], (EXPERTS, NTEST, PROJ * PROJ), (PROJ * PROJ) ** -0.5, 0.09375, ((0, 4), (1, 2))),
    }


def reference(tokens, out_grad, route_ids, route_slots, route_weight, w_gate, w_up, w_down, proj_hidden, proj_grad, test_feats):
    blocks = TOKENS // TOK_DEV
    slot_rows = blocks * CAP
    row_ids = jnp.arange(TOKENS, dtype=jnp.int32)
    live_mask = (route_slots >= 0) & (route_ids < EXPERTS)
    where_to = jnp.where(live_mask, route_ids * slot_rows + (row_ids // TOK_DEV)[:, None] * CAP + route_slots, EXPERTS * slot_rows).astype(jnp.int32)
    owners = jnp.broadcast_to(row_ids[:, None], where_to.shape).astype(jnp.int32)
    holder = jnp.full((EXPERTS * slot_rows,), TOKENS, jnp.int32).at[where_to.reshape(-1)].set(owners.reshape(-1), mode="drop")
    route_scale = jnp.zeros((EXPERTS * slot_rows,), jnp.float32).at[where_to.reshape(-1)].set(route_weight.astype(jnp.float32).reshape(-1), mode="drop")
    holder = holder.reshape(EXPERTS, slot_rows)
    route_scale = route_scale.reshape(EXPERTS, slot_rows)
    blocks_ff = N_DP * N_TEST
    ff_block = FF // blocks_ff

    def one_expert(totals, per_expert):
        grad_sum, score_sum = totals
        slot_owner, factor, gate_w, up_w, down_w, hid_proj, grad_proj, test_rows = per_expert
        valid_rows = slot_owner < TOKENS
        safe_index = jnp.minimum(slot_owner, TOKENS - 1).astype(jnp.int32)
        expert_in = jnp.where(valid_rows[:, None], tokens[safe_index], jnp.zeros((), tokens.dtype))
        expert_grad = (factor[:, None] * out_grad[safe_index].astype(jnp.float32)).astype(jnp.bfloat16)
        gate_pre = jnp.dot(expert_in, gate_w, preferred_element_type=jnp.float32)
        up_pre = jnp.dot(expert_in, up_w, preferred_element_type=jnp.float32)
        sigmoid_gate = jax.nn.sigmoid(gate_pre)
        act_gate = gate_pre * sigmoid_gate
        hidden = (act_gate * up_pre).astype(jnp.bfloat16)
        hidden_proj = jnp.dot(hidden, hid_proj.T, preferred_element_type=jnp.float32)
        grad_vec = jnp.dot(expert_grad, grad_proj.T, preferred_element_type=jnp.float32)
        hidden_grad = jnp.dot(expert_grad, down_w.T, preferred_element_type=jnp.float32)
        up_grad = (hidden_grad * act_gate).astype(jnp.bfloat16)
        gate_grad = (hidden_grad * up_pre * sigmoid_gate * (1.0 + gate_pre * (1.0 - sigmoid_gate))).astype(jnp.bfloat16)
        row_total = gate_grad.shape[0]
        pieces = jnp.einsum("rbf,dbf->brd", gate_grad.astype(jnp.float32).reshape(row_total, blocks_ff, ff_block), gate_w.astype(jnp.float32).reshape(D, blocks_ff, ff_block))
        pieces = pieces + jnp.einsum("rbf,dbf->brd", up_grad.astype(jnp.float32).reshape(row_total, blocks_ff, ff_block), up_w.astype(jnp.float32).reshape(D, blocks_ff, ff_block))
        pieces = lax.optimization_barrier(pieces.astype(jnp.bfloat16)).astype(jnp.float32)
        route_grad = jnp.sum(pieces, axis=0)
        feature = (hidden_proj[:, :, None] * grad_vec[:, None, :]).reshape(row_total, PROJ * PROJ).astype(jnp.bfloat16)
        route_score = jnp.dot(feature, test_rows.T, preferred_element_type=jnp.float32).astype(jnp.bfloat16)
        grad_sum = grad_sum.at[slot_owner].add(route_grad, mode="drop")
        score_sum = score_sum.at[slot_owner].add(route_score.astype(jnp.float32), mode="drop")
        return (grad_sum, score_sum), None

    initial = (jnp.zeros((TOKENS, D), jnp.float32), jnp.zeros((TOKENS, NTEST), jnp.float32))
    (grad_sum, score_sum), _ = lax.scan(one_expert, initial, (holder, route_scale, w_gate, w_up, w_down, proj_hidden, proj_grad, test_feats))
    return grad_sum.astype(jnp.bfloat16), score_sum
```

```python
import jax
import jax.numpy as jnp
from jax import lax
from jax.sharding import PartitionSpec as P

CAP = 2
PLANE = ("dp", "test")


def send_rel(block, axes, offset):
    size = lax.axis_size(axes)
    return lax.ppermute(block, axes, [(i, i ^ offset) for i in range(size)])


def pick_rows(ids_in, slots_in, weights_in, experts):
    rel = jnp.arange(experts * CAP, dtype=jnp.int32)
    here = lax.axis_index("expert")
    codes = ((rel // CAP) ^ here) * CAP + rel % CAP
    live_mask = (slots_in >= 0) & (ids_in < experts)
    slot_code = jnp.where(live_mask, ids_in * CAP + slots_in, -1)
    matches = slot_code[None, :, :] == codes[:, None, None]
    picks = jnp.sum(matches.astype(jnp.float32), axis=2)
    weighted = jnp.sum(jnp.where(matches, weights_in.astype(jnp.float32)[None], 0.0), axis=2)
    return picks.astype(jnp.bfloat16), weighted.astype(jnp.bfloat16)


def dot_f32(a, b, contract):
    return lax.dot_general(a, b, (contract, ((), ())), preferred_element_type=jnp.float32)


def on_device(
    tokens,
    out_grad,
    route_ids,
    route_slots,
    route_weight,
    w_gate,
    w_up,
    w_down,
    proj_hidden,
    proj_grad,
    test_feats,
):
    experts = lax.axis_size("expert")
    groups = lax.axis_size("dp")
    halves = lax.axis_size("test")
    plane = groups * halves
    half_width = tokens.shape[1]
    rows = experts * CAP
    core = lax.axis_index("test")
    gate_w, up_w, down_w = w_gate[0], w_up[0], w_down[0]
    hid_proj, grad_proj, test_rows = proj_hidden[0], proj_grad[0], test_feats[0]

    picks, weighted = pick_rows(route_ids, route_slots, route_weight, experts)
    own_in = dot_f32(picks, tokens, ((1,), (0,))).astype(jnp.bfloat16)
    own_grad = dot_f32(weighted, out_grad, ((1,), (0,))).astype(jnp.bfloat16)
    both = jnp.concatenate(
        [own_in.reshape(experts, CAP, half_width), own_grad.reshape(experts, CAP, half_width)], axis=1
    )
    arrived = [both[0]] + [send_rel(both[k], "expert", k) for k in range(1, experts)]
    block = jnp.stack(arrived)
    blocks = [block] + [send_rel(block, PLANE, j) for j in range(1, plane)]

    def side(half, first):
        return jnp.concatenate(
            [blocks[g * halves + half][:, first : first + CAP].reshape(rows, half_width) for g in range(groups)]
        )

    def whole(first):
        mine, other = side(0, first), side(1, first)
        return jnp.concatenate(
            [jnp.where(core == 0, mine, other), jnp.where(core == 0, other, mine)], axis=1
        )

    flat_in, flat_grad = whole(0), whole(CAP)
    gate_pre = dot_f32(flat_in, gate_w, ((1,), (0,)))
    up_pre = dot_f32(flat_in, up_w, ((1,), (0,)))
    sig = jax.nn.sigmoid(gate_pre)
    act_gate = gate_pre * sig
    hidden = (act_gate * up_pre).astype(jnp.bfloat16)
    hid_part = dot_f32(hidden, hid_proj, ((1,), (1,)))
    hid_high = hid_part.astype(jnp.bfloat16)
    hid_low = (hid_part - hid_high.astype(jnp.float32)).astype(jnp.bfloat16)
    hid_grad = dot_f32(flat_grad, down_w, ((1,), (1,)))
    up_grad = (hid_grad * act_gate).astype(jnp.bfloat16)
    gate_grad = (hid_grad * up_pre * sig * (1.0 + gate_pre * (1.0 - sig))).astype(jnp.bfloat16)
    parts = (
        dot_f32(gate_grad, gate_w, ((1,), (1,))) + dot_f32(up_grad, up_w, ((1,), (1,)))
    ).astype(jnp.bfloat16)
    low, high = parts[:, :half_width], parts[:, half_width:]
    sides = (jnp.where(core == 0, low, high), jnp.where(core == 0, high, low))
    tail = jnp.concatenate([hid_high, hid_low], axis=1)

    def outgoing(j):
        g, half = j // halves, j % halves
        cut = slice(g * rows, (g + 1) * rows)
        return jnp.concatenate([sides[half][cut], tail[cut]], axis=1)

    returned = [outgoing(0)] + [send_rel(outgoing(j), PLANE, j) for j in range(1, plane)]
    total = returned[0].astype(jnp.float32)
    for piece in returned[1:]:
        total = total + piece.astype(jnp.float32)
    proj = hid_part.shape[1]
    hid_mine = total[:, half_width : half_width + proj] + total[:, half_width + proj :]
    grad_mine = dot_f32(flat_grad[:rows], grad_proj, ((1,), (1,)))
    feature = (hid_mine[:, :, None] * grad_mine[:, None, :]).reshape(rows, -1).astype(jnp.bfloat16)
    route_score = dot_f32(feature, test_rows, ((1,), (1,)))
    back = jnp.concatenate([total[:, :half_width], route_score], axis=1).astype(jnp.bfloat16)
    back = back.reshape(experts, CAP, -1)
    home = [back[0]] + [send_rel(back[k], "expert", k) for k in range(1, experts)]
    home = jnp.concatenate(home, axis=0)
    result = dot_f32(picks, home, ((0,), (0,)))
    return result[:, :half_width].astype(jnp.bfloat16), result[:, half_width:]


def solution(mesh):
    placed = (
        P(("expert", "dp"), "test"),
        P(("expert", "dp"), "test"),
        P(("expert", "dp"), None),
        P(("expert", "dp"), None),
        P(("expert", "dp"), None),
        P("expert", None, ("dp", "test")),
        P("expert", None, ("dp", "test")),
        P("expert", ("dp", "test"), None),
        P("expert", None, ("dp", "test")),
        P("expert", None, None),
        P("expert", "test", None),
    )
    return jax.shard_map(
        on_device,
        mesh=mesh,
        in_specs=placed,
        out_specs=(P(("expert", "dp"), "test"), P(("expert", "dp"), "test")),
        check_vma=False,
    )
```

```python
import functools

import jax
import jax.numpy as jnp
from jax import lax
from jax.experimental import pallas as pl
from jax.experimental.pallas import tpu as pltpu
from jax.sharding import PartitionSpec as P

CAP = 2
KINDS = 4
BF16 = jnp.bfloat16
F32 = jnp.float32


def send_rel(block, axis, offset):
    size = lax.axis_size(axis)
    return lax.ppermute(block, axis, [(i, i ^ offset) for i in range(size)])


def dot_f32(a, b, contract):
    return lax.dot_general(a, b, (contract, ((), ())), preferred_element_type=F32)


def whole_vmem(count):
    return [pl.BlockSpec(memory_space=pltpu.VMEM)] * count


def in_hbm(count):
    return [pl.BlockSpec(memory_space=pltpu.HBM)] * count


def start_copies(pairs, sems):
    copies = [
        pltpu.make_async_copy(source, target, sems.at[index])
        for index, (source, target) in enumerate(pairs)
    ]
    for copy in copies:
        copy.start()
    return copies


def limit(rows):
    return pltpu.CompilerParams(vmem_limit_bytes=(8 << 20) + rows * (48 << 10))


def hit_tables(ids, slots, weights, want, experts):
    live = (slots >= 0) & (ids < experts)
    code = jnp.where(live, ids * CAP + slots, -1)
    hits = jnp.zeros((want.shape[0], ids.shape[1]), F32)
    scaled = hits
    for route in range(ids.shape[0]):
        match = code[route : route + 1, :] == want
        hits = jnp.where(match, 1.0, hits)
        scaled = jnp.where(match, weights[route : route + 1, :], scaled)
    return hits, scaled


def select_kernel(experts, *refs):
    sources, outs = refs[:5], refs[5 : 6 + experts]
    ids, slots, weight, tok, grad, sems = refs[6 + experts :]
    hit_ref, out_refs = outs[0], outs[1:]
    copies = start_copies(zip(sources, (ids, slots, weight, tok, grad)), sems)
    here = lax.axis_index("expert")
    unit = KINDS * CAP
    quarter = tok.shape[1] // 2
    row = lax.broadcasted_iota(jnp.int32, (experts * unit, 1), 0)
    kind = (row % unit) // CAP
    want = ((row // unit) ^ here) * CAP + row % CAP
    for copy in copies[:3]:
        copy.wait()
    hits, scaled = hit_tables(ids[...], slots[...], weight[...].astype(F32), want, experts)
    hit_ref[...] = hits
    total = None
    for index in range(KINDS):
        table, source = (hits, tok) if index < 2 else (scaled, grad)
        if index % 2 == 0:
            copies[3 + index // 2].wait()
        left = jnp.where(kind == index, table, 0.0).astype(BF16)
        first = (index % 2) * quarter
        part = dot_f32(left, source[:, first : first + quarter], ((1,), (0,)))
        total = part if total is None else total + part
    total = total.astype(BF16)
    for k in range(experts):
        out_refs[k][...] = total[k * unit : (k + 1) * unit]


def load_kernel(*refs):
    count = (len(refs) - 2) // 2
    for copy in start_copies(zip(refs[1 : 1 + count], refs[1 + count : -1]), refs[-1]):
        copy.wait()


def split_two(value):
    high = value.astype(BF16)
    return jnp.concatenate([high, (value - high.astype(F32)).astype(BF16)], axis=1)


def join_two(value):
    value = value.astype(F32)
    middle = value.shape[1] // 2
    return value[:, :middle] + value[:, middle:]


def expert_kernel(
    own_ref, other_ref, gate_w, up_w, down_w, proj_ref, keep_ref, send_ref, mine_ref, x_in, x_grad
):
    rows, width = x_in.shape
    half, quarter = width // 2, width // 4
    core = lax.axis_index("test")
    sides = (
        (own_ref, keep_ref, pl.multiple_of(core * half, 128)),
        (other_ref, send_ref, pl.multiple_of((1 - core) * half, 128)),
    )
    for source, _, base in sides:
        for index in range(KINDS):
            target = x_in if index < 2 else x_grad
            start = pl.multiple_of(base + (index % 2) * quarter, 128)
            target[:, pl.ds(start, quarter)] = source[index * rows : (index + 1) * rows]
    mine_ref[...] = x_grad[: mine_ref.shape[0]]
    gate_pre = dot_f32(x_in[...], gate_w[...], ((1,), (0,)))
    up_pre = dot_f32(x_in[...], up_w[...], ((1,), (0,)))
    hid_grad = dot_f32(x_grad[...], down_w[...], ((1,), (1,)))
    sig = 1.0 / (1.0 + jnp.exp(-gate_pre))
    act_gate = gate_pre * sig
    hidden = (act_gate * up_pre).astype(BF16)
    tail = split_two(dot_f32(hidden, proj_ref[...], ((1,), (1,))))
    up_grad = (hid_grad * act_gate).astype(BF16)
    gate_grad = (hid_grad * up_pre * sig * (1.0 + gate_pre * (1.0 - sig))).astype(BF16)
    for _, target, base in sides:
        target[:, half:] = tail
        for index in range(2):
            start = pl.multiple_of(base + index * quarter, 128)
            part = dot_f32(gate_grad, gate_w[pl.ds(start, quarter), :], ((1,), (1,)))
            part += dot_f32(up_grad, up_w[pl.ds(start, quarter), :], ((1,), (1,)))
            target[:, index * quarter : (index + 1) * quarter] = part.astype(BF16)


def pair_kernel(half, keep_ref, got_ref, *out_refs):
    kept, got = keep_ref[...].astype(F32), got_ref[...].astype(F32)
    main = (kept[:, :half] + got[:, :half]).astype(BF16)
    tail = split_two(join_two(kept[:, half:]) + join_two(got[:, half:]))
    rows = out_refs[0].shape[0]
    for g, out_ref in enumerate(out_refs):
        out_ref[:, :half] = main[g * rows : (g + 1) * rows]
        out_ref[:, half:] = tail[g * rows : (g + 1) * rows]


def score_kernel(half, *refs):
    *piece_refs, grad_ref, test_ref, out_ref, feature = refs
    total = piece_refs[0][...].astype(F32)
    for piece_ref in piece_refs[1:]:
        total = total + piece_ref[...].astype(F32)
    hid = join_two(total[:, half:])
    grad = grad_ref[...]
    proj = grad.shape[1]
    for p in range(proj):
        feature[:, p * proj : (p + 1) * proj] = (hid[:, p : p + 1] * grad).astype(BF16)
    out_ref[:, :half] = total[:, :half].astype(BF16)
    out_ref[:, half:] = dot_f32(feature[...], test_ref[...], ((1,), (1,))).astype(BF16)


def finish_kernel(hit_ref, home_ref, in_grad_ref, scores_ref):
    pairs, unit = home_ref.shape[0], KINDS * CAP
    hits = jnp.concatenate(
        [hit_ref[k * unit : k * unit + CAP] for k in range(pairs // CAP)], axis=0
    )
    half = in_grad_ref.shape[1]
    hits = hits.T.astype(BF16)
    in_grad_ref[...] = dot_f32(hits, home_ref[:, :half], ((1,), (0,))).astype(BF16)
    scores_ref[...] = dot_f32(hits, home_ref[:, half:], ((1,), (0,)))


def on_device(
    tokens,
    out_grad,
    route_ids,
    route_slots,
    route_weight,
    w_gate,
    w_up,
    w_down,
    proj_hidden,
    proj_grad,
    test_feats,
):
    experts = lax.axis_size("expert")
    groups = lax.axis_size("dp")
    tok_rows, half = tokens.shape
    quarter = half // 2
    width = half * lax.axis_size("test")
    proj, tests = proj_hidden.shape[1], test_feats.shape[1]
    pairs = experts * CAP
    rows = groups * pairs
    unit = KINDS * CAP
    out_width = half + 2 * proj
    ids_t, slots_t, weight_t = route_ids.T, route_slots.T, route_weight.T

    with jax.named_scope("select"):
        hits, *picked = pl.pallas_call(
            functools.partial(select_kernel, experts),
            out_shape=[jax.ShapeDtypeStruct((experts * unit, tok_rows), F32)]
            + [jax.ShapeDtypeStruct((unit, quarter), BF16)] * experts,
            in_specs=in_hbm(5),
            out_specs=whole_vmem(experts + 1),
            scratch_shapes=[
                pltpu.VMEM(x.shape, x.dtype) for x in (ids_t, slots_t, weight_t, tokens, out_grad)
            ]
            + [pltpu.SemaphoreType.DMA((5,))],
            compiler_params=limit(rows),
        )(ids_t, slots_t, weight_t, tokens, out_grad)
    params = [w_gate[0], w_up[0], w_down[0], proj_hidden[0], proj_grad[0], test_feats[0]]
    with jax.named_scope("load"):
        gate_w, up_w, down_w, hid_proj, grad_proj, test_rows = pl.pallas_call(
            load_kernel,
            out_shape=[jax.ShapeDtypeStruct(x.shape, x.dtype) for x in params],
            in_specs=whole_vmem(1) + in_hbm(len(params)),
            out_specs=whole_vmem(len(params)),
            scratch_shapes=[pltpu.SemaphoreType.DMA((len(params),))],
            compiler_params=limit(rows),
            cost_estimate=pl.CostEstimate(
                flops=0, bytes_accessed=sum(2 * x.size for x in params), transcendentals=0
            ),
        )(picked[0], *params)
    arrived = [picked[0]] + [send_rel(picked[k], "expert", k) for k in range(1, experts)]
    block = jnp.stack(arrived).reshape(experts, KINDS, CAP, quarter)
    block = block.transpose(1, 0, 2, 3).reshape(KINDS, pairs, quarter)
    blocks = [block] + [send_rel(block, "dp", g) for g in range(1, groups)]
    own = jnp.stack(blocks, axis=1).reshape(KINDS * rows, quarter)
    other = send_rel(own, "test", 1)

    with jax.named_scope("expert"):
        keep, send, mine = pl.pallas_call(
            expert_kernel,
            out_shape=[
                jax.ShapeDtypeStruct((rows, out_width), BF16),
                jax.ShapeDtypeStruct((rows, out_width), BF16),
                jax.ShapeDtypeStruct((pairs, width), BF16),
            ],
            in_specs=whole_vmem(6),
            out_specs=whole_vmem(3),
            scratch_shapes=[pltpu.VMEM((rows, width), BF16)] * 2,
            compiler_params=limit(rows),
        )(own, other, gate_w, up_w, down_w, hid_proj)
    got = send_rel(send, "test", 1)
    with jax.named_scope("pair"):
        sums = pl.pallas_call(
            functools.partial(pair_kernel, half),
            out_shape=[jax.ShapeDtypeStruct((pairs, out_width), BF16)] * groups,
            in_specs=whole_vmem(2),
            out_specs=whole_vmem(groups),
            compiler_params=limit(rows),
        )(keep, got)
    pieces = [sums[0]] + [send_rel(sums[g], "dp", g) for g in range(1, groups)]
    grad_mine = dot_f32(mine, grad_proj, ((1,), (1,)))
    with jax.named_scope("score"):
        back = pl.pallas_call(
            functools.partial(score_kernel, half),
            out_shape=jax.ShapeDtypeStruct((pairs, half + tests), BF16),
            in_specs=whole_vmem(groups + 2),
            out_specs=whole_vmem(1)[0],
            scratch_shapes=[pltpu.VMEM((pairs, proj * proj), BF16)],
            compiler_params=limit(rows),
        )(*pieces, grad_mine, test_rows)
    back = back.reshape(experts, CAP, half + tests)
    home = [back[0]] + [send_rel(back[k], "expert", k) for k in range(1, experts)]
    home = jnp.concatenate(home, axis=0)
    with jax.named_scope("finish"):
        return pl.pallas_call(
            finish_kernel,
            out_shape=[
                jax.ShapeDtypeStruct((tok_rows, half), BF16),
                jax.ShapeDtypeStruct((tok_rows, tests), F32),
            ],
            in_specs=whole_vmem(2),
            out_specs=whole_vmem(2),
            compiler_params=limit(rows),
        )(hits, home)


def solution(mesh):
    placed = (
        P(("expert", "dp"), "test"),
        P(("expert", "dp"), "test"),
        P(("expert", "dp"), None),
        P(("expert", "dp"), None),
        P(("expert", "dp"), None),
        P("expert", None, ("dp", "test")),
        P("expert", None, ("dp", "test")),
        P("expert", ("dp", "test"), None),
        P("expert", None, ("dp", "test")),
        P("expert", None, None),
        P("expert", "test", None),
    )
    return jax.shard_map(
        on_device,
        mesh=mesh,
        in_specs=placed,
        out_specs=(P(("expert", "dp"), "test"), P(("expert", "dp"), "test")),
        check_vma=False,
    )
```

```python
import functools

import jax
import jax.numpy as jnp
from jax import lax
from jax.experimental import pallas as pl
from jax.experimental.pallas import tpu as pltpu
from jax.sharding import PartitionSpec as P

CAP = 2
KINDS = 4
BF16 = jnp.bfloat16
F32 = jnp.float32


def send_rel(block, axis, offset):
    size = lax.axis_size(axis)
    return lax.ppermute(block, axis, [(i, i ^ offset) for i in range(size)])


def split_order(count):
    return list(range(0, count, 2)) + list(range(1, count, 2))


def exchange(stay, go, unit, count):
    order = split_order(count)
    half = count // 2
    slots = {}
    for index, k in enumerate(order[:half]):
        slots[k] = stay[index * unit : (index + 1) * unit]
    got = send_rel(go, "expert", 1)
    for index, k in enumerate(order[half:]):
        slots[k] = got[index * unit : (index + 1) * unit]
    bit = 2
    while bit < count:
        moving = [k for k in range(count) if k & bit]
        got = send_rel(jnp.concatenate([slots[k] for k in moving]), "expert", bit)
        for index, k in enumerate(moving):
            slots[k] = got[index * unit : (index + 1) * unit]
        bit *= 2
    return slots


def keep_in_hbm(array):
    return pltpu.with_memory_space_constraint(array, pltpu.HBM)


def dot_f32(a, b, contract):
    return lax.dot_general(a, b, (contract, ((), ())), preferred_element_type=F32)


def whole_vmem(count):
    return [pl.BlockSpec(memory_space=pltpu.VMEM)] * count


def in_hbm(count):
    return [pl.BlockSpec(memory_space=pltpu.HBM)] * count


def start_copies(pairs, sems):
    copies = [
        pltpu.make_async_copy(source, target, sems.at[index])
        for index, (source, target) in enumerate(pairs)
    ]
    for copy in copies:
        copy.start()
    return copies


def limit(rows):
    return pltpu.CompilerParams(vmem_limit_bytes=(8 << 20) + rows * (48 << 10))


def hit_tables(ids, slots, weights, want, experts):
    live = (slots >= 0) & (ids < experts)
    code = jnp.where(live, ids * CAP + slots, -1)
    hits = jnp.zeros((want.shape[0], ids.shape[1]), F32)
    scaled = hits
    for route in range(ids.shape[0]):
        match = code[route : route + 1, :] == want
        hits = jnp.where(match, 1.0, hits)
        scaled = jnp.where(match, weights[route : route + 1, :], scaled)
    return hits, scaled


def select_kernel(experts, *refs):
    sources, (hit_ref, *out_refs) = refs[:5], refs[5:8]
    ids, slots, weight, tok, grad, sems = refs[8:]
    copies = start_copies(zip(sources, (ids, slots, weight, tok, grad)), sems)
    here = lax.axis_index("expert")
    unit = KINDS * CAP
    quarter = tok.shape[1] // 2
    row = lax.broadcasted_iota(jnp.int32, (experts * unit, 1), 0)
    kind = (row % unit) // CAP
    turn = 2 * (row // unit)
    want = ((turn % experts + turn // experts) ^ here) * CAP + row % CAP
    for copy in copies[:3]:
        copy.wait()
    hits, scaled = hit_tables(ids[...], slots[...], weight[...].astype(F32), want, experts)
    hit_ref[...] = hits
    total = None
    for index in range(KINDS):
        table, source = (hits, tok) if index < 2 else (scaled, grad)
        if index % 2 == 0:
            copies[3 + index // 2].wait()
        left = jnp.where(kind == index, table, 0.0).astype(BF16)
        first = (index % 2) * quarter
        part = dot_f32(left, source[:, first : first + quarter], ((1,), (0,)))
        total = part if total is None else total + part
    total = total.astype(BF16)
    sent = experts * unit // 2
    out_refs[0][...] = total[:sent]
    out_refs[1][...] = total[sent:]


def load_kernel(*refs):
    count = (len(refs) - 2) // 2
    for copy in start_copies(zip(refs[1 : 1 + count], refs[1 + count : -1]), refs[-1]):
        copy.wait()


def split_two(value):
    high = value.astype(BF16)
    return jnp.concatenate([high, (value - high.astype(F32)).astype(BF16)], axis=1)


def join_two(value):
    value = value.astype(F32)
    middle = value.shape[1] // 2
    return value[:, :middle] + value[:, middle:]


def expert_kernel(
    own_ref, other_ref, gate_w, up_w, down_w, proj_ref, keep_ref, send_ref, mine_ref, x_in, x_grad
):
    rows, width = x_in.shape
    half, quarter = width // 2, width // 4
    core = lax.axis_index("test")
    sides = (
        (own_ref, keep_ref, pl.multiple_of(core * half, 128)),
        (other_ref, send_ref, pl.multiple_of((1 - core) * half, 128)),
    )
    for source, _, base in sides:
        for index in range(KINDS):
            target = x_in if index < 2 else x_grad
            start = pl.multiple_of(base + (index % 2) * quarter, 128)
            target[:, pl.ds(start, quarter)] = source[index * rows : (index + 1) * rows]
    mine_ref[...] = x_grad[: mine_ref.shape[0]]
    gate_pre = dot_f32(x_in[...], gate_w[...], ((1,), (0,)))
    up_pre = dot_f32(x_in[...], up_w[...], ((1,), (0,)))
    hid_grad = dot_f32(x_grad[...], down_w[...], ((1,), (1,)))
    sig = 1.0 / (1.0 + jnp.exp(-gate_pre))
    act_gate = gate_pre * sig
    hidden = (act_gate * up_pre).astype(BF16)
    tail = split_two(dot_f32(hidden, proj_ref[...], ((1,), (1,))))
    up_grad = (hid_grad * act_gate).astype(BF16)
    gate_grad = (hid_grad * up_pre * sig * (1.0 + gate_pre * (1.0 - sig))).astype(BF16)
    for _, target, base in sides:
        target[:, half:] = tail
        for index in range(2):
            start = pl.multiple_of(base + index * quarter, 128)
            part = dot_f32(gate_grad, gate_w[pl.ds(start, quarter), :], ((1,), (1,)))
            part += dot_f32(up_grad, up_w[pl.ds(start, quarter), :], ((1,), (1,)))
            target[:, index * quarter : (index + 1) * quarter] = part.astype(BF16)


def pair_kernel(half, keep_ref, got_ref, *out_refs):
    kept, got = keep_ref[...].astype(F32), got_ref[...].astype(F32)
    main = (kept[:, :half] + got[:, :half]).astype(BF16)
    tail = split_two(join_two(kept[:, half:]) + join_two(got[:, half:]))
    rows = out_refs[0].shape[0]
    for g, out_ref in enumerate(out_refs):
        out_ref[:, :half] = main[g * rows : (g + 1) * rows]
        out_ref[:, half:] = tail[g * rows : (g + 1) * rows]


def score_kernel(half, *refs):
    *piece_refs, grad_ref, test_ref, out_ref, feature = refs
    total = piece_refs[0][...].astype(F32)
    for piece_ref in piece_refs[1:]:
        total = total + piece_ref[...].astype(F32)
    hid = join_two(total[:, half:])
    grad = grad_ref[...]
    proj = grad.shape[1]
    for p in range(proj):
        feature[:, p * proj : (p + 1) * proj] = (hid[:, p : p + 1] * grad).astype(BF16)
    out_ref[:, :half] = total[:, :half].astype(BF16)
    out_ref[:, half:] = dot_f32(feature[...], test_ref[...], ((1,), (1,))).astype(BF16)


def finish_kernel(hit_ref, home_ref, in_grad_ref, scores_ref):
    pairs, unit = home_ref.shape[0], KINDS * CAP
    hits = jnp.concatenate(
        [hit_ref[k * unit : k * unit + CAP] for k in range(pairs // CAP)], axis=0
    )
    half = in_grad_ref.shape[1]
    hits = hits.T.astype(BF16)
    in_grad_ref[...] = dot_f32(hits, home_ref[:, :half], ((1,), (0,))).astype(BF16)
    scores_ref[...] = dot_f32(hits, home_ref[:, half:], ((1,), (0,)))


def on_device(
    tokens,
    out_grad,
    route_ids,
    route_slots,
    route_weight,
    w_gate,
    w_up,
    w_down,
    proj_hidden,
    proj_grad,
    test_feats,
):
    experts = lax.axis_size("expert")
    groups = lax.axis_size("dp")
    tok_rows, half = tokens.shape
    quarter = half // 2
    width = half * lax.axis_size("test")
    proj, tests = proj_hidden.shape[1], test_feats.shape[1]
    pairs = experts * CAP
    rows = groups * pairs
    unit = KINDS * CAP
    out_width = half + 2 * proj
    ids_t, slots_t, weight_t = route_ids.T, route_slots.T, route_weight.T

    with jax.named_scope("select"):
        hits, stay, go = pl.pallas_call(
            functools.partial(select_kernel, experts),
            out_shape=[jax.ShapeDtypeStruct((experts * unit, tok_rows), F32)]
            + [jax.ShapeDtypeStruct((experts * unit // 2, quarter), BF16)] * 2,
            in_specs=in_hbm(5),
            out_specs=whole_vmem(3),
            scratch_shapes=[
                pltpu.VMEM(x.shape, x.dtype) for x in (ids_t, slots_t, weight_t, tokens, out_grad)
            ]
            + [pltpu.SemaphoreType.DMA((5,))],
            compiler_params=limit(rows),
        )(*map(keep_in_hbm, (ids_t, slots_t, weight_t, tokens, out_grad)))
    params = [w_gate[0], w_up[0], w_down[0], proj_hidden[0], proj_grad[0], test_feats[0]]
    with jax.named_scope("load"):
        gate_w, up_w, down_w, hid_proj, grad_proj, test_rows = pl.pallas_call(
            load_kernel,
            out_shape=[jax.ShapeDtypeStruct(x.shape, x.dtype) for x in params],
            in_specs=whole_vmem(1) + in_hbm(len(params)),
            out_specs=whole_vmem(len(params)),
            scratch_shapes=[pltpu.SemaphoreType.DMA((len(params),))],
            compiler_params=limit(rows),
            cost_estimate=pl.CostEstimate(
                flops=0, bytes_accessed=sum(2 * x.size for x in params), transcendentals=0
            ),
        )(stay, *map(keep_in_hbm, params))
    slots = exchange(stay, go, unit, experts)
    block = jnp.stack([slots[k] for k in range(experts)]).reshape(experts, KINDS, CAP, quarter)
    block = block.transpose(1, 0, 2, 3).reshape(KINDS, pairs, quarter)
    blocks = [block] + [send_rel(block, "dp", g) for g in range(1, groups)]
    own = jnp.stack(blocks, axis=1).reshape(KINDS * rows, quarter)
    other = send_rel(own, "test", 1)

    with jax.named_scope("expert"):
        keep, send, mine = pl.pallas_call(
            expert_kernel,
            out_shape=[
                jax.ShapeDtypeStruct((rows, out_width), BF16),
                jax.ShapeDtypeStruct((rows, out_width), BF16),
                jax.ShapeDtypeStruct((pairs, width), BF16),
            ],
            in_specs=whole_vmem(6),
            out_specs=whole_vmem(3),
            scratch_shapes=[pltpu.VMEM((rows, width), BF16)] * 2,
            compiler_params=limit(rows),
        )(own, other, gate_w, up_w, down_w, hid_proj)
    got = send_rel(send, "test", 1)
    with jax.named_scope("pair"):
        sums = pl.pallas_call(
            functools.partial(pair_kernel, half),
            out_shape=[jax.ShapeDtypeStruct((pairs, out_width), BF16)] * groups,
            in_specs=whole_vmem(2),
            out_specs=whole_vmem(groups),
            compiler_params=limit(rows),
        )(keep, got)
    pieces = [sums[0]] + [send_rel(sums[g], "dp", g) for g in range(1, groups)]
    grad_mine = dot_f32(mine, grad_proj, ((1,), (1,)))
    with jax.named_scope("score"):
        back = pl.pallas_call(
            functools.partial(score_kernel, half),
            out_shape=jax.ShapeDtypeStruct((pairs, half + tests), BF16),
            in_specs=whole_vmem(groups + 2),
            out_specs=whole_vmem(1)[0],
            scratch_shapes=[pltpu.VMEM((pairs, proj * proj), BF16)],
            compiler_params=limit(rows),
        )(*pieces, grad_mine, test_rows)
    order = split_order(experts)
    back = jnp.concatenate([back[k * CAP : (k + 1) * CAP] for k in order])
    slots = exchange(back[: pairs // 2], back[pairs // 2 :], CAP, experts)
    home = jnp.concatenate([slots[k] for k in order])
    with jax.named_scope("finish"):
        return pl.pallas_call(
            finish_kernel,
            out_shape=[
                jax.ShapeDtypeStruct((tok_rows, half), BF16),
                jax.ShapeDtypeStruct((tok_rows, tests), F32),
            ],
            in_specs=whole_vmem(2),
            out_specs=whole_vmem(2),
            compiler_params=limit(rows),
        )(hits, home)


def solution(mesh):
    placed = (
        P(("expert", "dp"), "test"),
        P(("expert", "dp"), "test"),
        P(("expert", "dp"), None),
        P(("expert", "dp"), None),
        P(("expert", "dp"), None),
        P("expert", None, ("dp", "test")),
        P("expert", None, ("dp", "test")),
        P("expert", ("dp", "test"), None),
        P("expert", None, ("dp", "test")),
        P("expert", None, None),
        P("expert", "test", None),
    )
    return jax.shard_map(
        on_device,
        mesh=mesh,
        in_specs=placed,
        out_specs=(P(("expert", "dp"), "test"), P(("expert", "dp"), "test")),
        check_vma=False,
    )
```

```python
import functools

import jax
import jax.numpy as jnp
from jax import lax
from jax.experimental import pallas as pl
from jax.experimental.pallas import tpu as pltpu
from jax.sharding import PartitionSpec as P

CAP = 2
KINDS = 4
BF16 = jnp.bfloat16
F32 = jnp.float32


def send_rel(block, axis, offset):
    size = lax.axis_size(axis)
    return lax.ppermute(block, axis, [(i, i ^ offset) for i in range(size)])


def send_cross(block, axis, offset):
    return send_rel(block, (axis, "test"), offset * lax.axis_size("test") + 1)


def split_order(count):
    return list(range(0, count, 2)) + list(range(1, count, 2))


def exchange(send, stay, go, unit, count):
    order = split_order(count)
    half = count // 2
    slots = {}
    for index, k in enumerate(order[:half]):
        slots[k] = stay[index * unit : (index + 1) * unit]
    got = send(go, "expert", 1)
    for index, k in enumerate(order[half:]):
        slots[k] = got[index * unit : (index + 1) * unit]
    bit = 2
    while bit < count:
        moving = [k for k in range(count) if k & bit]
        got = send(jnp.concatenate([slots[k] for k in moving]), "expert", bit)
        for index, k in enumerate(moving):
            slots[k] = got[index * unit : (index + 1) * unit]
        bit *= 2
    return slots


def keep_in_hbm(array):
    return pltpu.with_memory_space_constraint(array, pltpu.HBM)


def dot_f32(a, b, contract):
    return lax.dot_general(a, b, (contract, ((), ())), preferred_element_type=F32)


def whole_vmem(count):
    return [pl.BlockSpec(memory_space=pltpu.VMEM)] * count


def in_hbm(count):
    return [pl.BlockSpec(memory_space=pltpu.HBM)] * count


def start_copies(pairs, sems):
    copies = [
        pltpu.make_async_copy(source, target, sems.at[index])
        for index, (source, target) in enumerate(pairs)
    ]
    for copy in copies:
        copy.start()
    return copies


def limit(rows):
    return pltpu.CompilerParams(vmem_limit_bytes=(8 << 20) + rows * (48 << 10))


def hit_tables(ids, slots, weights, want, experts):
    live = (slots >= 0) & (ids < experts)
    code = jnp.where(live, ids * CAP + slots, -1)
    hits = jnp.zeros((want.shape[0], ids.shape[1]), F32)
    scaled = hits
    for route in range(ids.shape[0]):
        match = code[route : route + 1, :] == want
        hits = jnp.where(match, 1.0, hits)
        scaled = jnp.where(match, weights[route : route + 1, :], scaled)
    return hits, scaled


def select_kernel(experts, *refs):
    sources, (hit_ref, *out_refs) = refs[:5], refs[5:8]
    ids, slots, weight, tok, grad, sems = refs[8:]
    copies = start_copies(zip(sources, (ids, slots, weight, tok, grad)), sems)
    here = lax.axis_index("expert")
    unit = KINDS * CAP
    quarter = tok.shape[1] // 2
    row = lax.broadcasted_iota(jnp.int32, (experts * unit, 1), 0)
    kind = (row % unit) // CAP
    turn = 2 * (row // unit)
    want = ((turn % experts + turn // experts) ^ here) * CAP + row % CAP
    for copy in copies[:3]:
        copy.wait()
    hits, scaled = hit_tables(ids[...], slots[...], weight[...].astype(F32), want, experts)
    hit_ref[...] = hits
    total = None
    for index in range(KINDS):
        table, source = (hits, tok) if index < 2 else (scaled, grad)
        if index % 2 == 0:
            copies[3 + index // 2].wait()
        left = jnp.where(kind == index, table, 0.0).astype(BF16)
        first = (index % 2) * quarter
        part = dot_f32(left, source[:, first : first + quarter], ((1,), (0,)))
        total = part if total is None else total + part
    total = total.astype(BF16)
    sent = experts * unit // 2
    out_refs[0][...] = total[:sent]
    out_refs[1][...] = total[sent:]


def load_kernel(*refs):
    count = (len(refs) - 2) // 2
    for copy in start_copies(zip(refs[1 : 1 + count], refs[1 + count : -1]), refs[-1]):
        copy.wait()


def split_two(value):
    high = value.astype(BF16)
    return jnp.concatenate([high, (value - high.astype(F32)).astype(BF16)], axis=1)


def join_two(value):
    value = value.astype(F32)
    middle = value.shape[1] // 2
    return value[:, :middle] + value[:, middle:]


def expert_kernel(
    own_ref, other_ref, gate_w, up_w, down_w, proj_ref, keep_ref, send_ref, mine_ref, x_in, x_grad
):
    rows, width = x_in.shape
    half, quarter = width // 2, width // 4
    pairs = mine_ref.shape[0]
    core = lax.axis_index("test")
    near, far = pl.multiple_of(core * half, 128), pl.multiple_of((1 - core) * half, 128)
    row = lax.broadcasted_iota(jnp.int32, (rows, quarter), 0)
    odd = jnp.where(row >= pairs, 1, 0)
    bits = (row % pairs) // CAP
    for _ in range(max(1, (pairs // CAP - 1).bit_length())):
        odd = odd ^ (bits & 1)
        bits = bits // 2
    odd = odd == 1
    for index in range(KINDS):
        target = x_in if index < 2 else x_grad
        own = own_ref[index * rows : (index + 1) * rows]
        other = other_ref[index * rows : (index + 1) * rows]
        first = (index % 2) * quarter
        target[:, pl.ds(pl.multiple_of(near + first, 128), quarter)] = jnp.where(odd, other, own)
        target[:, pl.ds(pl.multiple_of(far + first, 128), quarter)] = jnp.where(odd, own, other)
    mine_ref[...] = x_grad[:pairs]
    gate_pre = dot_f32(x_in[...], gate_w[...], ((1,), (0,)))
    up_pre = dot_f32(x_in[...], up_w[...], ((1,), (0,)))
    hid_grad = dot_f32(x_grad[...], down_w[...], ((1,), (1,)))
    sig = 1.0 / (1.0 + jnp.exp(-gate_pre))
    act_gate = gate_pre * sig
    hidden = (act_gate * up_pre).astype(BF16)
    tail = split_two(dot_f32(hidden, proj_ref[...], ((1,), (1,))))
    up_grad = (hid_grad * act_gate).astype(BF16)
    gate_grad = (hid_grad * up_pre * sig * (1.0 + gate_pre * (1.0 - sig))).astype(BF16)
    keep_ref[:, half:] = tail
    send_ref[:, half:] = tail
    for base, first_ref, rest_ref in ((far, send_ref, keep_ref), (near, keep_ref, send_ref)):
        for index in range(2):
            start = pl.multiple_of(base + index * quarter, 128)
            columns = slice(index * quarter, (index + 1) * quarter)
            part = dot_f32(gate_grad, gate_w[pl.ds(start, quarter), :], ((1,), (1,)))
            part += dot_f32(up_grad, up_w[pl.ds(start, quarter), :], ((1,), (1,)))
            part = part.astype(BF16)
            first_ref[:pairs, columns] = part[:pairs]
            rest_ref[pairs:, columns] = part[pairs:]


def pair_kernel(half, keep_ref, got_ref, *out_refs):
    kept, got = keep_ref[...].astype(F32), got_ref[...].astype(F32)
    main = (kept[:, :half] + got[:, :half]).astype(BF16)
    tail = split_two(join_two(kept[:, half:]) + join_two(got[:, half:]))
    rows = out_refs[0].shape[0]
    for g, out_ref in enumerate(out_refs):
        out_ref[:, :half] = main[g * rows : (g + 1) * rows]
        out_ref[:, half:] = tail[g * rows : (g + 1) * rows]


def score_kernel(half, *refs):
    *piece_refs, grad_ref, test_ref, out_ref, feature = refs
    total = piece_refs[0][...].astype(F32)
    for piece_ref in piece_refs[1:]:
        total = total + piece_ref[...].astype(F32)
    hid = join_two(total[:, half:])
    grad = grad_ref[...]
    proj = grad.shape[1]
    for p in range(proj):
        feature[:, p * proj : (p + 1) * proj] = (hid[:, p : p + 1] * grad).astype(BF16)
    out_ref[:, :half] = total[:, :half].astype(BF16)
    out_ref[:, half:] = dot_f32(feature[...], test_ref[...], ((1,), (1,))).astype(BF16)


def finish_kernel(hit_ref, home_ref, in_grad_hbm, scores_hbm, in_grad, scores, sems):
    pairs, unit = home_ref.shape[0], KINDS * CAP
    hits = jnp.concatenate(
        [hit_ref[k * unit : k * unit + CAP] for k in range(pairs // CAP)], axis=0
    )
    half = in_grad.shape[1]
    quarter = half // 2
    hits = hits.T.astype(BF16)
    copies = []
    for index in range(2):
        columns = slice(index * quarter, (index + 1) * quarter)
        in_grad[:, columns] = dot_f32(hits, home_ref[:, columns], ((1,), (0,))).astype(BF16)
        copies += start_copies(
            [(in_grad.at[:, columns], in_grad_hbm.at[:, columns])], sems.at[pl.ds(index, 1)]
        )
    scores[...] = dot_f32(hits, home_ref[:, half:], ((1,), (0,)))
    copies += start_copies([(scores, scores_hbm)], sems.at[pl.ds(2, 1)])
    for copy in copies:
        copy.wait()


def on_device(
    tokens,
    out_grad,
    route_ids,
    route_slots,
    route_weight,
    w_gate,
    w_up,
    w_down,
    proj_hidden,
    proj_grad,
    test_feats,
):
    experts = lax.axis_size("expert")
    groups = lax.axis_size("dp")
    tok_rows, half = tokens.shape
    quarter = half // 2
    width = half * lax.axis_size("test")
    proj, tests = proj_hidden.shape[1], test_feats.shape[1]
    pairs = experts * CAP
    rows = groups * pairs
    unit = KINDS * CAP
    out_width = half + 2 * proj
    ids_t, slots_t, weight_t = route_ids.T, route_slots.T, route_weight.T

    with jax.named_scope("select"):
        hits, stay, go = pl.pallas_call(
            functools.partial(select_kernel, experts),
            out_shape=[jax.ShapeDtypeStruct((experts * unit, tok_rows), F32)]
            + [jax.ShapeDtypeStruct((experts * unit // 2, quarter), BF16)] * 2,
            in_specs=in_hbm(5),
            out_specs=whole_vmem(3),
            scratch_shapes=[
                pltpu.VMEM(x.shape, x.dtype) for x in (ids_t, slots_t, weight_t, tokens, out_grad)
            ]
            + [pltpu.SemaphoreType.DMA((5,))],
            compiler_params=limit(rows),
        )(*map(keep_in_hbm, (ids_t, slots_t, weight_t, tokens, out_grad)))
    params = [w_gate[0], w_up[0], w_down[0], proj_hidden[0], proj_grad[0], test_feats[0]]
    with jax.named_scope("load"):
        loaded = pl.pallas_call(
            load_kernel,
            out_shape=[jax.ShapeDtypeStruct(x.shape, x.dtype) for x in params],
            in_specs=whole_vmem(1) + in_hbm(len(params)),
            out_specs=whole_vmem(len(params)),
            scratch_shapes=[pltpu.SemaphoreType.DMA((len(params),))],
            compiler_params=limit(rows),
            cost_estimate=pl.CostEstimate(
                flops=0, bytes_accessed=sum(2 * x.size for x in params), transcendentals=0
            ),
        )(stay, *map(keep_in_hbm, params))
    slots = exchange(send_cross, stay, go, unit, experts)
    loaded, slots = lax.optimization_barrier((loaded, slots))
    gate_w, up_w, down_w, hid_proj, grad_proj, test_rows = loaded
    block = jnp.stack([slots[k] for k in range(experts)]).reshape(experts, KINDS, CAP, quarter)
    block = block.transpose(1, 0, 2, 3).reshape(KINDS, pairs, quarter)
    blocks = [block] + [send_cross(block, "dp", g) for g in range(1, groups)]
    own = jnp.stack(blocks, axis=1).reshape(KINDS * rows, quarter)
    other = send_rel(own, "test", 1)

    with jax.named_scope("expert"):
        keep, send, mine = pl.pallas_call(
            expert_kernel,
            out_shape=[
                jax.ShapeDtypeStruct((rows, out_width), BF16),
                jax.ShapeDtypeStruct((rows, out_width), BF16),
                jax.ShapeDtypeStruct((pairs, width), BF16),
            ],
            in_specs=whole_vmem(6),
            out_specs=whole_vmem(3),
            scratch_shapes=[pltpu.VMEM((rows, width), BF16)] * 2,
            compiler_params=limit(rows),
        )(own, other, gate_w, up_w, down_w, hid_proj)
    got = send_rel(send, "test", 1)
    with jax.named_scope("pair"):
        sums = pl.pallas_call(
            functools.partial(pair_kernel, half),
            out_shape=[jax.ShapeDtypeStruct((pairs, out_width), BF16)] * groups,
            in_specs=whole_vmem(2),
            out_specs=whole_vmem(groups),
            compiler_params=limit(rows),
        )(keep, got)
    pieces = [sums[0]] + [send_cross(sums[g], "dp", g) for g in range(1, groups)]
    grad_mine = dot_f32(mine, grad_proj, ((1,), (1,)))
    with jax.named_scope("score"):
        back = pl.pallas_call(
            functools.partial(score_kernel, half),
            out_shape=jax.ShapeDtypeStruct((pairs, half + tests), BF16),
            in_specs=whole_vmem(groups + 2),
            out_specs=whole_vmem(1)[0],
            scratch_shapes=[pltpu.VMEM((pairs, proj * proj), BF16)],
            compiler_params=limit(rows),
        )(*pieces, grad_mine, test_rows)
    order = split_order(experts)
    back = jnp.concatenate([back[k * CAP : (k + 1) * CAP] for k in order])
    slots = exchange(send_rel, back[: pairs // 2], back[pairs // 2 :], CAP, experts)
    home = jnp.concatenate([slots[k] for k in order])
    with jax.named_scope("finish"):
        return pl.pallas_call(
            finish_kernel,
            out_shape=[
                jax.ShapeDtypeStruct((tok_rows, half), BF16),
                jax.ShapeDtypeStruct((tok_rows, tests), F32),
            ],
            in_specs=whole_vmem(2),
            out_specs=in_hbm(2),
            scratch_shapes=[
                pltpu.VMEM((tok_rows, half), BF16),
                pltpu.VMEM((tok_rows, tests), F32),
                pltpu.SemaphoreType.DMA((3,)),
            ],
            compiler_params=limit(rows),
        )(hits, home)


def solution(mesh):
    placed = (
        P(("expert", "dp"), "test"),
        P(("expert", "dp"), "test"),
        P(("expert", "dp"), None),
        P(("expert", "dp"), None),
        P(("expert", "dp"), None),
        P("expert", None, ("dp", "test")),
        P("expert", None, ("dp", "test")),
        P("expert", ("dp", "test"), None),
        P("expert", None, ("dp", "test")),
        P("expert", None, None),
        P("expert", "test", None),
    )
    return jax.shard_map(
        on_device,
        mesh=mesh,
        in_specs=placed,
        out_specs=(P(("expert", "dp"), "test"), P(("expert", "dp"), "test")),
        check_vma=False,
    )
```

```python
import functools

import jax
import jax.numpy as jnp
from jax import lax
from jax.experimental import pallas as pl
from jax.experimental.pallas import tpu as pltpu
from jax.sharding import PartitionSpec as P

CAP = 2
KINDS = 4
BF16 = jnp.bfloat16
F32 = jnp.float32


def send_rel(block, axis, offset):
    size = lax.axis_size(axis)
    return lax.ppermute(block, axis, [(i, i ^ offset) for i in range(size)])


def send_cross(block, axis, offset):
    return send_rel(block, (axis, "test"), offset * lax.axis_size("test") + 1)


def is_direct(count):
    return count <= 4


def slot_order(count):
    slots = list(range(count))
    return slots if is_direct(count) else slots[::2] + slots[1::2]


def exchange(send, parts, count):
    slots = dict(zip(slot_order(count), parts))
    if is_direct(count):
        return [slots[0]] + [send(slots[k], "expert", k) for k in range(1, count)]
    unit = parts[0].shape[0]
    bit = 1
    while bit < count:
        moving = [k for k in range(count) if k & bit]
        got = send(jnp.concatenate([slots[k] for k in moving]), "expert", bit)
        for index, k in enumerate(moving):
            slots[k] = got[index * unit : (index + 1) * unit]
        bit *= 2
    return [slots[k] for k in range(count)]


def keep_in_hbm(array):
    return pltpu.with_memory_space_constraint(array, pltpu.HBM)


def dot_f32(a, b, contract):
    return lax.dot_general(a, b, (contract, ((), ())), preferred_element_type=F32)


def whole_vmem(count):
    return [pl.BlockSpec(memory_space=pltpu.VMEM)] * count


def in_hbm(count):
    return [pl.BlockSpec(memory_space=pltpu.HBM)] * count


def start_copies(pairs, sems):
    copies = [
        pltpu.make_async_copy(source, target, sems.at[index])
        for index, (source, target) in enumerate(pairs)
    ]
    for copy in copies:
        copy.start()
    return copies


def limit(rows):
    return pltpu.CompilerParams(vmem_limit_bytes=(8 << 20) + rows * (48 << 10))


def hit_tables(ids, slots, weights, want, experts):
    live = (slots >= 0) & (ids < experts)
    code = jnp.where(live, ids * CAP + slots, -1)
    hits = jnp.zeros((want.shape[0], ids.shape[1]), F32)
    scaled = hits
    for route in range(ids.shape[0]):
        match = code[route : route + 1, :] == want
        hits = jnp.where(match, 1.0, hits)
        scaled = jnp.where(match, weights[route : route + 1, :], scaled)
    return hits, scaled


def select_kernel(experts, *refs):
    sources, (hit_ref, *out_refs) = refs[:5], refs[5:-6]
    ids, slots, weight, tok, grad, sems = refs[-6:]
    copies = start_copies(zip(sources, (ids, slots, weight, tok, grad)), sems)
    here = lax.axis_index("expert")
    unit = KINDS * CAP
    quarter = tok.shape[1] // 2
    row = lax.broadcasted_iota(jnp.int32, (experts * unit, 1), 0)
    kind = (row % unit) // CAP
    turn = row // unit
    if not is_direct(experts):
        turn = 2 * turn % experts + 2 * turn // experts
    want = (turn ^ here) * CAP + row % CAP
    for copy in copies[:3]:
        copy.wait()
    hits, scaled = hit_tables(ids[...], slots[...], weight[...].astype(F32), want, experts)
    hit_ref[...] = hits
    total = None
    for index in range(KINDS):
        table, source = (hits, tok) if index < 2 else (scaled, grad)
        if index % 2 == 0:
            copies[3 + index // 2].wait()
        left = jnp.where(kind == index, table, 0.0).astype(BF16)
        first = (index % 2) * quarter
        part = dot_f32(left, source[:, first : first + quarter], ((1,), (0,)))
        total = part if total is None else total + part
    total = total.astype(BF16)
    for k, out_ref in enumerate(out_refs):
        out_ref[...] = total[k * unit : (k + 1) * unit]


def load_kernel(*refs):
    count = (len(refs) - 2) // 2
    for copy in start_copies(zip(refs[1 : 1 + count], refs[1 + count : -1]), refs[-1]):
        copy.wait()


def split_two(value):
    high = value.astype(BF16)
    return jnp.concatenate([high, (value - high.astype(F32)).astype(BF16)], axis=1)


def join_two(value):
    value = value.astype(F32)
    middle = value.shape[1] // 2
    return value[:, :middle] + value[:, middle:]


def load(after, params, compiler_params):
    with jax.named_scope("load"):
        return pl.pallas_call(
            load_kernel,
            out_shape=[jax.ShapeDtypeStruct(x.shape, x.dtype) for x in params],
            in_specs=whole_vmem(1) + in_hbm(len(params)),
            out_specs=whole_vmem(len(params)),
            scratch_shapes=[pltpu.SemaphoreType.DMA((len(params),))],
            compiler_params=compiler_params,
            cost_estimate=pl.CostEstimate(
                flops=0, bytes_accessed=sum(2 * x.size for x in params), transcendentals=0
            ),
        )(after, *map(keep_in_hbm, params))


def expert_kernel(
    own_ref, other_ref, gate_w, up_w, down_w, proj_ref, keep_ref, send_ref, mine_ref, x_in, x_grad
):
    rows, width = x_in.shape
    half, quarter = width // 2, width // 4
    pairs = mine_ref.shape[0]
    core = lax.axis_index("test")
    near, far = pl.multiple_of(core * half, 128), pl.multiple_of((1 - core) * half, 128)
    row = lax.broadcasted_iota(jnp.int32, (rows, quarter), 0)
    odd = jnp.where(row >= pairs, 1, 0)
    slot = (row % pairs) // CAP
    if is_direct(pairs // CAP):
        odd = odd ^ jnp.where(slot > 0, 1, 0)
    else:
        for shift in range((pairs // CAP - 1).bit_length()):
            odd = odd ^ ((slot >> shift) & 1)
    odd = odd == 1
    for index in range(KINDS):
        target = x_in if index < 2 else x_grad
        own = own_ref[index * rows : (index + 1) * rows]
        other = other_ref[index * rows : (index + 1) * rows]
        first = (index % 2) * quarter
        target[:, pl.ds(pl.multiple_of(near + first, 128), quarter)] = jnp.where(odd, other, own)
        target[:, pl.ds(pl.multiple_of(far + first, 128), quarter)] = jnp.where(odd, own, other)
    mine_ref[...] = x_grad[:pairs]
    gate_pre = dot_f32(x_in[...], gate_w[...], ((1,), (0,)))
    up_pre = dot_f32(x_in[...], up_w[...], ((1,), (0,)))
    hid_grad = dot_f32(x_grad[...], down_w[...], ((1,), (1,)))
    sig = 1.0 / (1.0 + jnp.exp(-gate_pre))
    act_gate = gate_pre * sig
    hidden = (act_gate * up_pre).astype(BF16)
    tail = split_two(dot_f32(hidden, proj_ref[...], ((1,), (1,))))
    up_grad = (hid_grad * act_gate).astype(BF16)
    gate_grad = (hid_grad * up_pre * sig * (1.0 + gate_pre * (1.0 - sig))).astype(BF16)
    keep_ref[:, half:] = tail
    send_ref[:, half:] = tail
    for base, first_ref, rest_ref in ((far, send_ref, keep_ref), (near, keep_ref, send_ref)):
        for index in range(2):
            start = pl.multiple_of(base + index * quarter, 128)
            columns = slice(index * quarter, (index + 1) * quarter)
            part = dot_f32(gate_grad, gate_w[pl.ds(start, quarter), :], ((1,), (1,)))
            part += dot_f32(up_grad, up_w[pl.ds(start, quarter), :], ((1,), (1,)))
            part = part.astype(BF16)
            first_ref[:pairs, columns] = part[:pairs]
            rest_ref[pairs:, columns] = part[pairs:]


def pair_kernel(half, keep_ref, got_ref, *out_refs):
    kept, got = keep_ref[...].astype(F32), got_ref[...].astype(F32)
    main = (kept[:, :half] + got[:, :half]).astype(BF16)
    tail = split_two(join_two(kept[:, half:]) + join_two(got[:, half:]))
    rows = out_refs[0].shape[0]
    for g, out_ref in enumerate(out_refs):
        out_ref[:, :half] = main[g * rows : (g + 1) * rows]
        out_ref[:, half:] = tail[g * rows : (g + 1) * rows]


def score_kernel(half, *refs):
    *piece_refs, grad_ref, test_ref, out_ref, feature = refs
    total = piece_refs[0][...].astype(F32)
    for piece_ref in piece_refs[1:]:
        total = total + piece_ref[...].astype(F32)
    hid = join_two(total[:, half:])
    grad = grad_ref[...]
    proj = grad.shape[1]
    for p in range(proj):
        feature[:, p * proj : (p + 1) * proj] = (hid[:, p : p + 1] * grad).astype(BF16)
    out_ref[:, :half] = total[:, :half].astype(BF16)
    out_ref[:, half:] = dot_f32(feature[...], test_ref[...], ((1,), (1,))).astype(BF16)


def finish_kernel(hit_ref, home_ref, in_grad_hbm, scores_hbm, in_grad, scores, sems):
    pairs, unit = home_ref.shape[0], KINDS * CAP
    hits = jnp.concatenate(
        [hit_ref[k * unit : k * unit + CAP] for k in range(pairs // CAP)], axis=0
    )
    half = in_grad.shape[1]
    quarter = half // 2
    hits = hits.T.astype(BF16)
    copies = []
    for index in range(2):
        columns = slice(index * quarter, (index + 1) * quarter)
        in_grad[:, columns] = dot_f32(hits, home_ref[:, columns], ((1,), (0,))).astype(BF16)
        copies += start_copies(
            [(in_grad.at[:, columns], in_grad_hbm.at[:, columns])], sems.at[pl.ds(index, 1)]
        )
    scores[...] = dot_f32(hits, home_ref[:, half:], ((1,), (0,)))
    copies += start_copies([(scores, scores_hbm)], sems.at[pl.ds(2, 1)])
    for copy in copies:
        copy.wait()


def on_device(
    tokens,
    out_grad,
    route_ids,
    route_slots,
    route_weight,
    w_gate,
    w_up,
    w_down,
    proj_hidden,
    proj_grad,
    test_feats,
):
    experts = lax.axis_size("expert")
    groups = lax.axis_size("dp")
    tok_rows, half = tokens.shape
    quarter = half // 2
    width = half * lax.axis_size("test")
    proj, tests = proj_hidden.shape[1], test_feats.shape[1]
    pairs = experts * CAP
    rows = groups * pairs
    unit = KINDS * CAP
    out_width = half + 2 * proj
    ids_t, slots_t, weight_t = route_ids.T, route_slots.T, route_weight.T

    with jax.named_scope("select"):
        hits, *parts = pl.pallas_call(
            functools.partial(select_kernel, experts),
            out_shape=[jax.ShapeDtypeStruct((experts * unit, tok_rows), F32)]
            + [jax.ShapeDtypeStruct((unit, quarter), BF16)] * experts,
            in_specs=in_hbm(5),
            out_specs=whole_vmem(experts + 1),
            scratch_shapes=[
                pltpu.VMEM(x.shape, x.dtype) for x in (ids_t, slots_t, weight_t, tokens, out_grad)
            ]
            + [pltpu.SemaphoreType.DMA((5,))],
            compiler_params=limit(rows),
        )(*map(keep_in_hbm, (ids_t, slots_t, weight_t, tokens, out_grad)))
    slots = exchange(send_cross, parts, experts)
    block = jnp.stack(slots).reshape(experts, KINDS, CAP, quarter)
    block = block.transpose(1, 0, 2, 3).reshape(KINDS, pairs, quarter)
    blocks = [block] + [send_cross(block, "dp", g) for g in range(1, groups)]
    own = jnp.stack(blocks, axis=1).reshape(KINDS * rows, quarter)
    other = send_rel(own, "test", 1)
    gate_w, up_w, down_w, hid_proj = load(
        own, [w_gate[0], w_up[0], w_down[0], proj_hidden[0]], limit(rows)
    )

    with jax.named_scope("expert"):
        keep, send, mine = pl.pallas_call(
            expert_kernel,
            out_shape=[
                jax.ShapeDtypeStruct((rows, out_width), BF16),
                jax.ShapeDtypeStruct((rows, out_width), BF16),
                jax.ShapeDtypeStruct((pairs, width), BF16),
            ],
            in_specs=whole_vmem(6),
            out_specs=whole_vmem(3),
            scratch_shapes=[pltpu.VMEM((rows, width), BF16)] * 2,
            compiler_params=limit(rows),
        )(own, other, gate_w, up_w, down_w, hid_proj)
    got = send_rel(send, "test", 1)
    grad_proj, test_rows = load(send, [proj_grad[0], test_feats[0]], limit(rows))
    with jax.named_scope("pair"):
        sums = pl.pallas_call(
            functools.partial(pair_kernel, half),
            out_shape=[jax.ShapeDtypeStruct((pairs, out_width), BF16)] * groups,
            in_specs=whole_vmem(2),
            out_specs=whole_vmem(groups),
            compiler_params=limit(rows),
        )(keep, got)
    pieces = [sums[0]] + [send_cross(sums[g], "dp", g) for g in range(1, groups)]
    grad_mine = dot_f32(mine, grad_proj, ((1,), (1,)))
    with jax.named_scope("score"):
        back = pl.pallas_call(
            functools.partial(score_kernel, half),
            out_shape=jax.ShapeDtypeStruct((pairs, half + tests), BF16),
            in_specs=whole_vmem(groups + 2),
            out_specs=whole_vmem(1)[0],
            scratch_shapes=[pltpu.VMEM((pairs, proj * proj), BF16)],
            compiler_params=limit(rows),
        )(*pieces, grad_mine, test_rows)
    order = slot_order(experts)
    slots = exchange(send_rel, [back[k * CAP : (k + 1) * CAP] for k in order], experts)
    home = jnp.concatenate([slots[k] for k in order])
    with jax.named_scope("finish"):
        return pl.pallas_call(
            finish_kernel,
            out_shape=[
                jax.ShapeDtypeStruct((tok_rows, half), BF16),
                jax.ShapeDtypeStruct((tok_rows, tests), F32),
            ],
            in_specs=whole_vmem(2),
            out_specs=in_hbm(2),
            scratch_shapes=[
                pltpu.VMEM((tok_rows, half), BF16),
                pltpu.VMEM((tok_rows, tests), F32),
                pltpu.SemaphoreType.DMA((3,)),
            ],
            compiler_params=limit(rows),
        )(hits, home)


def solution(mesh):
    placed = (
        P(("expert", "dp"), "test"),
        P(("expert", "dp"), "test"),
        P(("expert", "dp"), None),
        P(("expert", "dp"), None),
        P(("expert", "dp"), None),
        P("expert", None, ("dp", "test")),
        P("expert", None, ("dp", "test")),
        P("expert", ("dp", "test"), None),
        P("expert", None, ("dp", "test")),
        P("expert", None, None),
        P("expert", "test", None),
    )
    return jax.shard_map(
        on_device,
        mesh=mesh,
        in_specs=placed,
        out_specs=(P(("expert", "dp"), "test"), P(("expert", "dp"), "test")),
        check_vma=False,
    )
```

```python
import functools

import jax
import jax.numpy as jnp
from jax import lax
from jax.experimental import pallas as pl
from jax.experimental.pallas import tpu as pltpu
from jax.sharding import PartitionSpec as P

CAP = 2
KINDS = 4
BF16 = jnp.bfloat16
F32 = jnp.float32


def send_rel(block, axis, offset):
    size = lax.axis_size(axis)
    return lax.ppermute(block, axis, [(i, i ^ offset) for i in range(size)])


def send_cross(block, axis, offset):
    return send_rel(block, (axis, "test"), offset * lax.axis_size("test") + 1)


def is_direct(count):
    return count <= 4


def slot_order(count):
    slots = list(range(count))
    return slots[::-1] if is_direct(count) else slots[::2] + slots[1::2]


def exchange(send, parts, count):
    slots = dict(zip(slot_order(count), parts))
    if is_direct(count):
        got = {k: send(slots[k], "expert", k) for k in reversed(range(1, count))}
        return [slots[0]] + [got[k] for k in range(1, count)]
    unit = parts[0].shape[0]
    bit = 1
    while bit < count:
        moving = [k for k in range(count) if k & bit]
        got = send(jnp.concatenate([slots[k] for k in moving]), "expert", bit)
        for index, k in enumerate(moving):
            slots[k] = got[index * unit : (index + 1) * unit]
        bit *= 2
    return [slots[k] for k in range(count)]


def keep_in_hbm(array):
    return pltpu.with_memory_space_constraint(array, pltpu.HBM)


def dot_f32(a, b, contract):
    return lax.dot_general(a, b, (contract, ((), ())), preferred_element_type=F32)


def whole_vmem(count):
    return [pl.BlockSpec(memory_space=pltpu.VMEM)] * count


def in_hbm(count):
    return [pl.BlockSpec(memory_space=pltpu.HBM)] * count


def start_copies(pairs, sems):
    copies = [
        pltpu.make_async_copy(source, target, sems.at[index])
        for index, (source, target) in enumerate(pairs)
    ]
    for copy in copies:
        copy.start()
    return copies


def limit(rows):
    return pltpu.CompilerParams(vmem_limit_bytes=(8 << 20) + rows * (48 << 10))


def hit_tables(ids, slots, weights, want, experts):
    live = (slots >= 0) & (ids < experts)
    code = jnp.where(live, ids * CAP + slots, -1)
    hits = jnp.zeros((want.shape[0], ids.shape[1]), F32)
    scaled = hits
    for route in range(ids.shape[0]):
        match = code[route : route + 1, :] == want
        hits = jnp.where(match, 1.0, hits)
        scaled = jnp.where(match, weights[route : route + 1, :], scaled)
    return hits, scaled


def select_kernel(experts, *refs):
    sources, (hit_ref, *out_refs) = refs[:5], refs[5:-6]
    ids, slots, weight, tok, grad, sems = refs[-6:]
    copies = start_copies(zip(sources, (ids, slots, weight, tok, grad)), sems)
    here = lax.axis_index("expert")
    unit = KINDS * CAP
    quarter = tok.shape[1] // 2
    row = lax.broadcasted_iota(jnp.int32, (experts * unit, 1), 0)
    kind = (row % unit) // CAP
    turn = row // unit
    if is_direct(experts):
        turn = experts - 1 - turn
    else:
        turn = 2 * turn % experts + 2 * turn // experts
    want = (turn ^ here) * CAP + row % CAP
    for copy in copies[:3]:
        copy.wait()
    hits, scaled = hit_tables(ids[...], slots[...], weight[...].astype(F32), want, experts)
    hit_ref[...] = hits
    total = None
    for index in range(KINDS):
        table, source = (hits, tok) if index < 2 else (scaled, grad)
        if index % 2 == 0:
            copies[3 + index // 2].wait()
        left = jnp.where(kind == index, table, 0.0).astype(BF16)
        first = (index % 2) * quarter
        part = dot_f32(left, source[:, first : first + quarter], ((1,), (0,)))
        total = part if total is None else total + part
    total = total.astype(BF16)
    for k, out_ref in enumerate(out_refs):
        out_ref[...] = total[k * unit : (k + 1) * unit]


def arrange_kernel(*refs):
    *slot_refs, out_ref = refs
    slots = [ref[...].astype(F32) for ref in slot_refs[::-1]]
    pairs = CAP * len(slots)
    for kind in range(KINDS):
        rows = [slot[kind * CAP : (kind + 1) * CAP] for slot in slots]
        out_ref[kind * pairs : (kind + 1) * pairs] = jnp.concatenate(rows).astype(BF16)


def load_kernel(shapes, *refs):
    count = sum(len(group) for group in shapes)
    sources, targets = list(refs[1 : 1 + count]), refs[1 + count : -1]
    pairs = []
    for group, target in zip(shapes, targets):
        first = 0
        for _, columns in group:
            pairs.append((sources.pop(0), target.at[:, first : first + columns]))
            first += columns
    for copy in start_copies(pairs, refs[-1]):
        copy.wait()


def split_two(value):
    high = value.astype(BF16)
    return jnp.concatenate([high, (value - high.astype(F32)).astype(BF16)], axis=1)


def join_two(value):
    value = value.astype(F32)
    middle = value.shape[1] // 2
    return value[:, :middle] + value[:, middle:]


def load(after, groups, compiler_params):
    params = [x for group in groups for x in group]
    shapes = [[x.shape for x in group] for group in groups]
    with jax.named_scope("load"):
        return pl.pallas_call(
            functools.partial(load_kernel, shapes),
            out_shape=[
                jax.ShapeDtypeStruct((group[0][0], sum(x[1] for x in group)), BF16)
                for group in shapes
            ],
            in_specs=whole_vmem(1) + in_hbm(len(params)),
            out_specs=whole_vmem(len(groups)),
            scratch_shapes=[pltpu.SemaphoreType.DMA((len(params),))],
            compiler_params=compiler_params,
            cost_estimate=pl.CostEstimate(
                flops=0, bytes_accessed=sum(2 * x.size for x in params), transcendentals=0
            ),
        )(after, *map(keep_in_hbm, params))


def expert_kernel(
    own_ref, other_ref, pair_w, down_w, proj_ref, keep_ref, send_ref, mine_ref, x_in, x_grad
):
    rows, width = x_in.shape
    half, quarter = width // 2, width // 4
    pairs = mine_ref.shape[0]
    core = lax.axis_index("test")
    near, far = pl.multiple_of(core * half, 128), pl.multiple_of((1 - core) * half, 128)
    row = lax.broadcasted_iota(jnp.int32, (rows, quarter), 0)
    odd = jnp.where(row >= pairs, 1, 0)
    slot = (row % pairs) // CAP
    if is_direct(pairs // CAP):
        odd = odd ^ jnp.where(slot > 0, 1, 0)
    else:
        for shift in range((pairs // CAP - 1).bit_length()):
            odd = odd ^ ((slot >> shift) & 1)
    odd = odd == 1
    for index in range(KINDS):
        target = x_in if index < 2 else x_grad
        own = own_ref[index * rows : (index + 1) * rows]
        other = other_ref[index * rows : (index + 1) * rows]
        first = (index % 2) * quarter
        target[:, pl.ds(pl.multiple_of(near + first, 128), quarter)] = jnp.where(odd, other, own)
        target[:, pl.ds(pl.multiple_of(far + first, 128), quarter)] = jnp.where(odd, own, other)
    mine_ref[...] = x_grad[:pairs]
    ff = down_w.shape[0]
    both_pre = dot_f32(x_in[...], pair_w[...], ((1,), (0,)))
    gate_pre, up_pre = both_pre[:, :ff], both_pre[:, ff:]
    hid_grad = dot_f32(x_grad[...], down_w[...], ((1,), (1,)))
    sig = 1.0 / (1.0 + jnp.exp(-gate_pre))
    act_gate = gate_pre * sig
    hidden = (act_gate * up_pre).astype(BF16)
    tail = split_two(dot_f32(hidden, proj_ref[...], ((1,), (1,))))
    up_grad = (hid_grad * act_gate).astype(BF16)
    gate_grad = (hid_grad * up_pre * sig * (1.0 + gate_pre * (1.0 - sig))).astype(BF16)
    both_grad = jnp.concatenate([gate_grad, up_grad], axis=1)
    keep_ref[:, half:] = tail
    send_ref[:, half:] = tail
    for base, first_ref, rest_ref in ((far, send_ref, keep_ref), (near, keep_ref, send_ref)):
        for index in range(2):
            start = pl.multiple_of(base + index * quarter, 128)
            columns = slice(index * quarter, (index + 1) * quarter)
            part = dot_f32(both_grad, pair_w[pl.ds(start, quarter), :], ((1,), (1,)))
            part = part.astype(BF16)
            first_ref[:pairs, columns] = part[:pairs]
            rest_ref[pairs:, columns] = part[pairs:]


def pair_kernel(half, keep_ref, got_ref, *out_refs):
    kept, got = keep_ref[...].astype(F32), got_ref[...].astype(F32)
    main = (kept[:, :half] + got[:, :half]).astype(BF16)
    tail = split_two(join_two(kept[:, half:]) + join_two(got[:, half:]))
    rows = out_refs[0].shape[0]
    for g, out_ref in enumerate(out_refs[::-1]):
        out_ref[:, :half] = main[g * rows : (g + 1) * rows]
        out_ref[:, half:] = tail[g * rows : (g + 1) * rows]


def score_kernel(half, order, *refs):
    pieces = len(refs) - len(order) - 3
    piece_refs, (grad_ref, test_ref) = refs[:pieces], refs[pieces : pieces + 2]
    out_refs, feature = refs[pieces + 2 : -1], refs[-1]
    total = piece_refs[0][...].astype(F32)
    for piece_ref in piece_refs[1:]:
        total = total + piece_ref[...].astype(F32)
    hid = join_two(total[:, half:])
    grad = grad_ref[...]
    proj = grad.shape[1]
    for p in range(proj):
        feature[:, p * proj : (p + 1) * proj] = (hid[:, p : p + 1] * grad).astype(BF16)
    score = dot_f32(feature[...], test_ref[...], ((1,), (1,)))
    for k, out_ref in zip(order, out_refs):
        out_ref[:, :half] = total[k * CAP : (k + 1) * CAP, :half].astype(BF16)
        out_ref[:, half:] = score[k * CAP : (k + 1) * CAP].astype(BF16)


def finish_kernel(experts, hit_ref, *refs):
    slot_refs = refs[:experts]
    in_grad_hbm, scores_hbm, in_grad, scores, home_ref, sems = refs[experts:]
    unit = KINDS * CAP
    hits = jnp.concatenate([hit_ref[k * unit : k * unit + CAP] for k in range(experts)])
    home_ref[...] = jnp.concatenate([ref[...].astype(F32) for ref in slot_refs]).astype(BF16)
    half = in_grad.shape[1]
    quarter = half // 2
    hits = hits.T.astype(BF16)
    copies = []
    for index in range(2):
        columns = slice(index * quarter, (index + 1) * quarter)
        in_grad[:, columns] = dot_f32(hits, home_ref[:, columns], ((1,), (0,))).astype(BF16)
        copies += start_copies(
            [(in_grad.at[:, columns], in_grad_hbm.at[:, columns])], sems.at[pl.ds(index, 1)]
        )
    scores[...] = dot_f32(hits, home_ref[:, half:], ((1,), (0,)))
    copies += start_copies([(scores, scores_hbm)], sems.at[pl.ds(2, 1)])
    for copy in copies:
        copy.wait()


def on_device(
    tokens,
    out_grad,
    route_ids,
    route_slots,
    route_weight,
    w_gate,
    w_up,
    w_down,
    proj_hidden,
    proj_grad,
    test_feats,
):
    experts = lax.axis_size("expert")
    groups = lax.axis_size("dp")
    tok_rows, half = tokens.shape
    quarter = half // 2
    width = half * lax.axis_size("test")
    proj, tests = proj_hidden.shape[1], test_feats.shape[1]
    pairs = experts * CAP
    rows = groups * pairs
    unit = KINDS * CAP
    out_width = half + 2 * proj
    ids_t, slots_t, weight_t = route_ids.T, route_slots.T, route_weight.T

    with jax.named_scope("select"):
        hits, *parts = pl.pallas_call(
            functools.partial(select_kernel, experts),
            out_shape=[jax.ShapeDtypeStruct((experts * unit, tok_rows), F32)]
            + [jax.ShapeDtypeStruct((unit, quarter), BF16)] * experts,
            in_specs=in_hbm(5),
            out_specs=whole_vmem(experts + 1),
            scratch_shapes=[
                pltpu.VMEM(x.shape, x.dtype) for x in (ids_t, slots_t, weight_t, tokens, out_grad)
            ]
            + [pltpu.SemaphoreType.DMA((5,))],
            compiler_params=limit(rows),
        )(*map(keep_in_hbm, (ids_t, slots_t, weight_t, tokens, out_grad)))
    slots = exchange(send_cross, parts, experts)
    with jax.named_scope("arrange"):
        block = pl.pallas_call(
            arrange_kernel,
            out_shape=jax.ShapeDtypeStruct((KINDS * pairs, quarter), BF16),
            in_specs=whole_vmem(experts),
            out_specs=whole_vmem(1)[0],
            compiler_params=limit(rows),
        )(*slots[::-1])
    block = block.reshape(KINDS, pairs, quarter)
    blocks = [block] + [send_cross(block, "dp", g) for g in range(1, groups)]
    own = jnp.stack(blocks, axis=1).reshape(KINDS * rows, quarter)
    other = send_rel(own, "test", 1)
    pair_w, down_w, hid_proj = load(
        own, [[w_gate[0], w_up[0]], [w_down[0]], [proj_hidden[0]]], limit(rows)
    )

    with jax.named_scope("expert"):
        keep, send, mine = pl.pallas_call(
            expert_kernel,
            out_shape=[
                jax.ShapeDtypeStruct((rows, out_width), BF16),
                jax.ShapeDtypeStruct((rows, out_width), BF16),
                jax.ShapeDtypeStruct((pairs, width), BF16),
            ],
            in_specs=whole_vmem(5),
            out_specs=whole_vmem(3),
            scratch_shapes=[pltpu.VMEM((rows, width), BF16)] * 2,
            compiler_params=limit(rows),
        )(own, other, pair_w, down_w, hid_proj)
    got = send_rel(send, "test", 1)
    grad_proj, test_rows = load(send, [[proj_grad[0]], [test_feats[0]]], limit(rows))
    with jax.named_scope("pair"):
        sums = pl.pallas_call(
            functools.partial(pair_kernel, half),
            out_shape=[jax.ShapeDtypeStruct((pairs, out_width), BF16)] * groups,
            in_specs=whole_vmem(2),
            out_specs=whole_vmem(groups),
            compiler_params=limit(rows),
        )(keep, got)
    pieces = [send_cross(sums[-1 - g], "dp", g) for g in reversed(range(1, groups))] + [sums[-1]]
    grad_mine = dot_f32(mine, grad_proj, ((1,), (1,)))
    order = slot_order(experts)
    with jax.named_scope("score"):
        back = pl.pallas_call(
            functools.partial(score_kernel, half, order),
            out_shape=[jax.ShapeDtypeStruct((CAP, half + tests), BF16)] * experts,
            in_specs=whole_vmem(groups + 2),
            out_specs=whole_vmem(experts),
            scratch_shapes=[pltpu.VMEM((pairs, proj * proj), BF16)],
            compiler_params=limit(rows),
        )(*pieces, grad_mine, test_rows)
    slots = exchange(send_rel, back, experts)
    home = [slots[k] for k in order]
    with jax.named_scope("finish"):
        return pl.pallas_call(
            functools.partial(finish_kernel, experts),
            out_shape=[
                jax.ShapeDtypeStruct((tok_rows, half), BF16),
                jax.ShapeDtypeStruct((tok_rows, tests), F32),
            ],
            in_specs=whole_vmem(experts + 1),
            out_specs=in_hbm(2),
            scratch_shapes=[
                pltpu.VMEM((tok_rows, half), BF16),
                pltpu.VMEM((tok_rows, tests), F32),
                pltpu.VMEM((pairs, half + tests), BF16),
                pltpu.SemaphoreType.DMA((3,)),
            ],
            compiler_params=limit(rows),
        )(hits, *home)


def solution(mesh):
    placed = (
        P(("expert", "dp"), "test"),
        P(("expert", "dp"), "test"),
        P(("expert", "dp"), None),
        P(("expert", "dp"), None),
        P(("expert", "dp"), None),
        P("expert", None, ("dp", "test")),
        P("expert", None, ("dp", "test")),
        P("expert", ("dp", "test"), None),
        P("expert", None, ("dp", "test")),
        P("expert", None, None),
        P("expert", "test", None),
    )
    return jax.shard_map(
        on_device,
        mesh=mesh,
        in_specs=placed,
        out_specs=(P(("expert", "dp"), "test"), P(("expert", "dp"), "test")),
        check_vma=False,
    )
```

```python
import functools

import jax
import jax.numpy as jnp
from jax import lax
from jax.experimental import pallas as pl
from jax.experimental.pallas import tpu as pltpu
from jax.sharding import PartitionSpec as P

CAP = 2
KINDS = 4
BF16 = jnp.bfloat16
F32 = jnp.float32


def send_rel(block, axis, offset):
    size = lax.axis_size(axis)
    return lax.ppermute(block, axis, [(i, i ^ offset) for i in range(size)])


def send_cross(block, axis, offset):
    return send_rel(block, (axis, "test"), offset * lax.axis_size("test") + 1)


def is_direct(count):
    return count <= 4


def slot_order(count):
    slots = list(range(count))
    return slots[::-1] if is_direct(count) else slots[::2] + slots[1::2]


def exchange(send, parts, count):
    slots = dict(zip(slot_order(count), parts))
    if is_direct(count):
        got = {k: send(slots[k], "expert", k) for k in reversed(range(1, count))}
        return [slots[0]] + [got[k] for k in range(1, count)]
    unit = parts[0].shape[0]
    bit = 1
    while bit < count:
        moving = [k for k in range(count) if k & bit]
        got = send(jnp.concatenate([slots[k] for k in moving]), "expert", bit)
        for index, k in enumerate(moving):
            slots[k] = got[index * unit : (index + 1) * unit]
        bit *= 2
    return [slots[k] for k in range(count)]


def keep_in_hbm(array):
    return pltpu.with_memory_space_constraint(array, pltpu.HBM)


def dot_f32(a, b, contract):
    return lax.dot_general(a, b, (contract, ((), ())), preferred_element_type=F32)


def whole_vmem(count):
    return [pl.BlockSpec(memory_space=pltpu.VMEM)] * count


def in_hbm(count):
    return [pl.BlockSpec(memory_space=pltpu.HBM)] * count


def start_copies(pairs, sems):
    copies = [
        pltpu.make_async_copy(source, target, sems.at[index])
        for index, (source, target) in enumerate(pairs)
    ]
    for copy in copies:
        copy.start()
    return copies


def limit(rows):
    return pltpu.CompilerParams(vmem_limit_bytes=(8 << 20) + rows * (48 << 10))


def hit_tables(ids, slots, weights, want, experts):
    live = (slots >= 0) & (ids < experts)
    code = jnp.where(live, ids * CAP + slots, -1)
    hits = jnp.zeros((want.shape[0], ids.shape[1]), F32)
    scaled = hits
    for route in range(ids.shape[0]):
        match = code[route : route + 1, :] == want
        hits = jnp.where(match, 1.0, hits)
        scaled = jnp.where(match, weights[route : route + 1, :], scaled)
    return hits, scaled


def select_kernel(experts, *refs):
    sources, (hit_ref, *out_refs) = refs[:5], refs[5:-6]
    ids, slots, weight, tok, grad, sems = refs[-6:]
    copies = start_copies(zip(sources, (ids, slots, weight, tok, grad)), sems)
    here = lax.axis_index("expert")
    unit = KINDS * CAP
    quarter = tok.shape[1] // 2
    row = lax.broadcasted_iota(jnp.int32, (experts * unit, 1), 0)
    kind = (row % unit) // CAP
    turn = row // unit
    if is_direct(experts):
        turn = experts - 1 - turn
    else:
        turn = 2 * turn % experts + 2 * turn // experts
    want = (turn ^ here) * CAP + row % CAP
    for copy in copies[:3]:
        copy.wait()
    hits, scaled = hit_tables(ids[...], slots[...], weight[...].astype(F32), want, experts)
    hit_ref[...] = hits
    total = None
    for index in range(KINDS):
        table, source = (hits, tok) if index < 2 else (scaled, grad)
        if index % 2 == 0:
            copies[3 + index // 2].wait()
        left = jnp.where(kind == index, table, 0.0).astype(BF16)
        first = (index % 2) * quarter
        part = dot_f32(left, source[:, first : first + quarter], ((1,), (0,)))
        total = part if total is None else total + part
    total = total.astype(BF16)
    for k, out_ref in enumerate(out_refs):
        out_ref[...] = total[k * unit : (k + 1) * unit]


def arrange_kernel(*refs):
    *slot_refs, out_ref = refs
    slots = [ref[...].astype(F32) for ref in slot_refs[::-1]]
    pairs = CAP * len(slots)
    for kind in range(KINDS):
        rows = [slot[kind * CAP : (kind + 1) * CAP] for slot in slots]
        out_ref[kind * pairs : (kind + 1) * pairs] = jnp.concatenate(rows).astype(BF16)


def join_kernel(*refs):
    *block_refs, out_ref = refs
    pairs = block_refs[0].shape[0] // KINDS
    for kind in range(KINDS):
        for g, block_ref in enumerate(block_refs[::-1]):
            first = (kind * len(block_refs) + g) * pairs
            out_ref[first : first + pairs] = block_ref[kind * pairs : (kind + 1) * pairs]


def load_kernel(shapes, *refs):
    count = sum(len(group) for group in shapes)
    sources, targets = list(refs[1 : 1 + count]), refs[1 + count : -1]
    pairs = []
    for group, target in zip(shapes, targets):
        first = 0
        for _, columns in group:
            pairs.append((sources.pop(0), target.at[:, first : first + columns]))
            first += columns
    for copy in start_copies(pairs, refs[-1]):
        copy.wait()


def split_two(value):
    high = value.astype(BF16)
    return jnp.concatenate([high, (value - high.astype(F32)).astype(BF16)], axis=1)


def join_two(value):
    value = value.astype(F32)
    middle = value.shape[1] // 2
    return value[:, :middle] + value[:, middle:]


def load(after, groups, compiler_params):
    params = [x for group in groups for x in group]
    shapes = [[x.shape for x in group] for group in groups]
    with jax.named_scope("load"):
        return pl.pallas_call(
            functools.partial(load_kernel, shapes),
            out_shape=[
                jax.ShapeDtypeStruct((group[0][0], sum(x[1] for x in group)), BF16)
                for group in shapes
            ],
            in_specs=whole_vmem(1) + in_hbm(len(params)),
            out_specs=whole_vmem(len(groups)),
            scratch_shapes=[pltpu.SemaphoreType.DMA((len(params),))],
            compiler_params=compiler_params,
            cost_estimate=pl.CostEstimate(
                flops=0, bytes_accessed=sum(2 * x.size for x in params), transcendentals=0
            ),
        )(after, *map(keep_in_hbm, params))


def expert_kernel(
    own_ref, other_ref, pair_w, down_w, proj_ref, keep_ref, send_ref, mine_ref, x_in, x_grad
):
    rows, width = x_in.shape
    half, quarter = width // 2, width // 4
    pairs = mine_ref.shape[0]
    core = lax.axis_index("test")
    near, far = pl.multiple_of(core * half, 128), pl.multiple_of((1 - core) * half, 128)
    row = lax.broadcasted_iota(jnp.int32, (rows, quarter), 0)
    odd = jnp.where(row >= pairs, 1, 0)
    slot = (row % pairs) // CAP
    if is_direct(pairs // CAP):
        odd = odd ^ jnp.where(slot > 0, 1, 0)
    else:
        for shift in range((pairs // CAP - 1).bit_length()):
            odd = odd ^ ((slot >> shift) & 1)
    odd = odd == 1
    for index in range(KINDS):
        target = x_in if index < 2 else x_grad
        own = own_ref[index * rows : (index + 1) * rows]
        other = other_ref[index * rows : (index + 1) * rows]
        first = (index % 2) * quarter
        target[:, pl.ds(pl.multiple_of(near + first, 128), quarter)] = jnp.where(odd, other, own)
        target[:, pl.ds(pl.multiple_of(far + first, 128), quarter)] = jnp.where(odd, own, other)
    mine_ref[...] = x_grad[:pairs]
    ff = down_w.shape[0]
    both_pre = dot_f32(x_in[...], pair_w[...], ((1,), (0,)))
    gate_pre, up_pre = both_pre[:, :ff], both_pre[:, ff:]
    hid_grad = dot_f32(x_grad[...], down_w[...], ((1,), (1,)))
    sig = 1.0 / (1.0 + jnp.exp(-gate_pre))
    act_gate = gate_pre * sig
    hidden = (act_gate * up_pre).astype(BF16)
    tail = split_two(dot_f32(hidden, proj_ref[...], ((1,), (1,))))
    up_grad = (hid_grad * act_gate).astype(BF16)
    gate_grad = (hid_grad * up_pre * sig * (1.0 + gate_pre * (1.0 - sig))).astype(BF16)
    both_grad = jnp.concatenate([gate_grad, up_grad], axis=1)
    keep_ref[:, half:] = tail
    send_ref[:, half:] = tail
    for base, first_ref, rest_ref in ((far, send_ref, keep_ref), (near, keep_ref, send_ref)):
        for index in range(2):
            start = pl.multiple_of(base + index * quarter, 128)
            columns = slice(index * quarter, (index + 1) * quarter)
            part = dot_f32(both_grad, pair_w[pl.ds(start, quarter), :], ((1,), (1,)))
            part = part.astype(BF16)
            first_ref[:pairs, columns] = part[:pairs]
            rest_ref[pairs:, columns] = part[pairs:]


def pair_kernel(half, keep_ref, got_ref, *out_refs):
    kept, got = keep_ref[...].astype(F32), got_ref[...].astype(F32)
    main = (kept[:, :half] + got[:, :half]).astype(BF16)
    tail = split_two(join_two(kept[:, half:]) + join_two(got[:, half:]))
    rows = out_refs[0].shape[0]
    for g, out_ref in enumerate(out_refs[::-1]):
        out_ref[:, :half] = main[g * rows : (g + 1) * rows]
        out_ref[:, half:] = tail[g * rows : (g + 1) * rows]


def score_kernel(half, order, *refs):
    pieces = len(refs) - len(order) - 3
    piece_refs, (grad_ref, test_ref) = refs[:pieces], refs[pieces : pieces + 2]
    out_refs, feature = refs[pieces + 2 : -1], refs[-1]
    total = piece_refs[0][...].astype(F32)
    for piece_ref in piece_refs[1:]:
        total = total + piece_ref[...].astype(F32)
    hid = join_two(total[:, half:])
    grad = grad_ref[...]
    proj = grad.shape[1]
    for p in range(proj):
        feature[:, p * proj : (p + 1) * proj] = (hid[:, p : p + 1] * grad).astype(BF16)
    score = dot_f32(feature[...], test_ref[...], ((1,), (1,)))
    for k, out_ref in zip(order, out_refs):
        out_ref[:, :half] = total[k * CAP : (k + 1) * CAP, :half].astype(BF16)
        out_ref[:, half:] = score[k * CAP : (k + 1) * CAP].astype(BF16)


def finish_kernel(experts, hit_ref, *refs):
    slot_refs = refs[:experts]
    in_grad_hbm, scores_hbm, in_grad, scores, home_ref, sems = refs[experts:]
    unit = KINDS * CAP
    hits = jnp.concatenate([hit_ref[k * unit : k * unit + CAP] for k in range(experts)])
    home_ref[...] = jnp.concatenate([ref[...].astype(F32) for ref in slot_refs]).astype(BF16)
    half = in_grad.shape[1]
    quarter = half // 2
    hits = hits.T.astype(BF16)
    copies = []
    for index in range(2):
        columns = slice(index * quarter, (index + 1) * quarter)
        in_grad[:, columns] = dot_f32(hits, home_ref[:, columns], ((1,), (0,))).astype(BF16)
        copies += start_copies(
            [(in_grad.at[:, columns], in_grad_hbm.at[:, columns])], sems.at[pl.ds(index, 1)]
        )
    scores[...] = dot_f32(hits, home_ref[:, half:], ((1,), (0,)))
    copies += start_copies([(scores, scores_hbm)], sems.at[pl.ds(2, 1)])
    for copy in copies:
        copy.wait()


def on_device(
    tokens,
    out_grad,
    route_ids,
    route_slots,
    route_weight,
    w_gate,
    w_up,
    w_down,
    proj_hidden,
    proj_grad,
    test_feats,
):
    experts = lax.axis_size("expert")
    groups = lax.axis_size("dp")
    tok_rows, half = tokens.shape
    quarter = half // 2
    width = half * lax.axis_size("test")
    proj, tests = proj_hidden.shape[1], test_feats.shape[1]
    pairs = experts * CAP
    rows = groups * pairs
    unit = KINDS * CAP
    out_width = half + 2 * proj
    ids_t, slots_t, weight_t = route_ids.T, route_slots.T, route_weight.T

    with jax.named_scope("select"):
        hits, *parts = pl.pallas_call(
            functools.partial(select_kernel, experts),
            out_shape=[jax.ShapeDtypeStruct((experts * unit, tok_rows), F32)]
            + [jax.ShapeDtypeStruct((unit, quarter), BF16)] * experts,
            in_specs=in_hbm(5),
            out_specs=whole_vmem(experts + 1),
            scratch_shapes=[
                pltpu.VMEM(x.shape, x.dtype) for x in (ids_t, slots_t, weight_t, tokens, out_grad)
            ]
            + [pltpu.SemaphoreType.DMA((5,))],
            compiler_params=limit(rows),
        )(*map(keep_in_hbm, (ids_t, slots_t, weight_t, tokens, out_grad)))
    slots = exchange(send_cross, parts, experts)
    with jax.named_scope("arrange"):
        block = pl.pallas_call(
            arrange_kernel,
            out_shape=jax.ShapeDtypeStruct((KINDS * pairs, quarter), BF16),
            in_specs=whole_vmem(experts),
            out_specs=whole_vmem(1)[0],
            compiler_params=limit(rows),
        )(*slots[::-1])
    blocks = [send_cross(block, "dp", g) for g in reversed(range(1, groups))] + [block]
    loaded = load(block, [[w_gate[0], w_up[0]], [w_down[0]], [proj_hidden[0]]], limit(rows))
    blocks, (pair_w, down_w, hid_proj) = lax.optimization_barrier((blocks, loaded))
    with jax.named_scope("join"):
        own = pl.pallas_call(
            join_kernel,
            out_shape=jax.ShapeDtypeStruct((KINDS * rows, quarter), BF16),
            in_specs=whole_vmem(groups),
            out_specs=whole_vmem(1)[0],
            compiler_params=limit(rows),
        )(*blocks)
    other = send_rel(own, "test", 1)
    with jax.named_scope("expert"):
        keep, send, mine = pl.pallas_call(
            expert_kernel,
            out_shape=[
                jax.ShapeDtypeStruct((rows, out_width), BF16),
                jax.ShapeDtypeStruct((rows, out_width), BF16),
                jax.ShapeDtypeStruct((pairs, width), BF16),
            ],
            in_specs=whole_vmem(5),
            out_specs=whole_vmem(3),
            scratch_shapes=[pltpu.VMEM((rows, width), BF16)] * 2,
            compiler_params=limit(rows),
        )(own, other, pair_w, down_w, hid_proj)
    got = send_rel(send, "test", 1)
    with jax.named_scope("pair"):
        sums = pl.pallas_call(
            functools.partial(pair_kernel, half),
            out_shape=[jax.ShapeDtypeStruct((pairs, out_width), BF16)] * groups,
            in_specs=whole_vmem(2),
            out_specs=whole_vmem(groups),
            compiler_params=limit(rows),
        )(keep, got)
    pieces = [send_cross(sums[-1 - g], "dp", g) for g in reversed(range(1, groups))] + [sums[-1]]
    grad_proj, test_rows = load(sums[-1], [[proj_grad[0]], [test_feats[0]]], limit(rows))
    grad_mine = dot_f32(mine, grad_proj, ((1,), (1,)))
    order = slot_order(experts)
    with jax.named_scope("score"):
        back = pl.pallas_call(
            functools.partial(score_kernel, half, order),
            out_shape=[jax.ShapeDtypeStruct((CAP, half + tests), BF16)] * experts,
            in_specs=whole_vmem(groups + 2),
            out_specs=whole_vmem(experts),
            scratch_shapes=[pltpu.VMEM((pairs, proj * proj), BF16)],
            compiler_params=limit(rows),
        )(*pieces, grad_mine, test_rows)
    slots = exchange(send_rel, back, experts)
    home = [slots[k] for k in order]
    with jax.named_scope("finish"):
        return pl.pallas_call(
            functools.partial(finish_kernel, experts),
            out_shape=[
                jax.ShapeDtypeStruct((tok_rows, half), BF16),
                jax.ShapeDtypeStruct((tok_rows, tests), F32),
            ],
            in_specs=whole_vmem(experts + 1),
            out_specs=in_hbm(2),
            scratch_shapes=[
                pltpu.VMEM((tok_rows, half), BF16),
                pltpu.VMEM((tok_rows, tests), F32),
                pltpu.VMEM((pairs, half + tests), BF16),
                pltpu.SemaphoreType.DMA((3,)),
            ],
            compiler_params=limit(rows),
        )(hits, *home)


def solution(mesh):
    placed = (
        P(("expert", "dp"), "test"),
        P(("expert", "dp"), "test"),
        P(("expert", "dp"), None),
        P(("expert", "dp"), None),
        P(("expert", "dp"), None),
        P("expert", None, ("dp", "test")),
        P("expert", None, ("dp", "test")),
        P("expert", ("dp", "test"), None),
        P("expert", None, ("dp", "test")),
        P("expert", None, None),
        P("expert", "test", None),
    )
    return jax.shard_map(
        on_device,
        mesh=mesh,
        in_specs=placed,
        out_specs=(P(("expert", "dp"), "test"), P(("expert", "dp"), "test")),
        check_vma=False,
    )
```

```python
import functools

import jax
import jax.numpy as jnp
from jax import lax
from jax.experimental import pallas as pl
from jax.experimental.pallas import tpu as pltpu
from jax.sharding import PartitionSpec as P

CAP = 2
KINDS = 4
BF16 = jnp.bfloat16
F32 = jnp.float32


def send_rel(block, axis, offset):
    size = lax.axis_size(axis)
    return lax.ppermute(block, axis, [(i, i ^ offset) for i in range(size)])


def send_cross(block, axis, offset):
    return send_rel(block, (axis, "test"), offset * lax.axis_size("test") + 1)


def plane_offsets(groups):
    offsets = [(g, g) for g in reversed(range(1, groups))]
    if groups > 2:
        offsets[-2:] = [(1, 2), (2, 1)]
    return offsets


def send_plane(block, offsets):
    pairs = []
    for g in range(lax.axis_size("dp")):
        pairs += [(2 * g + t, 2 * (g ^ offsets[t]) + 1 - t) for t in range(2)]
    return lax.ppermute(block, ("dp", "test"), pairs)


def is_direct(count):
    return count <= 4


def slot_order(count):
    slots = list(range(count))
    return slots[::-1] if is_direct(count) else slots[::2] + slots[1::2]


def exchange(send, parts, count):
    slots = dict(zip(slot_order(count), parts))
    if is_direct(count):
        got = {k: send(slots[k], "expert", k) for k in reversed(range(1, count))}
        return [slots[0]] + [got[k] for k in range(1, count)]
    unit = parts[0].shape[0]
    bit = 1
    while bit < count:
        moving = [k for k in range(count) if k & bit]
        got = send(jnp.concatenate([slots[k] for k in moving]), "expert", bit)
        for index, k in enumerate(moving):
            slots[k] = got[index * unit : (index + 1) * unit]
        bit *= 2
    return [slots[k] for k in range(count)]


def keep_in_hbm(array):
    return pltpu.with_memory_space_constraint(array, pltpu.HBM)


def dot_f32(a, b, contract):
    return lax.dot_general(a, b, (contract, ((), ())), preferred_element_type=F32)


def whole_vmem(count):
    return [pl.BlockSpec(memory_space=pltpu.VMEM)] * count


def in_hbm(count):
    return [pl.BlockSpec(memory_space=pltpu.HBM)] * count


def start_copies(pairs, sems):
    copies = [
        pltpu.make_async_copy(source, target, sems.at[index])
        for index, (source, target) in enumerate(pairs)
    ]
    for copy in copies:
        copy.start()
    return copies


def limit(rows):
    return pltpu.CompilerParams(vmem_limit_bytes=(8 << 20) + rows * (48 << 10))


def hit_tables(ids, slots, weights, want, experts):
    live = (slots >= 0) & (ids < experts)
    code = jnp.where(live, ids * CAP + slots, -1)
    hits = jnp.zeros((want.shape[0], ids.shape[1]), F32)
    scaled = hits
    for route in range(ids.shape[0]):
        match = code[route : route + 1, :] == want
        hits = jnp.where(match, 1.0, hits)
        scaled = jnp.where(match, weights[route : route + 1, :], scaled)
    return hits, scaled


def select_kernel(experts, *refs):
    (ids_hbm, slots_hbm, weight_hbm, tok_hbm, grad_hbm), (hit_ref, *out_refs) = refs[:5], refs[5:-5]
    ids, slots, weight, quarters, sems = refs[-5:]
    tokens, quarter = quarters.shape[0] // KINDS, quarters.shape[1]
    pairs = [(ids_hbm, ids), (slots_hbm, slots), (weight_hbm, weight)]
    for kind in range(KINDS):
        source, first = (tok_hbm, grad_hbm)[kind // 2], kind % 2 * quarter
        target = quarters.at[kind * tokens : (kind + 1) * tokens]
        pairs.append((source.at[:, first : first + quarter], target))
    copies = start_copies(pairs, sems)
    here = lax.axis_index("expert")
    unit = KINDS * CAP
    row = lax.broadcasted_iota(jnp.int32, (experts * unit, 1), 0)
    turn = row // unit
    if is_direct(experts):
        turn = experts - 1 - turn
    else:
        turn = 2 * turn % experts + 2 * turn // experts
    want = (turn ^ here) * CAP + row % CAP
    for copy in copies[:3]:
        copy.wait()
    hits, scaled = hit_tables(ids[...], slots[...], weight[...].astype(F32), want, experts)
    hit_ref[...] = hits
    left = jnp.concatenate([hits, hits, scaled, scaled], axis=1)
    column = lax.broadcasted_iota(jnp.int32, left.shape, 1)
    left = jnp.where(column // tokens == (row % unit) // CAP, left, 0.0).astype(BF16)
    for copy in copies[3:]:
        copy.wait()
    total = dot_f32(left, quarters[...], ((1,), (0,))).astype(BF16)
    for k, out_ref in enumerate(out_refs):
        out_ref[...] = total[k * unit : (k + 1) * unit]


def arrange_kernel(*refs):
    *slot_refs, out_ref = refs
    slots = [ref[...].astype(F32) for ref in slot_refs[::-1]]
    pairs = CAP * len(slots)
    for kind in range(KINDS):
        rows = [slot[kind * CAP : (kind + 1) * CAP] for slot in slots]
        out_ref[kind * pairs : (kind + 1) * pairs] = jnp.concatenate(rows).astype(BF16)


def join_kernel(offsets, *refs):
    *block_refs, own_ref, out_ref = refs
    count = len(offsets) + 1
    pairs = own_ref.shape[0] // KINDS

    def place(ref, g):
        for kind in range(KINDS):
            first = (kind * count + g) * pairs
            out_ref[first : first + pairs] = ref[kind * pairs : (kind + 1) * pairs]

    place(own_ref, 0)
    for core in range(2):

        @pl.when(lax.axis_index("test") == core)
        def _():
            for ref, offset in zip(block_refs, offsets):
                place(ref, offset[1 - core])


def load_kernel(shapes, *refs):
    count = sum(len(group) for group in shapes)
    sources, targets = list(refs[1 : 1 + count]), refs[1 + count : -1]
    pairs = []
    for group, target in zip(shapes, targets):
        first = 0
        for _, columns in group:
            pairs.append((sources.pop(0), target.at[:, first : first + columns]))
            first += columns
    for copy in start_copies(pairs, refs[-1]):
        copy.wait()


def split_two(value):
    high = value.astype(BF16)
    return jnp.concatenate([high, (value - high.astype(F32)).astype(BF16)], axis=1)


def join_two(value):
    value = value.astype(F32)
    middle = value.shape[1] // 2
    return value[:, :middle] + value[:, middle:]


def load(after, groups, compiler_params):
    params = [x for group in groups for x in group]
    shapes = [[x.shape for x in group] for group in groups]
    with jax.named_scope("load"):
        return pl.pallas_call(
            functools.partial(load_kernel, shapes),
            out_shape=[
                jax.ShapeDtypeStruct((group[0][0], sum(x[1] for x in group)), BF16)
                for group in shapes
            ],
            in_specs=whole_vmem(1) + in_hbm(len(params)),
            out_specs=whole_vmem(len(groups)),
            scratch_shapes=[pltpu.SemaphoreType.DMA((len(params),))],
            compiler_params=compiler_params,
            cost_estimate=pl.CostEstimate(
                flops=0, bytes_accessed=sum(2 * x.size for x in params), transcendentals=0
            ),
        )(after, *map(keep_in_hbm, params))


def expert_kernel(
    own_ref, other_ref, pair_w, down_w, proj_ref, keep_ref, send_ref, mine_ref, x_in, x_grad
):
    rows, width = x_in.shape
    half, quarter = width // 2, width // 4
    pairs = mine_ref.shape[0]
    core = lax.axis_index("test")
    near, far = pl.multiple_of(core * half, 128), pl.multiple_of((1 - core) * half, 128)
    row = lax.broadcasted_iota(jnp.int32, (rows, quarter), 0)
    odd = jnp.where(row >= pairs, 1, 0)
    slot = (row % pairs) // CAP
    if is_direct(pairs // CAP):
        odd = odd ^ jnp.where(slot > 0, 1, 0)
    else:
        for shift in range((pairs // CAP - 1).bit_length()):
            odd = odd ^ ((slot >> shift) & 1)
    odd = odd == 1
    for index in range(KINDS):
        target = x_in if index < 2 else x_grad
        own = own_ref[index * rows : (index + 1) * rows]
        other = other_ref[index * rows : (index + 1) * rows]
        first = (index % 2) * quarter
        target[:, pl.ds(pl.multiple_of(near + first, 128), quarter)] = jnp.where(odd, other, own)
        target[:, pl.ds(pl.multiple_of(far + first, 128), quarter)] = jnp.where(odd, own, other)
    mine_ref[...] = x_grad[:pairs]
    ff = down_w.shape[0]
    both_pre = dot_f32(x_in[...], pair_w[...], ((1,), (0,)))
    gate_pre, up_pre = both_pre[:, :ff], both_pre[:, ff:]
    hid_grad = dot_f32(x_grad[...], down_w[...], ((1,), (1,)))
    sig = 1.0 / (1.0 + jnp.exp(-gate_pre))
    act_gate = gate_pre * sig
    hidden = (act_gate * up_pre).astype(BF16)
    tail = split_two(dot_f32(hidden, proj_ref[...], ((1,), (1,))))
    up_grad = (hid_grad * act_gate).astype(BF16)
    gate_grad = (hid_grad * up_pre * sig * (1.0 + gate_pre * (1.0 - sig))).astype(BF16)
    both_grad = jnp.concatenate([gate_grad, up_grad], axis=1)
    keep_ref[:, half:] = tail
    send_ref[:, half:] = tail
    for base, first_ref, rest_ref in ((far, send_ref, keep_ref), (near, keep_ref, send_ref)):
        for index in range(2):
            start = pl.multiple_of(base + index * quarter, 128)
            columns = slice(index * quarter, (index + 1) * quarter)
            part = dot_f32(both_grad, pair_w[pl.ds(start, quarter), :], ((1,), (1,)))
            part = part.astype(BF16)
            first_ref[:pairs, columns] = part[:pairs]
            rest_ref[pairs:, columns] = part[pairs:]


def pair_kernel(half, offsets, keep_ref, got_ref, *refs):
    *out_refs, own_ref = refs
    kept, got = keep_ref[...].astype(F32), got_ref[...].astype(F32)
    main = (kept[:, :half] + got[:, :half]).astype(BF16)
    tail = split_two(join_two(kept[:, half:]) + join_two(got[:, half:]))
    rows = own_ref.shape[0]

    def place(ref, g):
        ref[:, :half] = main[g * rows : (g + 1) * rows]
        ref[:, half:] = tail[g * rows : (g + 1) * rows]

    place(own_ref, 0)
    for core in range(2):

        @pl.when(lax.axis_index("test") == core)
        def _():
            for ref, offset in zip(out_refs, offsets):
                place(ref, offset[core])


def score_kernel(half, order, *refs):
    pieces = len(refs) - len(order) - 3
    piece_refs, (grad_ref, test_ref) = refs[:pieces], refs[pieces : pieces + 2]
    out_refs, feature = refs[pieces + 2 : -1], refs[-1]
    total = piece_refs[0][...].astype(F32)
    for piece_ref in piece_refs[1:]:
        total = total + piece_ref[...].astype(F32)
    hid = join_two(total[:, half:])
    grad = grad_ref[...]
    proj = grad.shape[1]
    grad = jnp.concatenate([grad, grad], axis=1)
    left = lax.broadcasted_iota(jnp.int32, grad.shape, 1) < proj
    for p in range(0, proj, 2):
        pair = jnp.where(left, hid[:, p : p + 1], hid[:, p + 1 : p + 2])
        feature[:, p * proj : (p + 2) * proj] = (pair * grad).astype(BF16)
    score = dot_f32(feature[...], test_ref[...], ((1,), (1,)))
    for k, out_ref in zip(order, out_refs):
        out_ref[:, :half] = total[k * CAP : (k + 1) * CAP, :half].astype(BF16)
        out_ref[:, half:] = score[k * CAP : (k + 1) * CAP].astype(BF16)


def finish_kernel(experts, hit_ref, *refs):
    slot_refs = refs[:experts]
    in_grad_hbm, scores_hbm, in_grad, scores, home_ref, sems = refs[experts:]
    unit = KINDS * CAP
    hits = jnp.concatenate([hit_ref[k * unit : k * unit + CAP] for k in range(experts)])
    home_ref[...] = jnp.concatenate([ref[...].astype(F32) for ref in slot_refs]).astype(BF16)
    half = in_grad.shape[1]
    quarter = half // 2
    hits = hits.T.astype(BF16)
    copies = []
    for index in range(2):
        columns = slice(index * quarter, (index + 1) * quarter)
        in_grad[:, columns] = dot_f32(hits, home_ref[:, columns], ((1,), (0,))).astype(BF16)
        copies += start_copies(
            [(in_grad.at[:, columns], in_grad_hbm.at[:, columns])], sems.at[pl.ds(index, 1)]
        )
    scores[...] = dot_f32(hits, home_ref[:, half:], ((1,), (0,)))
    copies += start_copies([(scores, scores_hbm)], sems.at[pl.ds(2, 1)])
    for copy in copies:
        copy.wait()


def on_device(
    tokens,
    out_grad,
    route_ids,
    route_slots,
    route_weight,
    w_gate,
    w_up,
    w_down,
    proj_hidden,
    proj_grad,
    test_feats,
):
    experts = lax.axis_size("expert")
    groups = lax.axis_size("dp")
    tok_rows, half = tokens.shape
    quarter = half // 2
    width = half * lax.axis_size("test")
    proj, tests = proj_hidden.shape[1], test_feats.shape[1]
    pairs = experts * CAP
    rows = groups * pairs
    unit = KINDS * CAP
    out_width = half + 2 * proj
    ids_t, slots_t, weight_t = route_ids.T, route_slots.T, route_weight.T

    with jax.named_scope("select"):
        hits, *parts = pl.pallas_call(
            functools.partial(select_kernel, experts),
            out_shape=[jax.ShapeDtypeStruct((experts * unit, tok_rows), F32)]
            + [jax.ShapeDtypeStruct((unit, quarter), BF16)] * experts,
            in_specs=in_hbm(5),
            out_specs=whole_vmem(experts + 1),
            scratch_shapes=[pltpu.VMEM(x.shape, x.dtype) for x in (ids_t, slots_t, weight_t)]
            + [
                pltpu.VMEM((KINDS * tok_rows, quarter), BF16),
                pltpu.SemaphoreType.DMA((3 + KINDS,)),
            ],
            compiler_params=limit(rows),
        )(*map(keep_in_hbm, (ids_t, slots_t, weight_t, tokens, out_grad)))
    slots = exchange(send_cross, parts, experts)
    with jax.named_scope("arrange"):
        block = pl.pallas_call(
            arrange_kernel,
            out_shape=jax.ShapeDtypeStruct((KINDS * pairs, quarter), BF16),
            in_specs=whole_vmem(experts),
            out_specs=whole_vmem(1)[0],
            compiler_params=limit(rows),
        )(*slots[::-1])
    offsets = plane_offsets(groups)
    blocks = [block] + [send_plane(block, offset) for offset in offsets[::-1]]
    loaded = load(block, [[w_gate[0], w_up[0]], [w_down[0]], [proj_hidden[0]]], limit(rows))
    blocks, (pair_w, down_w, hid_proj) = lax.optimization_barrier((blocks, loaded))
    with jax.named_scope("join"):
        own = pl.pallas_call(
            functools.partial(join_kernel, offsets),
            out_shape=jax.ShapeDtypeStruct((KINDS * rows, quarter), BF16),
            in_specs=whole_vmem(groups),
            out_specs=whole_vmem(1)[0],
            compiler_params=limit(rows),
        )(*blocks[::-1])
    other = send_rel(own, "test", 1)
    with jax.named_scope("expert"):
        keep, send, mine = pl.pallas_call(
            expert_kernel,
            out_shape=[
                jax.ShapeDtypeStruct((rows, out_width), BF16),
                jax.ShapeDtypeStruct((rows, out_width), BF16),
                jax.ShapeDtypeStruct((pairs, width), BF16),
            ],
            in_specs=whole_vmem(5),
            out_specs=whole_vmem(3),
            scratch_shapes=[pltpu.VMEM((rows, width), BF16)] * 2,
            compiler_params=limit(rows),
        )(own, other, pair_w, down_w, hid_proj)
    got = send_rel(send, "test", 1)
    with jax.named_scope("pair"):
        sums = pl.pallas_call(
            functools.partial(pair_kernel, half, offsets),
            out_shape=[jax.ShapeDtypeStruct((pairs, out_width), BF16)] * groups,
            in_specs=whole_vmem(2),
            out_specs=whole_vmem(groups),
            compiler_params=limit(rows),
        )(keep, got)
    pieces = [send_plane(x, offset) for x, offset in zip(sums, offsets)] + [sums[-1]]
    grad_proj, test_rows = load(sums[-1], [[proj_grad[0]], [test_feats[0]]], limit(rows))
    grad_mine = dot_f32(mine, grad_proj, ((1,), (1,)))
    order = slot_order(experts)
    with jax.named_scope("score"):
        back = pl.pallas_call(
            functools.partial(score_kernel, half, order),
            out_shape=[jax.ShapeDtypeStruct((CAP, half + tests), BF16)] * experts,
            in_specs=whole_vmem(groups + 2),
            out_specs=whole_vmem(experts),
            scratch_shapes=[pltpu.VMEM((pairs, proj * proj), BF16)],
            compiler_params=limit(rows),
        )(*pieces, grad_mine, test_rows)
    slots = exchange(send_rel, back, experts)
    home = [slots[k] for k in order]
    with jax.named_scope("finish"):
        return pl.pallas_call(
            functools.partial(finish_kernel, experts),
            out_shape=[
                jax.ShapeDtypeStruct((tok_rows, half), BF16),
                jax.ShapeDtypeStruct((tok_rows, tests), F32),
            ],
            in_specs=whole_vmem(experts + 1),
            out_specs=in_hbm(2),
            scratch_shapes=[
                pltpu.VMEM((tok_rows, half), BF16),
                pltpu.VMEM((tok_rows, tests), F32),
                pltpu.VMEM((pairs, half + tests), BF16),
                pltpu.SemaphoreType.DMA((3,)),
            ],
            compiler_params=limit(rows),
        )(hits, *home)


def solution(mesh):
    placed = (
        P(("expert", "dp"), "test"),
        P(("expert", "dp"), "test"),
        P(("expert", "dp"), None),
        P(("expert", "dp"), None),
        P(("expert", "dp"), None),
        P("expert", None, ("dp", "test")),
        P("expert", None, ("dp", "test")),
        P("expert", ("dp", "test"), None),
        P("expert", None, ("dp", "test")),
        P("expert", None, None),
        P("expert", "test", None),
    )
    return jax.shard_map(
        on_device,
        mesh=mesh,
        in_specs=placed,
        out_specs=(P(("expert", "dp"), "test"), P(("expert", "dp"), "test")),
        check_vma=False,
    )
```

```python
import functools

import jax
import jax.numpy as jnp
from jax import lax
from jax.experimental import pallas as pl
from jax.experimental.pallas import tpu as pltpu
from jax.sharding import PartitionSpec as P

CAP = 2
KINDS = 4
BF16 = jnp.bfloat16
F32 = jnp.float32


def send_rel(block, axis, offset):
    size = lax.axis_size(axis)
    return lax.ppermute(block, axis, [(i, i ^ offset) for i in range(size)])


def send_cross(block, axis, offset):
    return send_rel(block, (axis, "test"), offset * lax.axis_size("test") + 1)


def plane_offsets(groups):
    offsets = [(g, g) for g in reversed(range(1, groups))]
    if groups > 2:
        offsets[-2:] = [(1, 2), (2, 1)]
    return offsets


def send_plane(block, offsets):
    pairs = []
    for g in range(lax.axis_size("dp")):
        pairs += [(2 * g + t, 2 * (g ^ offsets[t]) + 1 - t) for t in range(2)]
    return lax.ppermute(block, ("dp", "test"), pairs)


def is_direct(count):
    return count <= 4


def slot_order(count):
    slots = list(range(count))
    return slots[::-1] if is_direct(count) else slots[::2] + slots[1::2]


def exchange(send, parts, count):
    slots = dict(zip(slot_order(count), parts))
    if is_direct(count):
        got = {k: send(slots[k], "expert", k) for k in reversed(range(1, count))}
        return [slots[0]] + [got[k] for k in range(1, count)]
    unit = parts[0].shape[0]
    bit = 1
    while bit < count:
        moving = [k for k in range(count) if k & bit]
        got = send(jnp.concatenate([slots[k] for k in moving]), "expert", bit)
        for index, k in enumerate(moving):
            slots[k] = got[index * unit : (index + 1) * unit]
        bit *= 2
    return [slots[k] for k in range(count)]


def keep_in_hbm(array):
    return pltpu.with_memory_space_constraint(array, pltpu.HBM)


def dot_f32(a, b, contract):
    return lax.dot_general(a, b, (contract, ((), ())), preferred_element_type=F32)


def whole_vmem(count):
    return [pl.BlockSpec(memory_space=pltpu.VMEM)] * count


def in_hbm(count):
    return [pl.BlockSpec(memory_space=pltpu.HBM)] * count


def start_copies(pairs, sems):
    copies = [
        pltpu.make_async_copy(source, target, sems.at[index])
        for index, (source, target) in enumerate(pairs)
    ]
    for copy in copies:
        copy.start()
    return copies


def limit(rows):
    return pltpu.CompilerParams(vmem_limit_bytes=(8 << 20) + rows * (48 << 10))


def hit_tables(ids, slots, weights, want, experts):
    live = (slots >= 0) & (ids < experts)
    code = jnp.where(live, ids * CAP + slots, -1)
    hits = jnp.zeros((want.shape[0], ids.shape[1]), F32)
    scaled = hits
    for route in range(ids.shape[0]):
        match = code[route : route + 1, :] == want
        hits = jnp.where(match, 1.0, hits)
        scaled = jnp.where(match, weights[route : route + 1, :], scaled)
    return hits, scaled


def select_kernel(experts, *refs):
    sources, (hit_ref, *out_refs) = refs[:5], refs[5:-6]
    ids, slots, weight, tok, grad, sems = refs[-6:]
    copies = start_copies(zip(sources, (ids, slots, weight, tok, grad)), sems)
    here = lax.axis_index("expert")
    unit = KINDS * CAP
    quarter = tok.shape[1] // 2
    row = lax.broadcasted_iota(jnp.int32, (experts * unit, 1), 0)
    kind = (row % unit) // CAP
    turn = row // unit
    if is_direct(experts):
        turn = experts - 1 - turn
    else:
        turn = 2 * turn % experts + 2 * turn // experts
    want = (turn ^ here) * CAP + row % CAP
    for copy in copies[:3]:
        copy.wait()
    hits, scaled = hit_tables(ids[...], slots[...], weight[...].astype(F32), want, experts)
    hit_ref[...] = hits
    total = None
    for index in range(KINDS):
        table, source = (hits, tok) if index < 2 else (scaled, grad)
        if index % 2 == 0:
            copies[3 + index // 2].wait()
        left = jnp.where(kind == index, table, 0.0).astype(BF16)
        first = (index % 2) * quarter
        part = dot_f32(left, source[:, first : first + quarter], ((1,), (0,)))
        total = part if total is None else total + part
    total = total.astype(BF16)
    for k, out_ref in enumerate(out_refs):
        out_ref[...] = total[k * unit : (k + 1) * unit]


def arrange_kernel(*refs):
    *slot_refs, out_ref = refs
    slots = [ref[...].astype(F32) for ref in slot_refs[::-1]]
    pairs = CAP * len(slots)
    for kind in range(KINDS):
        rows = [slot[kind * CAP : (kind + 1) * CAP] for slot in slots]
        out_ref[kind * pairs : (kind + 1) * pairs] = jnp.concatenate(rows).astype(BF16)


def join_kernel(offsets, *refs):
    *block_refs, own_ref, out_ref = refs
    count = len(offsets) + 1
    pairs = own_ref.shape[0] // KINDS

    def place(ref, g):
        for kind in range(KINDS):
            first = (kind * count + g) * pairs
            out_ref[first : first + pairs] = ref[kind * pairs : (kind + 1) * pairs]

    place(own_ref, 0)
    for core in range(2):

        @pl.when(lax.axis_index("test") == core)
        def _():
            for ref, offset in zip(block_refs, offsets):
                place(ref, offset[1 - core])


def load_kernel(moves, *refs):
    count = 1 + max(move[0] for move in moves)
    sources, targets = refs[1 : 1 + count], refs[1 + count : -1]
    pairs = []
    for source, column, width, target, row, place in moves:
        rows = sources[source].shape[0]
        block = targets[target].at[row : row + rows, place : place + width]
        pairs.append((sources[source].at[:, column : column + width], block))
    for copy in start_copies(pairs, refs[-1]):
        copy.wait()


def split_two(value):
    high = value.astype(BF16)
    return jnp.concatenate([high, (value - high.astype(F32)).astype(BF16)], axis=1)


def join_two(value):
    value = value.astype(F32)
    middle = value.shape[1] // 2
    return value[:, :middle] + value[:, middle:]


def load(after, params, shapes, moves, compiler_params):
    with jax.named_scope("load"):
        return pl.pallas_call(
            functools.partial(load_kernel, moves),
            out_shape=[jax.ShapeDtypeStruct(shape, BF16) for shape in shapes],
            in_specs=whole_vmem(1) + in_hbm(len(params)),
            out_specs=whole_vmem(len(shapes)),
            scratch_shapes=[pltpu.SemaphoreType.DMA((len(moves),))],
            compiler_params=compiler_params,
            cost_estimate=pl.CostEstimate(
                flops=0, bytes_accessed=sum(2 * x.size for x in params), transcendentals=0
            ),
        )(after, *map(keep_in_hbm, params))


def expert_kernel(
    own_ref, other_ref, pair_w, down_w, proj_ref, keep_ref, send_ref, mine_ref, x_in, x_grad
):
    rows, width = x_in.shape
    half, quarter = width // 2, width // 4
    pairs, ff = mine_ref.shape[0], proj_ref.shape[1]
    core = lax.axis_index("test")
    near, far = pl.multiple_of(core * half, 128), pl.multiple_of((1 - core) * half, 128)
    row = lax.broadcasted_iota(jnp.int32, (rows, quarter), 0)
    odd = jnp.where(row >= pairs, 1, 0)
    slot = (row % pairs) // CAP
    if is_direct(pairs // CAP):
        odd = odd ^ jnp.where(slot > 0, 1, 0)
    else:
        for shift in range((pairs // CAP - 1).bit_length()):
            odd = odd ^ ((slot >> shift) & 1)
    odd = odd == 1
    for index in range(KINDS):
        own = own_ref[index * rows : (index + 1) * rows]
        other = other_ref[index * rows : (index + 1) * rows]
        for base, part in ((near, jnp.where(odd, other, own)), (far, jnp.where(odd, own, other))):
            first = (index % 2) * quarter
            if index < 2:
                x_in[:, pl.ds(pl.multiple_of(base + first, 128), quarter)] = part
            else:
                row = pl.multiple_of(base // half * rows, rows)
                x_grad[pl.ds(row, rows), first : first + quarter] = part
    mine_ref[:, :half] = x_grad[:pairs]
    mine_ref[:, half:] = x_grad[rows : rows + pairs]
    both_pre = dot_f32(x_in[...], pair_w[...], ((1,), (0,)))
    gate_pre, up_pre = both_pre[:, :ff], both_pre[:, ff:]
    hid_grads = dot_f32(x_grad[...], down_w[...], ((1,), (1,)))
    hid_grad = hid_grads[:rows, :ff] + hid_grads[rows:, ff:]
    sig = 1.0 / (1.0 + jnp.exp(-gate_pre))
    act_gate = gate_pre * sig
    hidden = (act_gate * up_pre).astype(BF16)
    tail = split_two(dot_f32(hidden, proj_ref[...], ((1,), (1,))))
    up_grad = (hid_grad * act_gate).astype(BF16)
    gate_grad = (hid_grad * up_pre * sig * (1.0 + gate_pre * (1.0 - sig))).astype(BF16)
    both_grad = jnp.concatenate([gate_grad, up_grad], axis=1)
    keep_ref[:, half:] = tail
    send_ref[:, half:] = tail
    for base, first_ref, rest_ref in ((far, send_ref, keep_ref), (near, keep_ref, send_ref)):
        for index in range(2):
            start = pl.multiple_of(base + index * quarter, 128)
            columns = slice(index * quarter, (index + 1) * quarter)
            part = dot_f32(both_grad, pair_w[pl.ds(start, quarter), :], ((1,), (1,)))
            part = part.astype(BF16)
            first_ref[:pairs, columns] = part[:pairs]
            rest_ref[pairs:, columns] = part[pairs:]


def pair_kernel(half, offsets, keep_ref, got_ref, *refs):
    *out_refs, own_ref = refs
    kept, got = keep_ref[...].astype(F32), got_ref[...].astype(F32)
    main = (kept[:, :half] + got[:, :half]).astype(BF16)
    tail = split_two(join_two(kept[:, half:]) + join_two(got[:, half:]))
    rows = own_ref.shape[0]

    def place(ref, g):
        ref[:, :half] = main[g * rows : (g + 1) * rows]
        ref[:, half:] = tail[g * rows : (g + 1) * rows]

    place(own_ref, 0)
    for core in range(2):

        @pl.when(lax.axis_index("test") == core)
        def _():
            for ref, offset in zip(out_refs, offsets):
                place(ref, offset[core])


def score_kernel(half, order, *refs):
    pieces = len(refs) - len(order) - 3
    piece_refs, (grad_ref, test_ref) = refs[:pieces], refs[pieces : pieces + 2]
    out_refs, feature = refs[pieces + 2 : -1], refs[-1]
    total = piece_refs[0][...].astype(F32)
    for piece_ref in piece_refs[1:]:
        total = total + piece_ref[...].astype(F32)
    hid = join_two(total[:, half:])
    grad = grad_ref[...]
    proj = grad.shape[1]
    grad = jnp.concatenate([grad, grad], axis=1)
    left = lax.broadcasted_iota(jnp.int32, grad.shape, 1) < proj
    for p in range(0, proj, 2):
        pair = jnp.where(left, hid[:, p : p + 1], hid[:, p + 1 : p + 2])
        feature[:, p * proj : (p + 2) * proj] = (pair * grad).astype(BF16)
    score = dot_f32(feature[...], test_ref[...], ((1,), (1,)))
    for k, out_ref in zip(order, out_refs):
        out_ref[:, :half] = total[k * CAP : (k + 1) * CAP, :half].astype(BF16)
        out_ref[:, half:] = score[k * CAP : (k + 1) * CAP].astype(BF16)


def finish_kernel(experts, hit_ref, *refs):
    slot_refs = refs[:experts]
    in_grad_hbm, scores_hbm, in_grad, scores, home_ref, sems = refs[experts:]
    unit = KINDS * CAP
    hits = jnp.concatenate([hit_ref[k * unit : k * unit + CAP] for k in range(experts)])
    home_ref[...] = jnp.concatenate([ref[...].astype(F32) for ref in slot_refs]).astype(BF16)
    half = in_grad.shape[1]
    quarter = half // 2
    hits = hits.T.astype(BF16)
    copies = []
    for index in range(2):
        columns = slice(index * quarter, (index + 1) * quarter)
        in_grad[:, columns] = dot_f32(hits, home_ref[:, columns], ((1,), (0,))).astype(BF16)
        copies += start_copies(
            [(in_grad.at[:, columns], in_grad_hbm.at[:, columns])], sems.at[pl.ds(index, 1)]
        )
    scores[...] = dot_f32(hits, home_ref[:, half:], ((1,), (0,)))
    copies += start_copies([(scores, scores_hbm)], sems.at[pl.ds(2, 1)])
    for copy in copies:
        copy.wait()


def on_device(
    tokens,
    out_grad,
    route_ids,
    route_slots,
    route_weight,
    w_gate,
    w_up,
    w_down,
    proj_hidden,
    proj_grad,
    test_feats,
):
    experts = lax.axis_size("expert")
    groups = lax.axis_size("dp")
    tok_rows, half = tokens.shape
    quarter = half // 2
    width = half * lax.axis_size("test")
    proj, tests = proj_hidden.shape[1], test_feats.shape[1]
    ff = w_gate.shape[2]
    pairs = experts * CAP
    rows = groups * pairs
    unit = KINDS * CAP
    out_width = half + 2 * proj
    ids_t, slots_t, weight_t = route_ids.T, route_slots.T, route_weight.T

    with jax.named_scope("select"):
        hits, *parts = pl.pallas_call(
            functools.partial(select_kernel, experts),
            out_shape=[jax.ShapeDtypeStruct((experts * unit, tok_rows), F32)]
            + [jax.ShapeDtypeStruct((unit, quarter), BF16)] * experts,
            in_specs=in_hbm(5),
            out_specs=whole_vmem(experts + 1),
            scratch_shapes=[
                pltpu.VMEM(x.shape, x.dtype) for x in (ids_t, slots_t, weight_t, tokens, out_grad)
            ]
            + [pltpu.SemaphoreType.DMA((5,))],
            compiler_params=limit(rows),
        )(*map(keep_in_hbm, (ids_t, slots_t, weight_t, tokens, out_grad)))
    slots = exchange(send_cross, parts, experts)
    with jax.named_scope("arrange"):
        block = pl.pallas_call(
            arrange_kernel,
            out_shape=jax.ShapeDtypeStruct((KINDS * pairs, quarter), BF16),
            in_specs=whole_vmem(experts),
            out_specs=whole_vmem(1)[0],
            compiler_params=limit(rows),
        )(*slots[::-1])
    offsets = plane_offsets(groups)
    blocks = [block] + [send_plane(block, offset) for offset in offsets[::-1]]
    loaded = load(
        block,
        [w_gate[0], w_up[0], w_down[0], proj_hidden[0]],
        [(width, 2 * ff), (2 * ff, half), (proj, ff)],
        [(0, 0, ff, 0, 0, 0), (1, 0, ff, 0, 0, ff)]
        + [(2, 0, half, 1, 0, 0), (2, half, half, 1, ff, 0), (3, 0, ff, 2, 0, 0)],
        limit(rows),
    )
    blocks, (pair_w, down_w, hid_proj) = lax.optimization_barrier((blocks, loaded))
    with jax.named_scope("join"):
        own = pl.pallas_call(
            functools.partial(join_kernel, offsets),
            out_shape=jax.ShapeDtypeStruct((KINDS * rows, quarter), BF16),
            in_specs=whole_vmem(groups),
            out_specs=whole_vmem(1)[0],
            compiler_params=limit(rows),
        )(*blocks[::-1])
    other = send_rel(own, "test", 1)
    with jax.named_scope("expert"):
        keep, send, mine = pl.pallas_call(
            expert_kernel,
            out_shape=[
                jax.ShapeDtypeStruct((rows, out_width), BF16),
                jax.ShapeDtypeStruct((rows, out_width), BF16),
                jax.ShapeDtypeStruct((pairs, width), BF16),
            ],
            in_specs=whole_vmem(5),
            out_specs=whole_vmem(3),
            scratch_shapes=[
                pltpu.VMEM((rows, width), BF16),
                pltpu.VMEM((2 * rows, half), BF16),
            ],
            compiler_params=limit(rows),
        )(own, other, pair_w, down_w, hid_proj)
    got = send_rel(send, "test", 1)
    with jax.named_scope("pair"):
        sums = pl.pallas_call(
            functools.partial(pair_kernel, half, offsets),
            out_shape=[jax.ShapeDtypeStruct((pairs, out_width), BF16)] * groups,
            in_specs=whole_vmem(2),
            out_specs=whole_vmem(groups),
            compiler_params=limit(rows),
        )(keep, got)
    pieces = [send_plane(x, offset) for x, offset in zip(sums, offsets)] + [sums[-1]]
    params = [proj_grad[0], test_feats[0]]
    moves = [(index, 0, x.shape[1], index, 0, 0) for index, x in enumerate(params)]
    grad_proj, test_rows = load(sums[-1], params, [x.shape for x in params], moves, limit(rows))
    grad_mine = dot_f32(mine, grad_proj, ((1,), (1,)))
    order = slot_order(experts)
    with jax.named_scope("score"):
        back = pl.pallas_call(
            functools.partial(score_kernel, half, order),
            out_shape=[jax.ShapeDtypeStruct((CAP, half + tests), BF16)] * experts,
            in_specs=whole_vmem(groups + 2),
            out_specs=whole_vmem(experts),
            scratch_shapes=[pltpu.VMEM((pairs, proj * proj), BF16)],
            compiler_params=limit(rows),
        )(*pieces, grad_mine, test_rows)
    slots = exchange(send_rel, back, experts)
    home = [slots[k] for k in order]
    with jax.named_scope("finish"):
        return pl.pallas_call(
            functools.partial(finish_kernel, experts),
            out_shape=[
                jax.ShapeDtypeStruct((tok_rows, half), BF16),
                jax.ShapeDtypeStruct((tok_rows, tests), F32),
            ],
            in_specs=whole_vmem(experts + 1),
            out_specs=in_hbm(2),
            scratch_shapes=[
                pltpu.VMEM((tok_rows, half), BF16),
                pltpu.VMEM((tok_rows, tests), F32),
                pltpu.VMEM((pairs, half + tests), BF16),
                pltpu.SemaphoreType.DMA((3,)),
            ],
            compiler_params=limit(rows),
        )(hits, *home)


def solution(mesh):
    placed = (
        P(("expert", "dp"), "test"),
        P(("expert", "dp"), "test"),
        P(("expert", "dp"), None),
        P(("expert", "dp"), None),
        P(("expert", "dp"), None),
        P("expert", None, ("dp", "test")),
        P("expert", None, ("dp", "test")),
        P("expert", ("dp", "test"), None),
        P("expert", None, ("dp", "test")),
        P("expert", None, None),
        P("expert", "test", None),
    )
    return jax.shard_map(
        on_device,
        mesh=mesh,
        in_specs=placed,
        out_specs=(P(("expert", "dp"), "test"), P(("expert", "dp"), "test")),
        check_vma=False,
    )
```

```python
import functools

import jax
import jax.numpy as jnp
from jax import lax
from jax.experimental import pallas as pl
from jax.experimental.pallas import tpu as pltpu
from jax.sharding import PartitionSpec as P

CAP = 2
KINDS = 4
BF16 = jnp.bfloat16
F32 = jnp.float32


def send_rel(block, axis, offset):
    size = lax.axis_size(axis)
    return lax.ppermute(block, axis, [(i, i ^ offset) for i in range(size)])


def send_cross(block, axis, offset):
    return send_rel(block, (axis, "test"), offset * lax.axis_size("test") + 1)


def plane_offsets(groups):
    offsets = [(g, g) for g in reversed(range(1, groups))]
    if groups > 2:
        offsets[-2:] = [(1, 2), (2, 1)]
    return offsets


def send_plane(block, offsets):
    pairs = []
    for g in range(lax.axis_size("dp")):
        pairs += [(2 * g + t, 2 * (g ^ offsets[t]) + 1 - t) for t in range(2)]
    return lax.ppermute(block, ("dp", "test"), pairs)


def is_direct(count):
    return count <= 4


def slot_order(count):
    slots = list(range(count))
    return slots[::-1] if is_direct(count) else slots[::2] + slots[1::2]


def exchange(send, parts, count):
    slots = dict(zip(slot_order(count), parts))
    if is_direct(count):
        got = {k: send(slots[k], "expert", k) for k in reversed(range(1, count))}
        return [slots[0]] + [got[k] for k in range(1, count)]
    unit = parts[0].shape[0]
    bit = 1
    while bit < count:
        moving = [k for k in range(count) if k & bit]
        got = send(jnp.concatenate([slots[k] for k in moving]), "expert", bit)
        for index, k in enumerate(moving):
            slots[k] = got[index * unit : (index + 1) * unit]
        bit *= 2
    return [slots[k] for k in range(count)]


def keep_in_hbm(array):
    return pltpu.with_memory_space_constraint(array, pltpu.HBM)


def dot_f32(a, b, contract):
    return lax.dot_general(a, b, (contract, ((), ())), preferred_element_type=F32)


def whole_vmem(count):
    return [pl.BlockSpec(memory_space=pltpu.VMEM)] * count


def in_hbm(count):
    return [pl.BlockSpec(memory_space=pltpu.HBM)] * count


def start_copies(pairs, sems):
    copies = [
        pltpu.make_async_copy(source, target, sems.at[index])
        for index, (source, target) in enumerate(pairs)
    ]
    for copy in copies:
        copy.start()
    return copies


def limit(rows):
    return pltpu.CompilerParams(vmem_limit_bytes=(8 << 20) + rows * (48 << 10))


def hit_tables(ids, slots, weights, want, experts):
    live = (slots >= 0) & (ids < experts)
    code = jnp.where(live, ids * CAP + slots, -1)
    hits = jnp.zeros((want.shape[0], ids.shape[1]), F32)
    scaled = hits
    for route in range(ids.shape[0]):
        match = code[route : route + 1, :] == want
        hits = jnp.where(match, 1.0, hits)
        scaled = jnp.where(match, weights[route : route + 1, :], scaled)
    return hits, scaled


def select_kernel(experts, *refs):
    sources, (hit_ref, *out_refs) = refs[:5], refs[5:-6]
    ids, slots, weight, tok, grad, sems = refs[-6:]
    copies = start_copies(zip(sources, (ids, slots, weight, tok, grad)), sems)
    here = lax.axis_index("expert")
    unit = KINDS * CAP
    quarter = tok.shape[1] // 2
    row = lax.broadcasted_iota(jnp.int32, (experts * unit, 1), 0)
    kind = (row % unit) // CAP
    turn = row // unit
    if is_direct(experts):
        turn = experts - 1 - turn
    else:
        turn = 2 * turn % experts + 2 * turn // experts
    want = (turn ^ here) * CAP + row % CAP
    for copy in copies[:3]:
        copy.wait()
    hits, scaled = hit_tables(ids[...], slots[...], weight[...].astype(F32), want, experts)
    hit_ref[...] = hits
    total = None
    for index in range(KINDS):
        table, source = (hits, tok) if index < 2 else (scaled, grad)
        if index % 2 == 0:
            copies[3 + index // 2].wait()
        left = jnp.where(kind == index, table, 0.0).astype(BF16)
        first = (index % 2) * quarter
        part = dot_f32(left, source[:, first : first + quarter], ((1,), (0,)))
        total = part if total is None else total + part
    total = total.astype(BF16)
    for k, out_ref in enumerate(out_refs):
        out_ref[...] = total[k * unit : (k + 1) * unit]


def arrange_kernel(*refs):
    *slot_refs, out_ref = refs
    slots = [ref[...].astype(F32) for ref in slot_refs[::-1]]
    pairs = CAP * len(slots)
    for kind in range(KINDS):
        rows = [slot[kind * CAP : (kind + 1) * CAP] for slot in slots]
        out_ref[kind * pairs : (kind + 1) * pairs] = jnp.concatenate(rows).astype(BF16)


def join_kernel(offsets, *refs):
    *block_refs, own_ref, out_ref = refs
    count = len(offsets) + 1
    pairs = own_ref.shape[0] // KINDS

    def place(ref, g):
        for kind in range(KINDS):
            first = (kind * count + g) * pairs
            out_ref[first : first + pairs] = ref[kind * pairs : (kind + 1) * pairs]

    place(own_ref, 0)
    for core in range(2):

        @pl.when(lax.axis_index("test") == core)
        def _():
            for ref, offset in zip(block_refs, offsets):
                place(ref, offset[1 - core])


def load_kernel(moves, *refs):
    count = 1 + max(move[0] for move in moves)
    sources, targets = refs[1 : 1 + count], refs[1 + count : -1]
    pairs = []
    for source, column, width, target, row, place in moves:
        rows = sources[source].shape[0]
        block = targets[target].at[row : row + rows, place : place + width]
        pairs.append((sources[source].at[:, column : column + width], block))
    for copy in start_copies(pairs, refs[-1]):
        copy.wait()


def split_two(value):
    high = value.astype(BF16)
    return jnp.concatenate([high, (value - high.astype(F32)).astype(BF16)], axis=1)


def join_two(value):
    value = value.astype(F32)
    middle = value.shape[1] // 2
    return value[:, :middle] + value[:, middle:]


def load(after, params, shapes, moves, compiler_params):
    with jax.named_scope("load"):
        return pl.pallas_call(
            functools.partial(load_kernel, moves),
            out_shape=[jax.ShapeDtypeStruct(shape, BF16) for shape in shapes],
            in_specs=whole_vmem(1) + in_hbm(len(params)),
            out_specs=whole_vmem(len(shapes)),
            scratch_shapes=[pltpu.SemaphoreType.DMA((len(moves),))],
            compiler_params=compiler_params,
            cost_estimate=pl.CostEstimate(
                flops=0, bytes_accessed=sum(2 * x.size for x in params), transcendentals=0
            ),
        )(after, *map(keep_in_hbm, params))


def expert_kernel(
    own_ref, other_ref, pair_w, down_w, proj_ref, keep_ref, send_ref, mine_ref, x_in, x_grad
):
    rows, width = x_in.shape
    half, quarter = width // 2, width // 4
    pairs, ff = mine_ref.shape[0], proj_ref.shape[1]
    core = lax.axis_index("test")
    near, far = pl.multiple_of(core * half, 128), pl.multiple_of((1 - core) * half, 128)
    row = lax.broadcasted_iota(jnp.int32, (rows, quarter), 0)
    odd = jnp.where(row >= pairs, 1, 0)
    slot = (row % pairs) // CAP
    if is_direct(pairs // CAP):
        odd = odd ^ jnp.where(slot > 0, 1, 0)
    else:
        for shift in range((pairs // CAP - 1).bit_length()):
            odd = odd ^ ((slot >> shift) & 1)
    odd = odd == 1
    for index in range(KINDS):
        own = own_ref[index * rows : (index + 1) * rows]
        other = other_ref[index * rows : (index + 1) * rows]
        for base, part in ((near, jnp.where(odd, other, own)), (far, jnp.where(odd, own, other))):
            first = (index % 2) * quarter
            if index < 2:
                x_in[:, pl.ds(pl.multiple_of(base + first, 128), quarter)] = part
            else:
                row = pl.multiple_of(base // half * rows, rows)
                x_grad[pl.ds(row, rows), first : first + quarter] = part
    mine_ref[:, :half] = x_grad[:pairs]
    mine_ref[:, half:] = x_grad[rows : rows + pairs]
    both_pre = dot_f32(x_in[...], pair_w[...], ((1,), (0,)))
    gate_pre, up_pre = both_pre[:, :ff], both_pre[:, ff:]
    hid_grads = dot_f32(x_grad[...], down_w[...], ((1,), (1,)))
    hid_grad = hid_grads[:rows, :ff] + hid_grads[rows:, ff:]
    sig = 1.0 / (1.0 + jnp.exp(-gate_pre))
    act_gate = gate_pre * sig
    hidden = (act_gate * up_pre).astype(BF16)
    tail = split_two(dot_f32(hidden, proj_ref[...], ((1,), (1,))))
    up_grad = (hid_grad * act_gate).astype(BF16)
    gate_grad = (hid_grad * up_pre * sig * (1.0 + gate_pre * (1.0 - sig))).astype(BF16)
    both_grad = jnp.concatenate([gate_grad, up_grad], axis=1)
    keep_ref[:, half:] = tail
    send_ref[:, half:] = tail
    for base, first_ref, rest_ref in ((far, send_ref, keep_ref), (near, keep_ref, send_ref)):
        for index in range(2):
            start = pl.multiple_of(base + index * quarter, 128)
            columns = slice(index * quarter, (index + 1) * quarter)
            part = dot_f32(both_grad, pair_w[pl.ds(start, quarter), :], ((1,), (1,)))
            part = part.astype(BF16)
            first_ref[:pairs, columns] = part[:pairs]
            rest_ref[pairs:, columns] = part[pairs:]


def pair_kernel(half, offsets, keep_ref, got_ref, *refs):
    *out_refs, own_ref = refs
    main = keep_ref[:, :half] + got_ref[:, :half]
    tail = split_two(join_two(keep_ref[:, half:]) + join_two(got_ref[:, half:]))
    rows = own_ref.shape[0]

    def place(ref, g):
        ref[:, :half] = main[g * rows : (g + 1) * rows]
        ref[:, half:] = tail[g * rows : (g + 1) * rows]

    place(own_ref, 0)
    for core in range(2):

        @pl.when(lax.axis_index("test") == core)
        def _():
            for ref, offset in zip(out_refs, offsets):
                place(ref, offset[core])


def score_kernel(half, order, *refs):
    pieces = len(refs) - len(order) - 3
    piece_refs, (grad_ref, test_ref) = refs[:pieces], refs[pieces : pieces + 2]
    out_refs, feature = refs[pieces + 2 : -1], refs[-1]
    total = piece_refs[0][...].astype(F32)
    for piece_ref in piece_refs[1:]:
        total = total + piece_ref[...].astype(F32)
    hid = join_two(total[:, half:])
    grad = grad_ref[...]
    proj = grad.shape[1]
    grad = jnp.concatenate([grad, grad], axis=1)
    left = lax.broadcasted_iota(jnp.int32, grad.shape, 1) < proj
    for p in range(0, proj, 2):
        pair = jnp.where(left, hid[:, p : p + 1], hid[:, p + 1 : p + 2])
        row, first = divmod(p * proj, feature.shape[1])
        row *= total.shape[0]
        feature[row : row + total.shape[0], first : first + 2 * proj] = (pair * grad).astype(BF16)
    scores = dot_f32(feature[...], test_ref[...], ((1,), (1,)))
    rows, tests = total.shape[0], test_ref.shape[0] // 2
    score = scores[:rows, :tests] + scores[rows:, tests:]
    for k, out_ref in zip(order, out_refs):
        out_ref[:, :half] = total[k * CAP : (k + 1) * CAP, :half].astype(BF16)
        out_ref[:, half:] = score[k * CAP : (k + 1) * CAP].astype(BF16)


def finish_kernel(experts, hit_ref, *refs):
    slot_refs = refs[:experts]
    in_grad_hbm, scores_hbm, in_grad, scores, home_ref, sems = refs[experts:]
    home_ref[...] = jnp.concatenate([ref[...].astype(F32) for ref in slot_refs]).astype(BF16)
    hits = hit_ref[...]
    half = in_grad.shape[1]
    quarter = half // 2
    copies = []
    for index in range(2):
        columns = slice(index * quarter, (index + 1) * quarter)
        in_grad[:, columns] = dot_f32(hits, home_ref[:, columns], ((1,), (0,))).astype(BF16)
        copies += start_copies(
            [(in_grad.at[:, columns], in_grad_hbm.at[:, columns])], sems.at[pl.ds(index, 1)]
        )
    scores[...] = dot_f32(hits, home_ref[:, half:], ((1,), (0,)))
    copies += start_copies([(scores, scores_hbm)], sems.at[pl.ds(2, 1)])
    for copy in copies:
        copy.wait()


def on_device(
    tokens,
    out_grad,
    route_ids,
    route_slots,
    route_weight,
    w_gate,
    w_up,
    w_down,
    proj_hidden,
    proj_grad,
    test_feats,
):
    experts = lax.axis_size("expert")
    groups = lax.axis_size("dp")
    tok_rows, half = tokens.shape
    quarter = half // 2
    width = half * lax.axis_size("test")
    proj, tests = proj_hidden.shape[1], test_feats.shape[1]
    ff = w_gate.shape[2]
    pairs = experts * CAP
    rows = groups * pairs
    unit = KINDS * CAP
    out_width = half + 2 * proj
    ids_t, slots_t, weight_t = route_ids.T, route_slots.T, route_weight.T

    with jax.named_scope("select"):
        hits, *parts = pl.pallas_call(
            functools.partial(select_kernel, experts),
            out_shape=[jax.ShapeDtypeStruct((experts * unit, tok_rows), F32)]
            + [jax.ShapeDtypeStruct((unit, quarter), BF16)] * experts,
            in_specs=in_hbm(5),
            out_specs=whole_vmem(experts + 1),
            scratch_shapes=[
                pltpu.VMEM(x.shape, x.dtype) for x in (ids_t, slots_t, weight_t, tokens, out_grad)
            ]
            + [pltpu.SemaphoreType.DMA((5,))],
            compiler_params=limit(rows),
        )(*map(keep_in_hbm, (ids_t, slots_t, weight_t, tokens, out_grad)))
    slots = exchange(send_cross, parts, experts)
    with jax.named_scope("arrange"):
        block = pl.pallas_call(
            arrange_kernel,
            out_shape=jax.ShapeDtypeStruct((KINDS * pairs, quarter), BF16),
            in_specs=whole_vmem(experts),
            out_specs=whole_vmem(1)[0],
            compiler_params=limit(rows),
        )(*slots[::-1])
    offsets = plane_offsets(groups)
    blocks = [block] + [send_plane(block, offset) for offset in offsets[::-1]]
    loaded = load(
        block,
        [w_gate[0], w_up[0], w_down[0], proj_hidden[0]],
        [(width, 2 * ff), (2 * ff, half), (proj, ff)],
        [(0, 0, ff, 0, 0, 0), (1, 0, ff, 0, 0, ff)]
        + [(2, 0, half, 1, 0, 0), (2, half, half, 1, ff, 0), (3, 0, ff, 2, 0, 0)],
        limit(rows),
    )
    blocks, (pair_w, down_w, hid_proj) = lax.optimization_barrier((blocks, loaded))
    with jax.named_scope("join"):
        own = pl.pallas_call(
            functools.partial(join_kernel, offsets),
            out_shape=jax.ShapeDtypeStruct((KINDS * rows, quarter), BF16),
            in_specs=whole_vmem(groups),
            out_specs=whole_vmem(1)[0],
            compiler_params=limit(rows),
        )(*blocks[::-1])
    other = send_rel(own, "test", 1)
    with jax.named_scope("expert"):
        keep, send, mine = pl.pallas_call(
            expert_kernel,
            out_shape=[
                jax.ShapeDtypeStruct((rows, out_width), BF16),
                jax.ShapeDtypeStruct((rows, out_width), BF16),
                jax.ShapeDtypeStruct((pairs, width), BF16),
            ],
            in_specs=whole_vmem(5),
            out_specs=whole_vmem(3),
            scratch_shapes=[
                pltpu.VMEM((rows, width), BF16),
                pltpu.VMEM((2 * rows, half), BF16),
            ],
            compiler_params=limit(rows),
        )(own, other, pair_w, down_w, hid_proj)
    got = send_rel(send, "test", 1)
    with jax.named_scope("pair"):
        sums = pl.pallas_call(
            functools.partial(pair_kernel, half, offsets),
            out_shape=[jax.ShapeDtypeStruct((pairs, out_width), BF16)] * groups,
            in_specs=whole_vmem(2),
            out_specs=whole_vmem(groups),
            compiler_params=limit(rows),
        )(keep, got)
    pieces = [send_plane(x, offset) for x, offset in zip(sums, offsets)] + [sums[-1]]
    depth = proj * proj // 2
    grad_proj, test_rows = load(
        sums[-1],
        [proj_grad[0], test_feats[0]],
        [(proj, width), (2 * tests, depth)],
        [(0, 0, width, 0, 0, 0), (1, 0, depth, 1, 0, 0), (1, depth, depth, 1, tests, 0)],
        limit(rows),
    )
    hits, mine = lax.optimization_barrier((hits, mine))
    hits = hits.reshape(experts, KINDS, CAP, tok_rows)[:, 0].reshape(pairs, tok_rows)
    hits = hits.T.astype(BF16)
    grad_mine = dot_f32(mine, grad_proj, ((1,), (1,)))
    order = slot_order(experts)
    with jax.named_scope("score"):
        back = pl.pallas_call(
            functools.partial(score_kernel, half, order),
            out_shape=[jax.ShapeDtypeStruct((CAP, half + tests), BF16)] * experts,
            in_specs=whole_vmem(groups + 2),
            out_specs=whole_vmem(experts),
            scratch_shapes=[pltpu.VMEM((2 * pairs, proj * proj // 2), BF16)],
            compiler_params=limit(rows),
        )(*pieces, grad_mine, test_rows)
    slots = exchange(send_rel, back, experts)
    home = [slots[k] for k in order]
    with jax.named_scope("finish"):
        return pl.pallas_call(
            functools.partial(finish_kernel, experts),
            out_shape=[
                jax.ShapeDtypeStruct((tok_rows, half), BF16),
                jax.ShapeDtypeStruct((tok_rows, tests), F32),
            ],
            in_specs=whole_vmem(experts + 1),
            out_specs=in_hbm(2),
            scratch_shapes=[
                pltpu.VMEM((tok_rows, half), BF16),
                pltpu.VMEM((tok_rows, tests), F32),
                pltpu.VMEM((pairs, half + tests), BF16),
                pltpu.SemaphoreType.DMA((3,)),
            ],
            compiler_params=limit(rows),
        )(hits, *home)


def solution(mesh):
    placed = (
        P(("expert", "dp"), "test"),
        P(("expert", "dp"), "test"),
        P(("expert", "dp"), None),
        P(("expert", "dp"), None),
        P(("expert", "dp"), None),
        P("expert", None, ("dp", "test")),
        P("expert", None, ("dp", "test")),
        P("expert", ("dp", "test"), None),
        P("expert", None, ("dp", "test")),
        P("expert", None, None),
        P("expert", "test", None),
    )
    return jax.shard_map(
        on_device,
        mesh=mesh,
        in_specs=placed,
        out_specs=(P(("expert", "dp"), "test"), P(("expert", "dp"), "test")),
        check_vma=False,
    )
```

```python
import functools

import jax
import jax.numpy as jnp
from jax import lax
from jax.experimental import pallas as pl
from jax.experimental.pallas import tpu as pltpu
from jax.sharding import PartitionSpec as P

CAP = 2
KINDS = 4
BF16 = jnp.bfloat16
F32 = jnp.float32


def send_rel(block, axis, offset):
    size = lax.axis_size(axis)
    return lax.ppermute(block, axis, [(i, i ^ offset) for i in range(size)])


def send_cross(block, axis, offset):
    return send_rel(block, (axis, "test"), offset * lax.axis_size("test") + 1)


def plane_offsets(groups):
    offsets = [(g, g) for g in reversed(range(1, groups))]
    if groups > 2:
        offsets[-2:] = [(1, 2), (2, 1)]
    return offsets


def send_plane(block, offsets):
    pairs = []
    for g in range(lax.axis_size("dp")):
        pairs += [(2 * g + t, 2 * (g ^ offsets[t]) + 1 - t) for t in range(2)]
    return lax.ppermute(block, ("dp", "test"), pairs)


def is_direct(count):
    return count <= 4


def slot_order(count):
    slots = list(range(count))
    return slots[::-1] if is_direct(count) else slots[::2] + slots[1::2]


def exchange(send, parts, count):
    slots = dict(zip(slot_order(count), parts))
    if is_direct(count):
        got = {k: send(slots[k], "expert", k) for k in reversed(range(1, count))}
        return [slots[0]] + [got[k] for k in range(1, count)]
    unit = parts[0].shape[0]
    bit = 1
    while bit < count:
        moving = [k for k in range(count) if k & bit]
        got = send(jnp.concatenate([slots[k] for k in moving]), "expert", bit)
        for index, k in enumerate(moving):
            slots[k] = got[index * unit : (index + 1) * unit]
        bit *= 2
    return [slots[k] for k in range(count)]


def keep_in_hbm(array):
    return pltpu.with_memory_space_constraint(array, pltpu.HBM)


def dot_f32(a, b, contract):
    return lax.dot_general(a, b, (contract, ((), ())), preferred_element_type=F32)


def whole_vmem(count):
    return [pl.BlockSpec(memory_space=pltpu.VMEM)] * count


def in_hbm(count):
    return [pl.BlockSpec(memory_space=pltpu.HBM)] * count


def start_copies(pairs, sems):
    copies = [
        pltpu.make_async_copy(source, target, sems.at[index])
        for index, (source, target) in enumerate(pairs)
    ]
    for copy in copies:
        copy.start()
    return copies


def limit(rows):
    return pltpu.CompilerParams(vmem_limit_bytes=(8 << 20) + rows * (48 << 10))


def hit_tables(ids, slots, weights, want, experts):
    live = (slots >= 0) & (ids < experts)
    code = jnp.where(live, ids * CAP + slots, -1)
    hits = jnp.zeros((want.shape[0], ids.shape[1]), F32)
    scaled = hits
    for route in range(ids.shape[0]):
        match = code[route : route + 1, :] == want
        hits = jnp.where(match, 1.0, hits)
        scaled = jnp.where(match, weights[route : route + 1, :], scaled)
    return hits, scaled


def select_kernel(experts, *refs):
    sources, (hit_ref, *out_refs) = refs[:5], refs[5:-6]
    ids, slots, weight, tok, grad, sems = refs[-6:]
    copies = start_copies(zip(sources, (ids, slots, weight, tok, grad)), sems)
    here = lax.axis_index("expert")
    unit = KINDS * CAP
    quarter = tok.shape[1] // 2
    row = lax.broadcasted_iota(jnp.int32, (experts * unit, 1), 0)
    kind = (row % unit) // CAP
    turn = row // unit
    if is_direct(experts):
        turn = experts - 1 - turn
    else:
        turn = 2 * turn % experts + 2 * turn // experts
    want = (turn ^ here) * CAP + row % CAP
    for copy in copies[:3]:
        copy.wait()
    hits, scaled = hit_tables(ids[...], slots[...], weight[...].astype(F32), want, experts)
    hit_ref[...] = hits
    total = None
    for index in range(KINDS):
        table, source = (hits, tok) if index < 2 else (scaled, grad)
        if index % 2 == 0:
            copies[3 + index // 2].wait()
        left = jnp.where(kind == index, table, 0.0).astype(BF16)
        first = (index % 2) * quarter
        part = dot_f32(left, source[:, first : first + quarter], ((1,), (0,)))
        total = part if total is None else total + part
    total = total.astype(BF16)
    for k, out_ref in enumerate(out_refs):
        out_ref[...] = total[k * unit : (k + 1) * unit]


def arrange_kernel(order, *refs):
    *slot_refs, out_ref = refs
    slots = [slot_refs[order.index(k)][...].astype(F32) for k in range(len(order))]
    pairs = CAP * len(slots)
    for kind in range(KINDS):
        rows = [slot[kind * CAP : (kind + 1) * CAP] for slot in slots]
        out_ref[kind * pairs : (kind + 1) * pairs] = jnp.concatenate(rows).astype(BF16)


def join_kernel(offsets, *refs):
    *block_refs, own_ref, out_ref = refs
    count = len(offsets) + 1
    pairs = own_ref.shape[0] // KINDS

    def place(ref, g):
        for kind in range(KINDS):
            first = (kind * count + g) * pairs
            out_ref[first : first + pairs] = ref[kind * pairs : (kind + 1) * pairs]

    place(own_ref, 0)
    for core in range(2):

        @pl.when(lax.axis_index("test") == core)
        def _():
            for ref, offset in zip(block_refs, offsets):
                place(ref, offset[1 - core])


def load_kernel(moves, *refs):
    count = 1 + max(move[0] for move in moves)
    sources, targets = refs[1 : 1 + count], refs[1 + count : -1]
    pairs = []
    for source, column, width, target, row, place in moves:
        rows = sources[source].shape[0]
        block = targets[target].at[row : row + rows, place : place + width]
        pairs.append((sources[source].at[:, column : column + width], block))
    for copy in start_copies(pairs, refs[-1]):
        copy.wait()


def split_two(value):
    high = value.astype(BF16)
    return jnp.concatenate([high, (value - high.astype(F32)).astype(BF16)], axis=1)


def join_two(value):
    value = value.astype(F32)
    middle = value.shape[1] // 2
    return value[:, :middle] + value[:, middle:]


def load(after, params, shapes, moves, compiler_params):
    with jax.named_scope("load"):
        return pl.pallas_call(
            functools.partial(load_kernel, moves),
            out_shape=[jax.ShapeDtypeStruct(shape, BF16) for shape in shapes],
            in_specs=whole_vmem(1) + in_hbm(len(params)),
            out_specs=whole_vmem(len(shapes)),
            scratch_shapes=[pltpu.SemaphoreType.DMA((len(moves),))],
            compiler_params=compiler_params,
            cost_estimate=pl.CostEstimate(
                flops=0, bytes_accessed=sum(2 * x.size for x in params), transcendentals=0
            ),
        )(after, *map(keep_in_hbm, params))


def expert_kernel(
    own_ref, other_ref, pair_w, down_w, proj_ref, keep_ref, send_ref, mine_ref, x_in, x_grad
):
    rows, width = x_in.shape
    half, quarter = width // 2, width // 4
    pairs, ff = mine_ref.shape[0], proj_ref.shape[1]
    core = lax.axis_index("test")
    near, far = pl.multiple_of(core * half, 128), pl.multiple_of((1 - core) * half, 128)
    row = lax.broadcasted_iota(jnp.int32, (rows, quarter), 0)
    odd = jnp.where(row >= pairs, 1, 0)
    slot = (row % pairs) // CAP
    if is_direct(pairs // CAP):
        odd = odd ^ jnp.where(slot > 0, 1, 0)
    else:
        for shift in range((pairs // CAP - 1).bit_length()):
            odd = odd ^ ((slot >> shift) & 1)
    odd = odd == 1
    for index in range(KINDS):
        own = own_ref[index * rows : (index + 1) * rows]
        other = other_ref[index * rows : (index + 1) * rows]
        for base, part in ((near, jnp.where(odd, other, own)), (far, jnp.where(odd, own, other))):
            first = (index % 2) * quarter
            if index < 2:
                x_in[:, pl.ds(pl.multiple_of(base + first, 128), quarter)] = part
            else:
                row = pl.multiple_of(base // half * rows, rows)
                x_grad[pl.ds(row, rows), first : first + quarter] = part
    mine_ref[:, :half] = x_grad[:pairs]
    mine_ref[:, half:] = x_grad[rows : rows + pairs]
    both_pre = dot_f32(x_in[...], pair_w[...], ((1,), (0,)))
    gate_pre, up_pre = both_pre[:, :ff], both_pre[:, ff:]
    hid_grads = dot_f32(x_grad[...], down_w[...], ((1,), (1,)))
    hid_grad = hid_grads[:rows, :ff] + hid_grads[rows:, ff:]
    sig = 1.0 / (1.0 + jnp.exp(-gate_pre))
    act_gate = gate_pre * sig
    hidden = (act_gate * up_pre).astype(BF16)
    tail = split_two(dot_f32(hidden, proj_ref[...], ((1,), (1,))))
    up_grad = (hid_grad * act_gate).astype(BF16)
    gate_grad = (hid_grad * up_pre * sig * (1.0 + gate_pre * (1.0 - sig))).astype(BF16)
    both_grad = jnp.concatenate([gate_grad, up_grad], axis=1)
    keep_ref[:, half:] = tail
    send_ref[:, half:] = tail
    for base, first_ref, rest_ref in ((far, send_ref, keep_ref), (near, keep_ref, send_ref)):
        for index in range(2):
            start = pl.multiple_of(base + index * quarter, 128)
            columns = slice(index * quarter, (index + 1) * quarter)
            part = dot_f32(both_grad, pair_w[pl.ds(start, quarter), :], ((1,), (1,)))
            part = part.astype(BF16)
            first_ref[:pairs, columns] = part[:pairs]
            rest_ref[pairs:, columns] = part[pairs:]


def pair_kernel(half, offsets, keep_ref, got_ref, *refs):
    *out_refs, own_ref = refs
    main = keep_ref[:, :half] + got_ref[:, :half]
    tail = split_two(join_two(keep_ref[:, half:]) + join_two(got_ref[:, half:]))
    rows = own_ref.shape[0]

    def place(ref, g):
        ref[:, :half] = main[g * rows : (g + 1) * rows]
        ref[:, half:] = tail[g * rows : (g + 1) * rows]

    place(own_ref, 0)
    for core in range(2):

        @pl.when(lax.axis_index("test") == core)
        def _():
            for ref, offset in zip(out_refs, offsets):
                place(ref, offset[core])


def score_kernel(half, order, *refs):
    pieces = len(refs) - len(order) - 3
    piece_refs, (grad_ref, test_ref) = refs[:pieces], refs[pieces : pieces + 2]
    out_refs, feature = refs[pieces + 2 : -1], refs[-1]
    total = piece_refs[0][...].astype(F32)
    for piece_ref in piece_refs[1:]:
        total = total + piece_ref[...].astype(F32)
    hid = join_two(total[:, half:])
    grad = grad_ref[...]
    proj = grad.shape[1]
    grad = jnp.concatenate([grad, grad], axis=1)
    left = lax.broadcasted_iota(jnp.int32, grad.shape, 1) < proj
    for p in range(0, proj, 2):
        pair = jnp.where(left, hid[:, p : p + 1], hid[:, p + 1 : p + 2])
        row, first = divmod(p * proj, feature.shape[1])
        row *= total.shape[0]
        feature[row : row + total.shape[0], first : first + 2 * proj] = (pair * grad).astype(BF16)
    scores = dot_f32(feature[...], test_ref[...], ((1,), (1,)))
    rows, tests = total.shape[0], test_ref.shape[0] // 2
    score = scores[:rows, :tests] + scores[rows:, tests:]
    for k, out_ref in zip(order, out_refs):
        out_ref[:, :half] = total[k * CAP : (k + 1) * CAP, :half].astype(BF16)
        out_ref[:, half:] = score[k * CAP : (k + 1) * CAP].astype(BF16)


def finish_kernel(experts, hit_ref, *refs):
    slot_refs = refs[:experts]
    in_grad_hbm, scores_hbm, in_grad, scores, home_ref, sems = refs[experts:]
    home_ref[...] = jnp.concatenate([ref[...].astype(F32) for ref in slot_refs]).astype(BF16)
    hits = hit_ref[...]
    half = in_grad.shape[1]
    quarter = half // 2
    copies = []
    for index in range(2):
        columns = slice(index * quarter, (index + 1) * quarter)
        in_grad[:, columns] = dot_f32(hits, home_ref[:, columns], ((1,), (0,))).astype(BF16)
        copies += start_copies(
            [(in_grad.at[:, columns], in_grad_hbm.at[:, columns])], sems.at[pl.ds(index, 1)]
        )
    scores[...] = dot_f32(hits, home_ref[:, half:], ((1,), (0,)))
    copies += start_copies([(scores, scores_hbm)], sems.at[pl.ds(2, 1)])
    for copy in copies:
        copy.wait()


def on_device(
    tokens,
    out_grad,
    route_ids,
    route_slots,
    route_weight,
    w_gate,
    w_up,
    w_down,
    proj_hidden,
    proj_grad,
    test_feats,
):
    experts = lax.axis_size("expert")
    groups = lax.axis_size("dp")
    tok_rows, half = tokens.shape
    quarter = half // 2
    width = half * lax.axis_size("test")
    proj, tests = proj_hidden.shape[1], test_feats.shape[1]
    ff = w_gate.shape[2]
    pairs = experts * CAP
    rows = groups * pairs
    unit = KINDS * CAP
    out_width = half + 2 * proj
    ids_t, slots_t, weight_t = route_ids.T, route_slots.T, route_weight.T

    with jax.named_scope("select"):
        hits, *parts = pl.pallas_call(
            functools.partial(select_kernel, experts),
            out_shape=[jax.ShapeDtypeStruct((experts * unit, tok_rows), F32)]
            + [jax.ShapeDtypeStruct((unit, quarter), BF16)] * experts,
            in_specs=in_hbm(5),
            out_specs=whole_vmem(experts + 1),
            scratch_shapes=[
                pltpu.VMEM(x.shape, x.dtype) for x in (ids_t, slots_t, weight_t, tokens, out_grad)
            ]
            + [pltpu.SemaphoreType.DMA((5,))],
            compiler_params=limit(rows),
        )(*map(keep_in_hbm, (ids_t, slots_t, weight_t, tokens, out_grad)))
    slots = exchange(send_cross, parts, experts)
    arrival = [2, 3, 1, 0] if experts == 4 else slot_order(experts)
    with jax.named_scope("arrange"):
        block = pl.pallas_call(
            functools.partial(arrange_kernel, arrival),
            out_shape=jax.ShapeDtypeStruct((KINDS * pairs, quarter), BF16),
            in_specs=whole_vmem(experts),
            out_specs=whole_vmem(1)[0],
            compiler_params=limit(rows),
        )(*[slots[k] for k in arrival])
    offsets = plane_offsets(groups)
    blocks = [block] + [send_plane(block, offset) for offset in offsets[::-1]]
    loaded = load(
        block,
        [w_gate[0], w_up[0], w_down[0], proj_hidden[0]],
        [(width, 2 * ff), (2 * ff, half), (proj, ff)],
        [(0, 0, ff, 0, 0, 0), (1, 0, ff, 0, 0, ff)]
        + [(2, 0, half, 1, 0, 0), (2, half, half, 1, ff, 0), (3, 0, ff, 2, 0, 0)],
        limit(rows),
    )
    blocks, (pair_w, down_w, hid_proj) = lax.optimization_barrier((blocks, loaded))
    with jax.named_scope("join"):
        own = pl.pallas_call(
            functools.partial(join_kernel, offsets),
            out_shape=jax.ShapeDtypeStruct((KINDS * rows, quarter), BF16),
            in_specs=whole_vmem(groups),
            out_specs=whole_vmem(1)[0],
            compiler_params=limit(rows),
        )(*blocks[::-1])
    other = send_rel(own, "test", 1)
    with jax.named_scope("expert"):
        keep, send, mine = pl.pallas_call(
            expert_kernel,
            out_shape=[
                jax.ShapeDtypeStruct((rows, out_width), BF16),
                jax.ShapeDtypeStruct((rows, out_width), BF16),
                jax.ShapeDtypeStruct((pairs, width), BF16),
            ],
            in_specs=whole_vmem(5),
            out_specs=whole_vmem(3),
            scratch_shapes=[
                pltpu.VMEM((rows, width), BF16),
                pltpu.VMEM((2 * rows, half), BF16),
            ],
            compiler_params=limit(rows),
        )(own, other, pair_w, down_w, hid_proj)
    got = send_rel(send, "test", 1)
    with jax.named_scope("pair"):
        sums = pl.pallas_call(
            functools.partial(pair_kernel, half, offsets),
            out_shape=[jax.ShapeDtypeStruct((pairs, out_width), BF16)] * groups,
            in_specs=whole_vmem(2),
            out_specs=whole_vmem(groups),
            compiler_params=limit(rows),
        )(keep, got)
    pieces = [send_plane(x, offset) for x, offset in zip(sums, offsets)] + [sums[-1]]
    depth = proj * proj // 2
    grad_proj, test_rows = load(
        sums[-1],
        [proj_grad[0], test_feats[0]],
        [(proj, width), (2 * tests, depth)],
        [(0, 0, width, 0, 0, 0), (1, 0, depth, 1, 0, 0), (1, depth, depth, 1, tests, 0)],
        limit(rows),
    )
    hits, mine = lax.optimization_barrier((hits, mine))
    hits = hits.reshape(experts, KINDS, CAP, tok_rows)[:, 0].reshape(pairs, tok_rows)
    hits = hits.T.astype(BF16)
    grad_mine = dot_f32(mine, grad_proj, ((1,), (1,)))
    order = slot_order(experts)
    with jax.named_scope("score"):
        back = pl.pallas_call(
            functools.partial(score_kernel, half, order),
            out_shape=[jax.ShapeDtypeStruct((CAP, half + tests), BF16)] * experts,
            in_specs=whole_vmem(groups + 2),
            out_specs=whole_vmem(experts),
            scratch_shapes=[pltpu.VMEM((2 * pairs, proj * proj // 2), BF16)],
            compiler_params=limit(rows),
        )(*pieces, grad_mine, test_rows)
    slots = exchange(send_rel, back, experts)
    home = [slots[k] for k in order]
    with jax.named_scope("finish"):
        return pl.pallas_call(
            functools.partial(finish_kernel, experts),
            out_shape=[
                jax.ShapeDtypeStruct((tok_rows, half), BF16),
                jax.ShapeDtypeStruct((tok_rows, tests), F32),
            ],
            in_specs=whole_vmem(experts + 1),
            out_specs=in_hbm(2),
            scratch_shapes=[
                pltpu.VMEM((tok_rows, half), BF16),
                pltpu.VMEM((tok_rows, tests), F32),
                pltpu.VMEM((pairs, half + tests), BF16),
                pltpu.SemaphoreType.DMA((3,)),
            ],
            compiler_params=limit(rows),
        )(hits, *home)


def solution(mesh):
    placed = (
        P(("expert", "dp"), "test"),
        P(("expert", "dp"), "test"),
        P(("expert", "dp"), None),
        P(("expert", "dp"), None),
        P(("expert", "dp"), None),
        P("expert", None, ("dp", "test")),
        P("expert", None, ("dp", "test")),
        P("expert", ("dp", "test"), None),
        P("expert", None, ("dp", "test")),
        P("expert", None, None),
        P("expert", "test", None),
    )
    return jax.shard_map(
        on_device,
        mesh=mesh,
        in_specs=placed,
        out_specs=(P(("expert", "dp"), "test"), P(("expert", "dp"), "test")),
        check_vma=False,
    )
```

```python
import functools

import jax
import jax.numpy as jnp
from jax import lax
from jax.experimental import pallas as pl
from jax.experimental.pallas import tpu as pltpu
from jax.sharding import PartitionSpec as P

CAP = 2
KINDS = 4
BF16 = jnp.bfloat16
F32 = jnp.float32


def send_rel(block, axis, offset):
    size = lax.axis_size(axis)
    return lax.ppermute(block, axis, [(i, i ^ offset) for i in range(size)])


def send_cross(block, axis, offset):
    return send_rel(block, (axis, "test"), offset * lax.axis_size("test") + 1)


def plane_offsets(groups):
    offsets = [(g, g) for g in reversed(range(1, groups))]
    if groups > 2:
        offsets[-2:] = [(1, 2), (2, 1)]
    return offsets


def send_plane(block, offsets):
    pairs = []
    for g in range(lax.axis_size("dp")):
        pairs += [(2 * g + t, 2 * (g ^ offsets[t]) + 1 - t) for t in range(2)]
    return lax.ppermute(block, ("dp", "test"), pairs)


def is_direct(count):
    return count <= 4


def slot_order(count):
    slots = list(range(count))
    return slots[::-1] if is_direct(count) else slots[::2] + slots[1::2]


def exchange(send, parts, count):
    slots = dict(zip(slot_order(count), parts))
    if is_direct(count):
        got = {k: send(slots[k], "expert", k) for k in reversed(range(1, count))}
        return [slots[0]] + [got[k] for k in range(1, count)]
    unit = parts[0].shape[0]
    bit = 1
    while bit < count:
        moving = [k for k in range(count) if k & bit]
        got = send(jnp.concatenate([slots[k] for k in moving]), "expert", bit)
        for index, k in enumerate(moving):
            slots[k] = got[index * unit : (index + 1) * unit]
        bit *= 2
    return [slots[k] for k in range(count)]


def keep_in_hbm(array):
    return pltpu.with_memory_space_constraint(array, pltpu.HBM)


def dot_f32(a, b, contract):
    return lax.dot_general(a, b, (contract, ((), ())), preferred_element_type=F32)


def whole_vmem(count):
    return [pl.BlockSpec(memory_space=pltpu.VMEM)] * count


def in_hbm(count):
    return [pl.BlockSpec(memory_space=pltpu.HBM)] * count


def start_copies(pairs, sems):
    copies = [
        pltpu.make_async_copy(source, target, sems.at[index])
        for index, (source, target) in enumerate(pairs)
    ]
    for copy in copies:
        copy.start()
    return copies


def limit(rows):
    return pltpu.CompilerParams(vmem_limit_bytes=(8 << 20) + rows * (48 << 10))


def hit_tables(ids, slots, weights, want, experts):
    live = (slots >= 0) & (ids < experts)
    code = jnp.where(live, ids * CAP + slots, -1)
    hits = jnp.zeros((want.shape[0], ids.shape[1]), F32)
    scaled = hits
    for route in range(ids.shape[0]):
        match = code[route : route + 1, :] == want
        hits = jnp.where(match, 1.0, hits)
        scaled = jnp.where(match, weights[route : route + 1, :], scaled)
    return hits, scaled


def select_kernel(experts, *refs):
    sources, (hit_ref, *out_refs) = refs[:5], refs[5:-6]
    ids, slots, weight, tok, grad, sems = refs[-6:]
    copies = start_copies(zip(sources, (ids, slots, weight, tok, grad)), sems)
    here = lax.axis_index("expert")
    unit = KINDS * CAP
    quarter = tok.shape[1] // 2
    row = lax.broadcasted_iota(jnp.int32, (experts * unit, 1), 0)
    kind = (row % unit) // CAP
    turn = row // unit
    if is_direct(experts):
        turn = experts - 1 - turn
    else:
        turn = 2 * turn % experts + 2 * turn // experts
    want = (turn ^ here) * CAP + row % CAP
    for copy in copies[:3]:
        copy.wait()
    hits, scaled = hit_tables(ids[...], slots[...], weight[...].astype(F32), want, experts)
    hit_ref[...] = hits
    total = None
    for index in range(KINDS):
        table, source = (hits, tok) if index < 2 else (scaled, grad)
        if index % 2 == 0:
            copies[3 + index // 2].wait()
        left = jnp.where(kind == index, table, 0.0).astype(BF16)
        first = (index % 2) * quarter
        part = dot_f32(left, source[:, first : first + quarter], ((1,), (0,)))
        total = part if total is None else total + part
    total = total.astype(BF16)
    for k, out_ref in enumerate(out_refs):
        out_ref[...] = total[k * unit : (k + 1) * unit]


def arrange_kernel(*refs):
    *slot_refs, out_ref = refs
    slots = [ref[...].astype(F32) for ref in slot_refs[::-1]]
    pairs = CAP * len(slots)
    for kind in range(KINDS):
        rows = [slot[kind * CAP : (kind + 1) * CAP] for slot in slots]
        out_ref[kind * pairs : (kind + 1) * pairs] = jnp.concatenate(rows).astype(BF16)


def join_kernel(offsets, *refs):
    *block_refs, own_ref, out_ref = refs
    count = len(offsets) + 1
    pairs = own_ref.shape[0] // KINDS

    def place(ref, g):
        for kind in range(KINDS):
            first = (kind * count + g) * pairs
            out_ref[first : first + pairs] = ref[kind * pairs : (kind + 1) * pairs]

    place(own_ref, 0)
    for core in range(2):

        @pl.when(lax.axis_index("test") == core)
        def _():
            for ref, offset in zip(block_refs, offsets):
                place(ref, offset[1 - core])


def load_kernel(moves, *refs):
    count = 1 + max(move[0] for move in moves)
    sources, targets = refs[1 : 1 + count], refs[1 + count : -1]
    pairs = []
    for source, column, width, target, row, place in moves:
        rows = sources[source].shape[0]
        block = targets[target].at[row : row + rows, place : place + width]
        pairs.append((sources[source].at[:, column : column + width], block))
    for copy in start_copies(pairs, refs[-1]):
        copy.wait()


def split_two(value):
    high = value.astype(BF16)
    return jnp.concatenate([high, (value - high.astype(F32)).astype(BF16)], axis=1)


def join_two(value):
    value = value.astype(F32)
    middle = value.shape[1] // 2
    return value[:, :middle] + value[:, middle:]


def load(after, params, shapes, moves, compiler_params):
    with jax.named_scope("load"):
        return pl.pallas_call(
            functools.partial(load_kernel, moves),
            out_shape=[jax.ShapeDtypeStruct(shape, BF16) for shape in shapes],
            in_specs=whole_vmem(1) + in_hbm(len(params)),
            out_specs=whole_vmem(len(shapes)),
            scratch_shapes=[pltpu.SemaphoreType.DMA((len(moves),))],
            compiler_params=compiler_params,
            cost_estimate=pl.CostEstimate(
                flops=0, bytes_accessed=sum(2 * x.size for x in params), transcendentals=0
            ),
        )(after, *map(keep_in_hbm, params))


def expert_kernel(
    own_ref, other_ref, pair_w, down_w, proj_ref, keep_ref, send_ref, mine_ref, x_in, x_grad
):
    rows, width = x_in.shape
    half, quarter = width // 2, width // 4
    pairs, ff = mine_ref.shape[0], proj_ref.shape[1]
    core = lax.axis_index("test")
    near, far = pl.multiple_of(core * half, 128), pl.multiple_of((1 - core) * half, 128)
    row = lax.broadcasted_iota(jnp.int32, (rows, quarter), 0)
    odd = jnp.where(row >= pairs, 1, 0)
    slot = (row % pairs) // CAP
    if is_direct(pairs // CAP):
        odd = odd ^ jnp.where(slot > 0, 1, 0)
    else:
        for shift in range((pairs // CAP - 1).bit_length()):
            odd = odd ^ ((slot >> shift) & 1)
    odd = odd == 1
    for index in range(KINDS):
        own = own_ref[index * rows : (index + 1) * rows]
        other = other_ref[index * rows : (index + 1) * rows]
        for base, part in ((near, jnp.where(odd, other, own)), (far, jnp.where(odd, own, other))):
            first = (index % 2) * quarter
            if index < 2:
                x_in[:, pl.ds(pl.multiple_of(base + first, 128), quarter)] = part
            else:
                row = pl.multiple_of(base // half * rows, rows)
                x_grad[pl.ds(row, rows), first : first + quarter] = part
    mine_ref[:, :half] = x_grad[:pairs]
    mine_ref[:, half:] = x_grad[rows : rows + pairs]
    both_pre = dot_f32(x_in[...], pair_w[...], ((1,), (0,)))
    gate_pre, up_pre = both_pre[:, :ff], both_pre[:, ff:]
    hid_grads = dot_f32(x_grad[...], down_w[...], ((1,), (1,)))
    hid_grad = hid_grads[:rows, :ff] + hid_grads[rows:, ff:]
    sig = 1.0 / (1.0 + jnp.exp(-gate_pre))
    act_gate = gate_pre * sig
    hidden = (act_gate * up_pre).astype(BF16)
    tail = split_two(dot_f32(hidden, proj_ref[...], ((1,), (1,))))
    up_grad = (hid_grad * act_gate).astype(BF16)
    gate_grad = (hid_grad * up_pre * sig * (1.0 + gate_pre * (1.0 - sig))).astype(BF16)
    both_grad = jnp.concatenate([gate_grad, up_grad], axis=1)
    keep_ref[:, half:] = tail
    send_ref[:, half:] = tail
    for base, first_ref, rest_ref in ((far, send_ref, keep_ref), (near, keep_ref, send_ref)):
        for index in range(2):
            start = pl.multiple_of(base + index * quarter, 128)
            columns = slice(index * quarter, (index + 1) * quarter)
            part = dot_f32(both_grad, pair_w[pl.ds(start, quarter), :], ((1,), (1,)))
            part = part.astype(BF16)
            first_ref[:pairs, columns] = part[:pairs]
            rest_ref[pairs:, columns] = part[pairs:]


def pair_kernel(half, offsets, keep_ref, got_ref, *refs):
    *out_refs, own_ref = refs
    main = keep_ref[:, :half] + got_ref[:, :half]
    tail = split_two(join_two(keep_ref[:, half:]) + join_two(got_ref[:, half:]))
    rows = own_ref.shape[0]

    def place(ref, g):
        ref[:, :half] = main[g * rows : (g + 1) * rows]
        ref[:, half:] = tail[g * rows : (g + 1) * rows]

    place(own_ref, 0)
    for core in range(2):

        @pl.when(lax.axis_index("test") == core)
        def _():
            for ref, offset in zip(out_refs, offsets):
                place(ref, offset[core])


def score_kernel(half, order, *refs):
    pieces = len(refs) - len(order) - 3
    piece_refs, (grad_ref, test_ref) = refs[:pieces], refs[pieces : pieces + 2]
    out_refs, feature = refs[pieces + 2 : -1], refs[-1]
    def total(columns):
        return sum(ref[:, columns].astype(F32) for ref in piece_refs)

    hid = join_two(total(slice(half, None)))
    grad = grad_ref[...]
    proj = grad.shape[1]
    grad = jnp.concatenate([grad, grad], axis=1)
    left = lax.broadcasted_iota(jnp.int32, grad.shape, 1) < proj
    for p in range(0, proj, 2):
        pair = jnp.where(left, hid[:, p : p + 1], hid[:, p + 1 : p + 2])
        row, first = divmod(p * proj, feature.shape[1])
        row *= hid.shape[0]
        feature[row : row + hid.shape[0], first : first + 2 * proj] = (pair * grad).astype(BF16)
    scores = dot_f32(feature[...], test_ref[...], ((1,), (1,)))
    rows, tests = hid.shape[0], test_ref.shape[0] // 2
    score = scores[:rows, :tests] + scores[rows:, tests:]
    main = total(slice(0, half)).astype(BF16)
    for k, out_ref in zip(order, out_refs):
        out_ref[:, :half] = main[k * CAP : (k + 1) * CAP]
        out_ref[:, half:] = score[k * CAP : (k + 1) * CAP].astype(BF16)


def finish_kernel(experts, hit_ref, *refs):
    slot_refs = refs[:experts]
    in_grad_hbm, scores_hbm, in_grad, scores, home_ref, sems = refs[experts:]
    home_ref[...] = jnp.concatenate([ref[...].astype(F32) for ref in slot_refs]).astype(BF16)
    hits = hit_ref[...]
    half = in_grad.shape[1]
    quarter = half // 2
    copies = []
    for index in range(2):
        columns = slice(index * quarter, (index + 1) * quarter)
        in_grad[:, columns] = dot_f32(hits, home_ref[:, columns], ((1,), (0,))).astype(BF16)
        copies += start_copies(
            [(in_grad.at[:, columns], in_grad_hbm.at[:, columns])], sems.at[pl.ds(index, 1)]
        )
    scores[...] = dot_f32(hits, home_ref[:, half:], ((1,), (0,)))
    copies += start_copies([(scores, scores_hbm)], sems.at[pl.ds(2, 1)])
    for copy in copies:
        copy.wait()


def on_device(
    tokens,
    out_grad,
    route_ids,
    route_slots,
    route_weight,
    w_gate,
    w_up,
    w_down,
    proj_hidden,
    proj_grad,
    test_feats,
):
    experts = lax.axis_size("expert")
    groups = lax.axis_size("dp")
    tok_rows, half = tokens.shape
    quarter = half // 2
    width = half * lax.axis_size("test")
    proj, tests = proj_hidden.shape[1], test_feats.shape[1]
    ff = w_gate.shape[2]
    pairs = experts * CAP
    rows = groups * pairs
    unit = KINDS * CAP
    out_width = half + 2 * proj
    ids_t, slots_t, weight_t = route_ids.T, route_slots.T, route_weight.T

    with jax.named_scope("select"):
        hits, *parts = pl.pallas_call(
            functools.partial(select_kernel, experts),
            out_shape=[jax.ShapeDtypeStruct((experts * unit, tok_rows), F32)]
            + [jax.ShapeDtypeStruct((unit, quarter), BF16)] * experts,
            in_specs=in_hbm(5),
            out_specs=whole_vmem(experts + 1),
            scratch_shapes=[
                pltpu.VMEM(x.shape, x.dtype) for x in (ids_t, slots_t, weight_t, tokens, out_grad)
            ]
            + [pltpu.SemaphoreType.DMA((5,))],
            compiler_params=limit(rows),
        )(*map(keep_in_hbm, (ids_t, slots_t, weight_t, tokens, out_grad)))
    slots = exchange(send_cross, parts, experts)
    with jax.named_scope("arrange"):
        block = pl.pallas_call(
            arrange_kernel,
            out_shape=jax.ShapeDtypeStruct((KINDS * pairs, quarter), BF16),
            in_specs=whole_vmem(experts),
            out_specs=whole_vmem(1)[0],
            compiler_params=limit(rows),
        )(*slots[::-1])
    offsets = plane_offsets(groups)
    blocks = [block] + [send_plane(block, offset) for offset in offsets[::-1]]
    loaded = load(
        block,
        [w_gate[0], w_up[0], w_down[0], proj_hidden[0]],
        [(width, 2 * ff), (2 * ff, half), (proj, ff)],
        [(0, 0, ff, 0, 0, 0), (1, 0, ff, 0, 0, ff)]
        + [(2, 0, half, 1, 0, 0), (2, half, half, 1, ff, 0), (3, 0, ff, 2, 0, 0)],
        limit(rows),
    )
    blocks, (pair_w, down_w, hid_proj) = lax.optimization_barrier((blocks, loaded))
    with jax.named_scope("join"):
        own = pl.pallas_call(
            functools.partial(join_kernel, offsets),
            out_shape=jax.ShapeDtypeStruct((KINDS * rows, quarter), BF16),
            in_specs=whole_vmem(groups),
            out_specs=whole_vmem(1)[0],
            compiler_params=limit(rows),
        )(*blocks[::-1])
    other = send_rel(own, "test", 1)
    with jax.named_scope("expert"):
        keep, send, mine = pl.pallas_call(
            expert_kernel,
            out_shape=[
                jax.ShapeDtypeStruct((rows, out_width), BF16),
                jax.ShapeDtypeStruct((rows, out_width), BF16),
                jax.ShapeDtypeStruct((pairs, width), BF16),
            ],
            in_specs=whole_vmem(5),
            out_specs=whole_vmem(3),
            scratch_shapes=[
                pltpu.VMEM((rows, width), BF16),
                pltpu.VMEM((2 * rows, half), BF16),
            ],
            compiler_params=limit(rows),
        )(own, other, pair_w, down_w, hid_proj)
    got = send_rel(send, "test", 1)
    with jax.named_scope("pair"):
        sums = pl.pallas_call(
            functools.partial(pair_kernel, half, offsets),
            out_shape=[jax.ShapeDtypeStruct((pairs, out_width), BF16)] * groups,
            in_specs=whole_vmem(2),
            out_specs=whole_vmem(groups),
            compiler_params=limit(rows),
        )(keep, got)
    pieces = [send_plane(x, offset) for x, offset in zip(sums, offsets)] + [sums[-1]]
    depth = proj * proj // 2
    grad_proj, test_rows = load(
        sums[-1],
        [proj_grad[0], test_feats[0]],
        [(proj, width), (2 * tests, depth)],
        [(0, 0, width, 0, 0, 0), (1, 0, depth, 1, 0, 0), (1, depth, depth, 1, tests, 0)],
        limit(rows),
    )
    hits, mine = lax.optimization_barrier((hits, mine))
    hits = hits.reshape(experts, KINDS, CAP, tok_rows)[:, 0].reshape(pairs, tok_rows)
    hits = hits.T.astype(BF16)
    grad_mine = dot_f32(mine, grad_proj, ((1,), (1,)))
    order = slot_order(experts)
    with jax.named_scope("score"):
        back = pl.pallas_call(
            functools.partial(score_kernel, half, order),
            out_shape=[jax.ShapeDtypeStruct((CAP, half + tests), BF16)] * experts,
            in_specs=whole_vmem(groups + 2),
            out_specs=whole_vmem(experts),
            scratch_shapes=[pltpu.VMEM((2 * pairs, proj * proj // 2), BF16)],
            compiler_params=limit(rows),
        )(*pieces, grad_mine, test_rows)
    slots = exchange(send_rel, back, experts)
    home = [slots[k] for k in order]
    with jax.named_scope("finish"):
        return pl.pallas_call(
            functools.partial(finish_kernel, experts),
            out_shape=[
                jax.ShapeDtypeStruct((tok_rows, half), BF16),
                jax.ShapeDtypeStruct((tok_rows, tests), F32),
            ],
            in_specs=whole_vmem(experts + 1),
            out_specs=in_hbm(2),
            scratch_shapes=[
                pltpu.VMEM((tok_rows, half), BF16),
                pltpu.VMEM((tok_rows, tests), F32),
                pltpu.VMEM((pairs, half + tests), BF16),
                pltpu.SemaphoreType.DMA((3,)),
            ],
            compiler_params=limit(rows),
        )(hits, *home)


def solution(mesh):
    placed = (
        P(("expert", "dp"), "test"),
        P(("expert", "dp"), "test"),
        P(("expert", "dp"), None),
        P(("expert", "dp"), None),
        P(("expert", "dp"), None),
        P("expert", None, ("dp", "test")),
        P("expert", None, ("dp", "test")),
        P("expert", ("dp", "test"), None),
        P("expert", None, ("dp", "test")),
        P("expert", None, None),
        P("expert", "test", None),
    )
    return jax.shard_map(
        on_device,
        mesh=mesh,
        in_specs=placed,
        out_specs=(P(("expert", "dp"), "test"), P(("expert", "dp"), "test")),
        check_vma=False,
    )
```
